32 devices in a mesh: dp: 16 (over z, y, x), outer: 2 (over core).
Axes of the slice: x: 2, y: 2, z: 4, core: 2. Of those that a mesh axis runs over, the one named last changes fastest.
Arguments:
- input_big: bfloat16 [64, 14, 14, 1024], P(('dp', 'outer'))
- input_small: bfloat16 [64, 10, 10, 1024], P(('dp', 'outer'))
- views_big: int32 [64], P(('dp', 'outer')), may hold values from 0 to 1, as said below
- views_small: int32 [64], P(('dp', 'outer')), may hold values from 0 to 1, as said below
- cotan_big: bfloat16 [64, 7, 7, 2048], P(('dp', 'outer'))
- cotan_small: bfloat16 [64, 5, 5, 2048], P(('dp', 'outer'))
- narrow_filter: bfloat16 [1024, 256], P('dp'), may hold values from -0.1875 to 0.1875
- narrow_affine: bfloat16 [256, 2], P('dp')
- spatial_filter: bfloat16 [2304, 256], P('dp'), may hold values from -0.125 to 0.125
- spatial_affine: bfloat16 [256, 2], P('dp')
- widen_filter: bfloat16 [256, 1024], P('dp'), may hold values from -0.375 to 0.375
- widen_affine: bfloat16 [1024, 2], P('dp')
- shrink_filter: bfloat16 [1024, 512], P('dp'), may hold values from -0.1875 to 0.1875
- shrink_affine: bfloat16 [512, 2], P('dp')
- stride_filter: bfloat16 [4608, 512], P('dp'), may hold values from -0.09375 to 0.09375
- stride_affine: bfloat16 [512, 2], P('dp')
- expand_filter: bfloat16 [512, 2048], P('dp'), may hold values from -0.25 to 0.25
- expand_affine: bfloat16 [2048, 2], P('dp')
- bypass_filter: bfloat16 [1024, 2048], P('dp'), may hold values from -0.1875 to 0.1875
- bypass_affine: bfloat16 [2048, 2], P('dp')
Outputs:
- output_big: bfloat16 [64, 7, 7, 2048], P(('dp', 'outer'))
- output_small: bfloat16 [64, 5, 5, 2048], P(('dp', 'outer'))
- dinput_big: bfloat16 [64, 14, 14, 1024], P(('dp', 'outer'))
- dinput_small: bfloat16 [64, 10, 10, 1024], P(('dp', 'outer'))
- narrow_dfilter: float32 [1024, 256], P('dp')
- narrow_daffine: float32 [256, 2], P('dp')
- spatial_dfilter: float32 [2304, 256], P('dp')
- spatial_daffine: float32 [256, 2], P('dp')
- widen_dfilter: float32 [256, 1024], P('dp')
- widen_daffine: float32 [1024, 2], P('dp')
- shrink_dfilter: float32 [1024, 512], P('dp')
- shrink_daffine: float32 [512, 2], P('dp')
- stride_dfilter: float32 [4608, 512], P('dp')
- stride_daffine: float32 [512, 2], P('dp')
- expand_dfilter: float32 [512, 2048], P('dp')
- expand_daffine: float32 [2048, 2], P('dp')
- bypass_dfilter: float32 [1024, 2048], P('dp')
- bypass_daffine: float32 [2048, 2], P('dp')
The draws below stay inside these ranges and needn't reach their ends.
Inputs may be any that keep to these rules, and one draw needn't show every extreme that they name: `views_big`: each image's view; each group holds at least one image of each view. `views_small`: each image's view; each group holds at least one image of each view.
All inputs are finite; a program needn't handle non-finite values.
Results may differ from the reference program's by a relative error of at most 0.02.
Values may be sent and summed in bfloat16 or wider, within the bound.
A program may use at most 192 MiB of HBM per device.

```python
import math
import jax
import jax.numpy as jnp
from jax import lax

C_IN = 1024
MID1 = 256
MID2 = 512
C_OUT = 2048
SIDE_BIG = 14
SIDE_SMALL = 10
IMAGES_BIG = 64
IMAGES_SMALL = 64


def field_draw(key, count, side, width, span, offset):
    keys = jax.random.split(key, 5)
    base = jax.random.normal(keys[0], (count, side, side, width), jnp.float32)
    noise = base
    rising = jnp.exp(math.log(3.0) * jnp.arange(count, dtype=jnp.float32) / max(count - 1, 1))
    jitter = jnp.exp(jax.random.uniform(keys[2], (count,), jnp.float32, 0.0, math.log(span)))
    channel = jnp.exp(jax.random.uniform(keys[3], (width,), jnp.float32, math.log(0.5), math.log(2.0)))
    centre = offset * jax.random.uniform(keys[4], (width,), jnp.float32, -1.0, 1.0)
    return ((noise * channel + centre) * (rising * jitter)[:, None, None, None]).astype(jnp.bfloat16)


def view_draw(key, count):
    first, second = jax.random.split(key)
    split_at = jax.random.randint(first, (), 1, count)
    order = jax.random.permutation(second, count)
    return (order < split_at).astype(jnp.int32)


def affine_draw(key, width):
    first, second = jax.random.split(key)
    gain = jax.random.uniform(first, (width,), jnp.float32, 0.5, 1.5)
    bias = 0.5 * jax.random.normal(second, (width,), jnp.float32)
    return jnp.stack([gain, bias], axis=1).astype(jnp.bfloat16)


def draw_input_big(key, part):
    key = jax.random.fold_in(key, 11)
    return field_draw(key, IMAGES_BIG, SIDE_BIG, C_IN, 1.5, 0.5)


def draw_input_small(key, part):
    key = jax.random.fold_in(key, 12)
    return field_draw(key, IMAGES_SMALL, SIDE_SMALL, C_IN, 1.5, 0.5)


def draw_views_big(key, part):
    key = jax.random.fold_in(key, 21)
    return view_draw(key, IMAGES_BIG)


def draw_views_small(key, part):
    key = jax.random.fold_in(key, 22)
    return view_draw(key, IMAGES_SMALL)


def draw_cotan_big(key, part):
    key = jax.random.fold_in(key, 13)
    return field_draw(key, IMAGES_BIG, SIDE_BIG // 2, C_OUT, 1.5, 0.3)


def draw_cotan_small(key, part):
    key = jax.random.fold_in(key, 14)
    return field_draw(key, IMAGES_SMALL, SIDE_SMALL // 2, C_OUT, 1.5, 0.3)


def draw_narrow_affine(key, part):
    return affine_draw(jax.random.fold_in(key, 31), MID1)


def draw_spatial_affine(key, part):
    return affine_draw(jax.random.fold_in(key, 32), MID1)


def draw_widen_affine(key, part):
    return affine_draw(jax.random.fold_in(key, 33), C_IN)


def draw_shrink_affine(key, part):
    return affine_draw(jax.random.fold_in(key, 34), MID2)


def draw_stride_affine(key, part):
    return affine_draw(jax.random.fold_in(key, 35), MID2)


def draw_expand_affine(key, part):
    return affine_draw(jax.random.fold_in(key, 36), C_OUT)


def draw_bypass_affine(key, part):
    return affine_draw(jax.random.fold_in(key, 37), C_OUT)


def levels(stream_key, extent, cuts, smallest, largest):
    def one(axis_at, blocks):
        heights = jax.random.uniform(jax.random.fold_in(jax.random.fold_in(stream_key, 6), axis_at), (blocks,), jnp.float32, smallest / len(cuts), largest / len(cuts))
        return jnp.repeat(jnp.exp(heights), extent[axis_at] // blocks).reshape((-1,) + (1,) * (len(extent) - axis_at - 1))

    level = one(*cuts[0])
    for cut in cuts[1:]:
        level = level * one(*cut)
    return level


def normal_values(own_key, shape, spread, limit, cuts=(), held_as=jnp.bfloat16):
    entries = spread * jax.random.normal(own_key, shape, jnp.float32)
    if cuts:
        entries = entries * levels(own_key, shape, cuts, -0.22, 0.18)
    return jnp.clip(entries, -limit, limit).astype(held_as)


def setup_inputs(seed: int = 0) -> dict:
    key_list = jax.random.split(jax.random.key(seed), 21)
    return {
        "input_big": draw_input_big(jax.random.fold_in(key_list[20], 71), 0),
        "input_small": draw_input_small(jax.random.fold_in(key_list[20], 71), 0),
        "views_big": draw_views_big(jax.random.fold_in(key_list[20], 71), 0),
        "views_small": draw_views_small(jax.random.fold_in(key_list[20], 71), 0),
        "cotan_big": draw_cotan_big(jax.random.fold_in(key_list[20], 71), 0),
        "cotan_small": draw_cotan_small(jax.random.fold_in(key_list[20], 71), 0),
        "narrow_filter": normal_values(key_list[6], (C_IN, MID1), C_IN ** -0.5, 0.1875, ((0, 16),)),
        "narrow_affine": draw_narrow_affine(jax.random.fold_in(key_list[20], 71), 0),
        "spatial_filter": normal_values(key_list[8], (9 * MID1, MID1), (9 * MID1) ** -0.5, 0.125, ((0, 16),)),
        "spatial_affine": draw_spatial_affine(jax.random.fold_in(key_list[20], 71), 0),
        "widen_filter": normal_values(key_list[10], (MID1, C_IN), MID1 ** -0.5, 0.375, ((0, 16),)),
        "widen_affine": draw_widen_affine(jax.random.fold_in(key_list[20], 71), 0),
        "shrink_filter": normal_values(key_list[12], (C_IN, MID2), C_IN ** -0.5, 0.1875, ((0, 16),)),
        "shrink_affine": draw_shrink_affine(jax.random.fold_in(key_list[20], 71), 0),
        "stride_filter": normal_values(key_list[14], (9 * MID2, MID2), (9 * MID2) ** -0.5, 0.09375, ((0, 16),)),
        "stride_affine": draw_stride_affine(jax.random.fold_in(key_list[20], 71), 0),
        "expand_filter": normal_values(key_list[16], (MID2, C_OUT), MID2 ** -0.5, 0.25, ((0, 16),)),
        "expand_affine": draw_expand_affine(jax.random.fold_in(key_list[20], 71), 0),
        "bypass_filter": normal_values(key_list[18], (C_IN, C_OUT), C_IN ** -0.5, 0.1875, ((0, 16),)),
        "bypass_affine": draw_bypass_affine(jax.random.fold_in(key_list[20], 71), 0),
    }


EPS = 1e-05
HIGH = lax.Precision.HIGHEST

@jax.custom_vjp
def low(v):
    return lax.optimization_barrier(v.astype(jnp.bfloat16)).astype(jnp.float32)

@jax.custom_vjp
def low_back(v):
    return v

def low_keep(v):
    return (low(v), None)

def low_pass(kept, grad):
    return (grad,)

def back_keep(v):
    return (v, None)

def back_low(kept, grad):
    return (low(grad),)
low.defvjp(low_keep, low_pass)
low_back.defvjp(back_keep, back_low)

def one_hot(views):
    return (views[:, None] == jnp.arange(2, dtype=jnp.int32)[None, :]).astype(jnp.float32)

def gelu(value):
    return jax.nn.gelu(value, approximate=False)

def pointwise(field, kernel):
    return jnp.einsum('nhwc,cd->nhwd', field, kernel, precision=HIGH)

def spatial(field, kernel, stride):
    width = field.shape[-1]
    taps = kernel.reshape(3, 3, width, kernel.shape[1])
    return lax.conv_general_dilated(field, taps, (stride, stride), ((1, 1), (1, 1)), dimension_numbers=('NHWC', 'HWIO', 'NHWC'), precision=HIGH)

def batch_norm(field, affine, hot, sizes):
    total = jnp.einsum('nhwc,nv->vc', field, hot, precision=HIGH)
    square = jnp.einsum('nhwc,nv->vc', field * field, hot, precision=HIGH)
    mean = total / sizes[:, None]
    scale = lax.rsqrt(square / sizes[:, None] - mean * mean + EPS)
    centre = jnp.einsum('nv,vc->nc', hot, mean, precision=HIGH)[:, None, None, :]
    stretch = jnp.einsum('nv,vc->nc', hot, scale, precision=HIGH)[:, None, None, :]
    return (field - centre) * stretch * affine[:, 0] + affine[:, 1]

def reference(input_big, input_small, views_big, views_small, cotan_big, cotan_small, narrow_filter, narrow_affine, spatial_filter, spatial_affine, widen_filter, widen_affine, shrink_filter, shrink_affine, stride_filter, stride_affine, expand_filter, expand_affine, bypass_filter, bypass_affine):
    hots = (one_hot(views_big), one_hot(views_small))
    sides = (input_big.shape[1], input_small.shape[1])
    sizes = tuple((lax.optimization_barrier(jnp.sum(hot, axis=0)) * float(side * side) for hot, side in zip(hots, sides)))
    params = tuple((item.astype(jnp.float32) for item in (narrow_filter, narrow_affine, spatial_filter, spatial_affine, widen_filter, widen_affine, shrink_filter, shrink_affine, stride_filter, stride_affine, expand_filter, expand_affine, bypass_filter, bypass_affine)))

    def forward(field_big, field_small, narrow_w, narrow_a, spatial_w, spatial_a, widen_w, widen_a, shrink_w, shrink_a, stride_w, stride_a, expand_w, expand_a, bypass_w, bypass_a):
        results = []
        for field, hot, size in zip((field_big, field_small), hots, sizes):
            hidden = low(gelu(batch_norm(low_back(pointwise(field, narrow_w)), narrow_a, hot, size)))
            hidden = low(gelu(batch_norm(low_back(spatial(hidden, spatial_w, 1)), spatial_a, hot, size)))
            upper = low(gelu(batch_norm(low_back(pointwise(hidden, widen_w)), widen_a, hot, size) + field))
            hidden = low(gelu(batch_norm(low_back(pointwise(upper, shrink_w)), shrink_a, hot, size)))
            hidden = low(gelu(batch_norm(low_back(spatial(hidden, stride_w, 2)), stride_a, hot, size)))
            main = batch_norm(low_back(pointwise(hidden, expand_w)), expand_a, hot, size)
            branch = batch_norm(low_back(pointwise(upper[:, ::2, ::2, :], bypass_w)), bypass_a, hot, size)
            results.append(gelu(main + branch))
        return (results[0], results[1])
    fields = (input_big.astype(jnp.float32), input_small.astype(jnp.float32))
    outputs, pull = jax.vjp(forward, *fields, *params)
    grads = pull((cotan_big.astype(jnp.float32), cotan_small.astype(jnp.float32)))
    return (outputs[0].astype(jnp.bfloat16), outputs[1].astype(jnp.bfloat16), grads[0].astype(jnp.bfloat16), grads[1].astype(jnp.bfloat16), grads[2], grads[3], grads[4], grads[5], grads[6], grads[7], grads[8], grads[9], grads[10], grads[11], grads[12], grads[13], grads[14], grads[15])
```

```python
import functools

import jax
import jax.numpy as jnp
from jax import lax
from jax.experimental import pallas as pl
from jax.experimental.pallas import tpu as pltpu
from jax.sharding import PartitionSpec as P

MESH = pl.DeviceIdType.MESH
F32 = jnp.float32
BF16 = jnp.bfloat16


class Place:
    def __init__(self, spare):
        self.spare = spare
        dp = lax.axis_index("dp")
        self.core = lax.axis_index("outer")
        self.rest = lax.rem(dp, spare)
        group = lax.div(dp, spare)
        self.far = lax.div(group, 4)
        self.near = lax.rem(group, 4)
        high, low = lax.div(self.near, 2), lax.rem(self.near, 2)
        self.first = 2 * lax.rem(high + 1 - self.core, 2) + lax.rem(low + self.core, 2)
        self.second = 2 * lax.rem(high + self.core, 2) + lax.rem(low + 1 - self.core, 2)
        self.both = 3 - self.near

    def device(self, far=None, near=None, core=None, rest=None):
        far = self.far if far is None else far
        near = self.near if near is None else near
        core = self.core if core is None else core
        rest = self.rest if rest is None else rest
        return ((far * 4 + near) * self.spare + rest, core)

    def fars(self):
        return [self.device(far=lax.rem(self.far + k, 4)) for k in range(1, 4)]

    def nears(self):
        return [self.device(near=lax.rem(self.near + k, 4)) for k in range(1, 4)]

    def cross_nears(self):
        return [
            self.device(near=lax.rem(self.near + k, 4), core=1 - self.core) for k in range(1, 4)
        ]

    def sibling(self):
        return self.device(core=1 - self.core)

    def rests(self):
        return [
            self.device(rest=lax.rem(self.rest + k, self.spare)) for k in range(1, self.spare)
        ]


def greet(devices):
    barrier = pltpu.get_barrier_semaphore()
    for device in devices:
        pl.semaphore_signal(barrier, inc=1, device_id=device, device_id_type=MESH)
    pl.semaphore_wait(barrier, len(devices))


def send(src, dst, send_sem, recv_sem, device):
    pltpu.make_async_remote_copy(
        src_ref=src,
        dst_ref=dst,
        send_sem=send_sem,
        recv_sem=recv_sem,
        device_id=device,
        device_id_type=MESH,
    ).start()


def await_bytes(like, sem):
    pltpu.make_async_copy(like, like, sem).wait()


class Reduce:
    def __init__(self, place, split, refs):
        self.place = place
        self.split = split
        self.refs = refs

    @staticmethod
    def scratch(rows, width, spare, split):
        piece = width // 2 if split else width
        shapes = []
        for count in Reduce.counts(spare, split):
            shapes.append(pltpu.VMEM((count, rows, piece), F32))
            shapes.append(pltpu.VMEM((rows, piece), F32))
        phases = len(Reduce.counts(spare, split))
        shapes.append(pltpu.SemaphoreType.DMA((phases + 1,)))
        shapes.append(pltpu.SemaphoreType.DMA((phases + 1,)))
        return shapes

    @staticmethod
    def counts(spare, split):
        counts = [1, 3, 3] if split else [7, 3]
        return counts + ([spare - 1] if spare > 1 else [])

    def run(self, src, out, between=None):
        place, split = self.place, self.split
        send_sem, recv_sem = self.refs[-2:]
        width = src.shape[1]
        piece = width // 2
        if split:
            phases = [[place.sibling()], place.nears(), place.fars()]
            mine = pl.ds(pl.multiple_of(place.core * piece, 128), piece)
            other = pl.ds(pl.multiple_of((1 - place.core) * piece, 128), piece)
        else:
            phases = [[place.sibling()] + place.nears() + place.cross_nears(), place.fars()]
        if place.spare > 1:
            phases.append(place.rests())
        held = src
        for p, devices in enumerate(phases):
            slots, total = self.refs[2 * p], self.refs[2 * p + 1]
            crossing = split and p == 0
            sent = src.at[:, other] if crossing else held
            for k, device in enumerate(devices):
                send(sent, slots.at[k], send_sem.at[p], recv_sem.at[p], device)
            if between is not None:
                between(p)
            await_bytes(slots, recv_sem.at[p])
            value = src[:, mine] if crossing else held[...]
            for k in range(len(devices)):
                value = value + slots[k]
            last = p == len(phases) - 1 and not split
            if last:
                out[...] = value
            else:
                total[...] = value
            held = total
        if split:
            send(held, out.at[:, mine], send_sem.at[len(phases)], recv_sem.at[len(phases)], place.sibling())
            out[:, mine] = held[...]
            await_bytes(out.at[:, other], recv_sem.at[len(phases)])
        for p in range(len(phases)):
            await_bytes(self.refs[2 * p], send_sem.at[p])
        if split:
            await_bytes(held, send_sem.at[len(phases)])


class Gather:
    PHASES = 5

    def __init__(self, place, whole, send_sem, recv_sem, halved=True):
        self.place, self.whole, self.halved = place, whole, halved
        self.send_sem, self.recv_sem = send_sem, recv_sem
        columns = whole.shape[3]
        if halved:
            half = columns // 2
            self.cols = pl.ds(pl.multiple_of(place.core * half, 128), half)
            self.others = pl.ds(pl.multiple_of((1 - place.core) * half, 128), half)
        else:
            self.cols = pl.ds(0, columns)

    def part(self, far, near):
        return self.whole.at[far, near, :, self.cols]

    def start(self):
        place = self.place
        for device in place.fars():
            block = self.part(place.far, place.near)
            send(block, block, self.send_sem.at[0], self.recv_sem.at[0], device)

    def near(self):
        place = self.place
        await_bytes(self.part(pl.ds(0, 3), 0), self.recv_sem.at[0])
        block = self.part(pl.ds(0, 4), place.near)
        for phase, partner in ((1, place.first), (2, place.second)):
            send(
                block,
                block,
                self.send_sem.at[phase],
                self.recv_sem.at[phase],
                place.device(near=partner),
            )

    def forward(self):
        place = self.place
        block = self.part(pl.ds(0, 4), place.first)
        await_bytes(block, self.recv_sem.at[1])
        send(
            block, block, self.send_sem.at[3], self.recv_sem.at[3], place.device(near=place.second)
        )

    def cross(self):
        place = self.place
        await_bytes(self.part(pl.ds(0, 4), place.second), self.recv_sem.at[2])
        await_bytes(self.part(pl.ds(0, 4), place.both), self.recv_sem.at[3])
        if self.halved:
            block = self.part(pl.ds(0, 4), pl.ds(0, 4))
            send(block, block, self.send_sem.at[4], self.recv_sem.at[4], place.sibling())

    def finish(self):
        if self.halved:
            await_bytes(
                self.whole.at[pl.ds(0, 4), pl.ds(0, 4), :, self.others], self.recv_sem.at[4]
            )

    def settle(self):
        await_bytes(self.part(pl.ds(0, 3), 0), self.send_sem.at[0])
        for phase in (1, 2, 3):
            await_bytes(self.part(pl.ds(0, 4), 0), self.send_sem.at[phase])
        if self.halved:
            await_bytes(self.part(pl.ds(0, 4), pl.ds(0, 4)), self.send_sem.at[4])


class Scatter:
    PHASES = 5

    def __init__(self, place, whole, landing, done, send_sem, recv_sem):
        self.place, self.whole, self.landing, self.done = place, whole, landing, done
        self.send_sem, self.recv_sem = send_sem, recv_sem
        half = whole.shape[3] // 2
        self.half = half
        self.base = place.core * half
        self.cols = pl.ds(pl.multiple_of(place.core * half, 128), half)
        self.others = pl.ds(pl.multiple_of((1 - place.core) * half, 128), half)

    @staticmethod
    def scratch(rows, columns):
        half = columns // 2
        return [
            pltpu.VMEM((4, 4, rows, half), BF16),
            pltpu.VMEM((2, 4, rows, half), BF16),
            pltpu.VMEM((4, rows, half), BF16),
            pltpu.VMEM((3, rows, half), BF16),
        ]

    def add(self, near, block):
        blocks = self.half // 128
        whole, base = self.whole, self.base

        @pl.loop(0, 4 * blocks)
        def _(i):
            far, b = lax.div(i, blocks), lax.rem(i, blocks)
            here = pl.ds(pl.multiple_of(base + b * 128, 128), 128)
            there = pl.ds(pl.multiple_of(b * 128, 128), 128)
            total = whole[far, near, :, here].astype(F32) + block[far, :, there].astype(F32)
            whole[far, near, :, here] = total.astype(BF16)

    def start(self):
        send(
            self.whole.at[pl.ds(0, 4), pl.ds(0, 4), :, self.others],
            self.landing[0],
            self.send_sem.at[0],
            self.recv_sem.at[0],
            self.place.sibling(),
        )

    def second(self):
        place = self.place
        await_bytes(self.landing[0], self.recv_sem.at[0])
        blocks = self.half // 128
        whole, base, block = self.whole, self.base, self.landing[0]

        @pl.loop(0, 16 * blocks)
        def _(i):
            group, b = lax.div(i, blocks), lax.rem(i, blocks)
            far, near = lax.div(group, 4), lax.rem(group, 4)
            here = pl.ds(pl.multiple_of(base + b * 128, 128), 128)
            there = pl.ds(pl.multiple_of(b * 128, 128), 128)
            total = whole[far, near, :, here].astype(F32) + block[far, near, :, there].astype(F32)
            whole[far, near, :, here] = total.astype(BF16)

        for k, near in enumerate((place.second, place.both)):
            send(
                whole.at[pl.ds(0, 4), near, :, self.cols],
                self.landing[1].at[k],
                self.send_sem.at[1],
                self.recv_sem.at[1],
                place.device(near=place.second),
            )

    def first(self):
        place = self.place
        await_bytes(self.landing[1], self.recv_sem.at[1])
        self.add(place.first, self.landing[1].at[1])
        send(
            self.whole.at[pl.ds(0, 4), place.first, :, self.cols],
            self.landing[2],
            self.send_sem.at[2],
            self.recv_sem.at[2],
            place.device(near=place.first),
        )
        self.add(place.near, self.landing[1].at[0])

    def fars(self):
        place = self.place
        await_bytes(self.landing[2], self.recv_sem.at[2])
        self.add(place.near, self.landing[2])
        for k in range(1, 4):
            far = lax.rem(place.far + k, 4)
            send(
                self.whole.at[far, place.near, :, self.cols],
                self.landing[3].at[k - 1],
                self.send_sem.at[3],
                self.recv_sem.at[3],
                place.device(far=far),
            )

    def cross(self):
        place = self.place
        await_bytes(self.landing[3], self.recv_sem.at[3])
        blocks = self.half // 128
        whole, base, block, done = self.whole, self.base, self.landing[3], self.done

        @pl.loop(0, blocks)
        def _(b):
            here = pl.ds(pl.multiple_of(base + b * 128, 128), 128)
            there = pl.ds(pl.multiple_of(b * 128, 128), 128)
            total = whole[place.far, place.near, :, here].astype(F32)
            for k in range(3):
                total = total + block[k, :, there].astype(F32)
            done[:, here] = total.astype(BF16)

        half = done.at[:, self.cols]
        send(half, half, self.send_sem.at[4], self.recv_sem.at[4], place.sibling())

    def finish(self):
        await_bytes(self.done.at[:, self.others], self.recv_sem.at[4])

    def settle(self):
        await_bytes(self.landing[0], self.send_sem.at[0])
        await_bytes(self.landing[1], self.send_sem.at[1])
        await_bytes(self.landing[2], self.send_sem.at[2])
        await_bytes(self.landing[3], self.send_sem.at[3])
        await_bytes(self.done.at[:, self.cols], self.send_sem.at[4])


EPS = 1e-05
HIGH = lax.Precision.HIGHEST


def as_sent(value):
    return jax.tree.map(lambda a: a.astype(jnp.bfloat16) if a.dtype == jnp.float32 else a, value)


def one_hot(views):
    return (views[:, None] == jnp.arange(2, dtype=jnp.int32)[None, :]).astype(jnp.float32)


def view_sum(rows, hot):
    return jnp.dot(hot.T, rows, precision=HIGH)


def spread(stat, hot):
    return jnp.dot(hot, stat, precision=HIGH)[:, None, None, :]


def gelu_value(value):
    return jax.nn.gelu(value, approximate=False)


def gelu_slope(value):
    cdf = 0.5 * (1.0 + lax.erf(value * 0.7071067811865476))
    return cdf + value * jnp.exp(-0.5 * value * value) * 0.3989422804014327


def pointwise(field, kernel):
    shape = field.shape
    flat = jnp.dot(field.reshape(-1, shape[-1]), kernel, preferred_element_type=jnp.float32)
    return flat.reshape(shape[:-1] + (kernel.shape[1],))


def back_pointwise(grad, kernel):
    shape = grad.shape
    flat = lax.dot_general(
        grad.reshape(-1, shape[-1]),
        kernel,
        (((1,), (1,)), ((), ())),
        preferred_element_type=jnp.float32,
    )
    return flat.reshape(shape[:-1] + (kernel.shape[0],))


def filter_grad(field, grad):
    return lax.dot_general(
        field.reshape(-1, field.shape[-1]),
        grad.reshape(-1, grad.shape[-1]),
        (((0,), (0,)), ((), ())),
        preferred_element_type=jnp.float32,
    )


def columns(field, stride):
    side = field.shape[1]
    outside = (side - 1) // stride + 1
    reach = stride * (outside - 1) + 1
    padded = jnp.pad(field, ((0, 0), (1, 1), (1, 1), (0, 0)))
    taps = []
    for row in range(3):
        for across in range(3):
            taps.append(padded[:, row : row + reach : stride, across : across + reach : stride, :])
    return jnp.concatenate(taps, axis=-1)


def uncolumns(grads, side, stride):
    count, outside = (grads.shape[0], grads.shape[1])
    width = grads.shape[-1] // 9
    reach = stride * (outside - 1) + 1
    padded = jnp.zeros((count, side + 2, side + 2, width), jnp.float32)
    for row in range(3):
        for across in range(3):
            tap = 3 * row + across
            padded = padded.at[
                :, row : row + reach : stride, across : across + reach : stride, :
            ].add(grads[..., tap * width : (tap + 1) * width])
    return padded[:, 1:-1, 1:-1, :]


def affine_apply(normed, affine):
    return normed * affine[:, 0].astype(jnp.float32) + affine[:, 1].astype(jnp.float32)


def normalize(pairs, hots, sizes, extra):
    terms = []
    for pair in pairs:
        for field, hot in zip(pair, hots):
            terms.append(view_sum(jnp.sum(field, axis=(1, 2)), hot))
            terms.append(view_sum(jnp.sum(field * field, axis=(1, 2)), hot))
    totals = psum(terms, extra)
    if extra:
        sizes = totals[-1]
    kept = []
    for layer in range(len(pairs)):
        groups = []
        for group in range(2):
            counted = sizes[group][:, None]
            mean = totals[4 * layer + 2 * group] / counted
            scale = lax.rsqrt(totals[4 * layer + 2 * group + 1] / counted - mean * mean + EPS)
            hot = hots[group]
            stretch = spread(scale, hot)
            groups.append(((pairs[layer][group] - spread(mean, hot)) * stretch, stretch))
        kept.append(groups)
    return (kept, sizes)


def denormalize(douts, kept, affines, hots, sizes):
    terms = []
    for layer in range(len(kept)):
        for group in range(2):
            incoming = douts[layer][group]
            normed = kept[layer][group][0]
            terms.append(view_sum(jnp.sum(incoming, axis=(1, 2)), hots[group]))
            terms.append(view_sum(jnp.sum(incoming * normed, axis=(1, 2)), hots[group]))
    totals = psum(terms, ())
    results = []
    affine_grads = []
    for layer in range(len(kept)):
        gain = affines[layer][:, 0].astype(jnp.float32)
        outs = []
        for group in range(2):
            normed, stretch = kept[layer][group]
            hot = hots[group]
            counted = sizes[group][:, None]
            first = spread(totals[4 * layer + 2 * group] / counted, hot)
            second = spread(totals[4 * layer + 2 * group + 1] / counted, hot)
            grad = gain * stretch * (douts[layer][group] - first - normed * second)
            outs.append(grad.astype(jnp.bfloat16))
        bias_grad = jnp.sum(totals[4 * layer] + totals[4 * layer + 2], axis=0)
        gain_grad = jnp.sum(totals[4 * layer + 1] + totals[4 * layer + 3], axis=0)
        affine_grads.append(jnp.stack([gain_grad, bias_grad], axis=1))
        results.append(outs)
    return (results, affine_grads)


CALLS = [0]


def psum(terms, extra):
    widths = [term.shape[1] for term in terms]
    stacked = jnp.concatenate(list(terms) + [jnp.pad(item, ((0, 0), (0, 126))) for item in extra], axis=1)
    rows = stacked.reshape(2, -1, 128).reshape(-1, 128)
    total = reduce_call(rows).reshape(2, -1)
    outs, at = [], 0
    for width in widths:
        outs.append(total[:, at : at + width])
        at += width
    if extra:
        outs.append(total[:, at : at + 2])
    return outs


def reduce_call(rows):
    spare = lax.axis_size("dp") // 16
    CALLS[0] += 1

    def kernel(src, out, *refs):
        place = Place(spare)
        greet([place.sibling()] + place.nears() + place.cross_nears() + place.fars() + place.rests())
        Reduce(place, False, refs).run(src, out)

    return pl.pallas_call(
        kernel,
        out_shape=jax.ShapeDtypeStruct(rows.shape, F32),
        in_specs=[pl.BlockSpec(memory_space=pltpu.VMEM)],
        out_specs=pl.BlockSpec(memory_space=pltpu.VMEM),
        scratch_shapes=Reduce.scratch(rows.shape[0], rows.shape[1], spare, False),
        compiler_params=pltpu.CompilerParams(collective_id=CALLS[0], has_side_effects=True, vmem_limit_bytes=48 << 20),
    )(rows)


def spare_groups(spare):
    count = lax.axis_size("dp")
    return [list(range(at, at + spare)) for at in range(0, count, spare)]


def gather_call(shards):
    spare = lax.axis_size("dp") // 16
    if spare > 1:
        shards = [
            lax.all_gather(item, "dp", axis_index_groups=spare_groups(spare), tiled=True)
            for item in shards
        ]
    count = len(shards)

    def kernel(*refs):
        ins, outs = refs[:count], refs[count : 2 * count]
        local_sem, send_sem, recv_sem = refs[2 * count :]
        place = Place(spare)
        items, copies = [], []
        for k in range(count):
            halved = ins[k].shape[1] > 128
            items.append(Gather(place, outs[k], send_sem.at[k], recv_sem.at[k], halved))
            copies.append(
                pltpu.make_async_copy(
                    ins[k].at[:, items[k].cols], items[k].part(place.far, place.near), local_sem.at[k]
                )
            )
            copies[k].start()
        greet(place.fars() + place.nears() + [place.sibling()])
        for k in range(count):
            copies[k].wait()
            items[k].start()
        for step in ("near", "forward", "cross", "finish", "settle"):
            for item in items:
                getattr(item, step)()

    return pl.pallas_call(
        kernel,
        out_shape=[jax.ShapeDtypeStruct((4, 4) + item.shape, BF16) for item in shards],
        in_specs=[pl.BlockSpec(memory_space=pl.ANY)] * count,
        out_specs=[pl.BlockSpec(memory_space=pl.ANY)] * count,
        scratch_shapes=[
            pltpu.SemaphoreType.DMA((count,)),
            pltpu.SemaphoreType.DMA((count, Gather.PHASES)),
            pltpu.SemaphoreType.DMA((count, Gather.PHASES)),
        ],
        compiler_params=pltpu.CompilerParams(collective_id=20, has_side_effects=True, vmem_limit_bytes=60 << 20),
    )(*shards)


def scatter_call(grads):
    spare = lax.axis_size("dp") // 16
    count = len(grads)
    grads = [item.astype(BF16).reshape(4, 4, item.shape[0] // 16, item.shape[1]) for item in grads]

    def kernel(*refs):
        ins, outs = refs[:count], refs[count : 2 * count]
        wholes = refs[2 * count : 3 * count]
        landings = [refs[3 * count + 4 * k : 3 * count + 4 * k + 4] for k in range(count)]
        local_sem, send_sem, recv_sem = refs[7 * count :]
        place = Place(spare)
        copies = []
        for k in range(count):
            copies.append(pltpu.make_async_copy(ins[k], wholes[k], local_sem.at[k]))
            copies[-1].start()
        greet(place.fars() + place.nears() + [place.sibling()])
        items = [
            Scatter(place, wholes[k], landings[k], outs[k], send_sem.at[k], recv_sem.at[k])
            for k in range(count)
        ]
        for k in range(count):
            copies[k].wait()
            items[k].start()
        for step in ("second", "first", "fars", "cross", "finish", "settle"):
            for item in items:
                getattr(item, step)()

    landings = []
    for item in grads:
        landings += Scatter.scratch(item.shape[2], item.shape[3])
    done = pl.pallas_call(
        kernel,
        out_shape=[jax.ShapeDtypeStruct(item.shape[2:], BF16) for item in grads],
        in_specs=[pl.BlockSpec(memory_space=pl.ANY)] * count,
        out_specs=[pl.BlockSpec(memory_space=pltpu.VMEM)] * count,
        scratch_shapes=[pltpu.VMEM(item.shape, BF16) for item in grads]
        + landings
        + [
            pltpu.SemaphoreType.DMA((count,)),
            pltpu.SemaphoreType.DMA((count, Scatter.PHASES)),
            pltpu.SemaphoreType.DMA((count, Scatter.PHASES)),
        ],
        compiler_params=pltpu.CompilerParams(collective_id=21, has_side_effects=True, vmem_limit_bytes=60 << 20),
    )(*grads)
    if spare > 1:
        done = [
            lax.psum_scatter(
                item.astype(F32), "dp", axis_index_groups=spare_groups(spare), tiled=True
            )
            for item in done
        ]
    return [item.astype(F32) for item in done]


def local(
    input_big,
    input_small,
    views_big,
    views_small,
    cotan_big,
    cotan_small,
    narrow_filter,
    narrow_affine,
    spatial_filter,
    spatial_affine,
    widen_filter,
    widen_affine,
    shrink_filter,
    shrink_affine,
    stride_filter,
    stride_affine,
    expand_filter,
    expand_affine,
    bypass_filter,
    bypass_affine,
):
    hots = (one_hot(views_big), one_hot(views_small))
    inputs = (input_big, input_small)
    cotans = (cotan_big, cotan_small)
    groups = range(2)
    pixels = jnp.stack(
        [
            jnp.sum(hot, axis=0) * float(field.shape[1] * field.shape[2])
            for hot, field in zip(hots, inputs)
        ]
    )
    upper_local = (
        narrow_filter,
        narrow_affine,
        spatial_filter,
        spatial_affine,
        widen_filter,
        widen_affine,
    )
    lower_local = (
        shrink_filter,
        shrink_affine,
        stride_filter,
        stride_affine,
        expand_filter,
        expand_affine,
        bypass_filter,
        bypass_affine,
    )
    filters = upper_local[0::2] + lower_local[0::2]
    affines = upper_local[1::2] + lower_local[1::2]
    gains = jnp.concatenate([item[:, 0] for item in affines])
    biases = jnp.concatenate([item[:, 1] for item in affines])
    order = [item.shape[0] for item in affines]
    packed = jnp.stack([gains, biases])
    spare = lax.axis_size("dp") // 16
    lanes = 512 // spare
    packed = jnp.pad(packed, ((0, 0), (0, lanes - packed.shape[1]))).reshape(8 // spare, 128)
    packed = jnp.pad(packed, ((0, 16 // spare - packed.shape[0]), (0, 0)))
    CALLS[0] = 0
    *wholes, table = gather_call(list(filters) + [packed])
    wholes = [item.reshape(-1, item.shape[3]) for item in wholes]
    table = table.reshape(16 * spare, 16 // spare, 128)[:, : 8 // spare].reshape(16 * spare, 2, lanes)
    norms, at = [], 0
    for width in order:
        norms.append(jnp.stack([table[:, 0, at : at + width].reshape(-1), table[:, 1, at : at + width].reshape(-1)], axis=1))
        at += width
    narrow_kernel, spatial_kernel, widen_kernel, shrink_kernel, stride_kernel, expand_kernel, bypass_kernel = wholes
    narrow_norm, spatial_norm, widen_norm, shrink_norm, stride_norm, expand_norm, bypass_norm = norms
    kept_narrow, sizes = normalize(
        [[pointwise(field, narrow_kernel) for field in inputs]], hots, None, (pixels,)
    )
    narrow_act = [
        gelu_value(affine_apply(kept_narrow[0][g][0], narrow_norm)).astype(jnp.bfloat16)
        for g in groups
    ]
    kept_spatial, sizes = normalize(
        [[pointwise(columns(narrow_act[g], 1), spatial_kernel) for g in groups]], hots, sizes, ()
    )
    spatial_act = [
        gelu_value(affine_apply(kept_spatial[0][g][0], spatial_norm)).astype(jnp.bfloat16)
        for g in groups
    ]
    kept_widen, sizes = normalize(
        [[pointwise(spatial_act[g], widen_kernel) for g in groups]], hots, sizes, ()
    )
    upper_sum = [
        affine_apply(kept_widen[0][g][0], widen_norm) + inputs[g].astype(jnp.float32)
        for g in groups
    ]
    upper_out = [gelu_value(upper_sum[g]).astype(jnp.bfloat16) for g in groups]
    kept_shrink, sizes = normalize(
        [[pointwise(upper_out[g], shrink_kernel) for g in groups]], hots, sizes, ()
    )
    shrink_act = [
        gelu_value(affine_apply(kept_shrink[0][g][0], shrink_norm)).astype(jnp.bfloat16)
        for g in groups
    ]
    kept_stride, sizes = normalize(
        [[pointwise(columns(shrink_act[g], 2), stride_kernel) for g in groups]], hots, sizes, ()
    )
    stride_act = [
        gelu_value(affine_apply(kept_stride[0][g][0], stride_norm)).astype(jnp.bfloat16)
        for g in groups
    ]
    bypass_in = [upper_out[g][:, ::2, ::2, :] for g in groups]
    kept_last, sizes = normalize(
        [
            [pointwise(stride_act[g], expand_kernel) for g in groups],
            [pointwise(bypass_in[g], bypass_kernel) for g in groups],
        ],
        hots,
        sizes,
        (),
    )
    lower_sum = [
        affine_apply(kept_last[0][g][0], expand_norm)
        + affine_apply(kept_last[1][g][0], bypass_norm)
        for g in groups
    ]
    output_big = gelu_value(lower_sum[0]).astype(jnp.bfloat16)
    output_small = gelu_value(lower_sum[1]).astype(jnp.bfloat16)
    lower_grad = [cotans[g].astype(jnp.float32) * gelu_slope(lower_sum[g]) for g in groups]
    last_grads, last_affine = denormalize(
        [lower_grad, lower_grad], kept_last, [expand_norm, bypass_norm], hots, sizes
    )
    expand_grad, bypass_grad = last_grads
    expand_dfilter = filter_grad(stride_act[0], expand_grad[0]) + filter_grad(
        stride_act[1], expand_grad[1]
    )
    bypass_dfilter = filter_grad(bypass_in[0], bypass_grad[0]) + filter_grad(
        bypass_in[1], bypass_grad[1]
    )
    stride_in = [
        back_pointwise(expand_grad[g], expand_kernel)
        * gelu_slope(affine_apply(kept_stride[0][g][0], stride_norm))
        for g in groups
    ]
    stride_grads, stride_affine_grad = denormalize(
        [stride_in], kept_stride, [stride_norm], hots, sizes
    )
    stride_grad = stride_grads[0]
    stride_dfilter = filter_grad(columns(shrink_act[0], 2), stride_grad[0]) + filter_grad(
        columns(shrink_act[1], 2), stride_grad[1]
    )
    shrink_in = [
        uncolumns(back_pointwise(stride_grad[g], stride_kernel), shrink_act[g].shape[1], 2)
        * gelu_slope(affine_apply(kept_shrink[0][g][0], shrink_norm))
        for g in groups
    ]
    shrink_grads, shrink_affine_grad = denormalize(
        [shrink_in], kept_shrink, [shrink_norm], hots, sizes
    )
    shrink_grad = shrink_grads[0]
    shrink_dfilter = filter_grad(upper_out[0], shrink_grad[0]) + filter_grad(
        upper_out[1], shrink_grad[1]
    )
    upper_grad = []
    for g in groups:
        through = back_pointwise(shrink_grad[g], shrink_kernel)
        through = through.at[:, ::2, ::2, :].add(back_pointwise(bypass_grad[g], bypass_kernel))
        upper_grad.append(through * gelu_slope(upper_sum[g]))
    widen_grads, widen_affine_grad = denormalize(
        [upper_grad], kept_widen, [widen_norm], hots, sizes
    )
    widen_grad = widen_grads[0]
    widen_dfilter = filter_grad(spatial_act[0], widen_grad[0]) + filter_grad(
        spatial_act[1], widen_grad[1]
    )
    spatial_in = [
        back_pointwise(widen_grad[g], widen_kernel)
        * gelu_slope(affine_apply(kept_spatial[0][g][0], spatial_norm))
        for g in groups
    ]
    spatial_grads, spatial_affine_grad = denormalize(
        [spatial_in], kept_spatial, [spatial_norm], hots, sizes
    )
    spatial_grad = spatial_grads[0]
    spatial_dfilter = filter_grad(columns(narrow_act[0], 1), spatial_grad[0]) + filter_grad(
        columns(narrow_act[1], 1), spatial_grad[1]
    )
    narrow_in = [
        uncolumns(back_pointwise(spatial_grad[g], spatial_kernel), narrow_act[g].shape[1], 1)
        * gelu_slope(affine_apply(kept_narrow[0][g][0], narrow_norm))
        for g in groups
    ]
    narrow_grads, narrow_affine_grad = denormalize(
        [narrow_in], kept_narrow, [narrow_norm], hots, sizes
    )
    narrow_grad = narrow_grads[0]
    narrow_dfilter = filter_grad(inputs[0], narrow_grad[0]) + filter_grad(inputs[1], narrow_grad[1])
    dinput = [
        (upper_grad[g] + back_pointwise(narrow_grad[g], narrow_kernel)).astype(jnp.bfloat16)
        for g in groups
    ]
    done = scatter_call(
        [narrow_dfilter, spatial_dfilter, widen_dfilter, shrink_dfilter, stride_dfilter, expand_dfilter, bypass_dfilter]
    )
    aff = [narrow_affine_grad[0], spatial_affine_grad[0], widen_affine_grad[0], shrink_affine_grad[0], stride_affine_grad[0], last_affine[0], last_affine[1]]
    me = lax.axis_index("dp")
    outs = [output_big, output_small, dinput[0], dinput[1]]
    for k in range(7):
        share = aff[k].shape[0] // lax.axis_size("dp")
        outs += [done[k], lax.dynamic_slice_in_dim(aff[k], me * share, share)]
    return tuple(outs)


def solution(mesh):
    placed = (
        P(("dp", "outer"), None, None, None),
        P(("dp", "outer"), None, None, None),
        P(("dp", "outer")),
        P(("dp", "outer")),
        P(("dp", "outer"), None, None, None),
        P(("dp", "outer"), None, None, None),
        P("dp", None),
        P("dp", None),
        P("dp", None),
        P("dp", None),
        P("dp", None),
        P("dp", None),
        P("dp", None),
        P("dp", None),
        P("dp", None),
        P("dp", None),
        P("dp", None),
        P("dp", None),
        P("dp", None),
        P("dp", None),
    )
    return jax.shard_map(
        local,
        mesh=mesh,
        in_specs=placed,
        out_specs=(
            P(("dp", "outer"), None, None, None),
            P(("dp", "outer"), None, None, None),
            P(("dp", "outer"), None, None, None),
            P(("dp", "outer"), None, None, None),
            P("dp", None),
            P("dp", None),
            P("dp", None),
            P("dp", None),
            P("dp", None),
            P("dp", None),
            P("dp", None),
            P("dp", None),
            P("dp", None),
            P("dp", None),
            P("dp", None),
            P("dp", None),
            P("dp", None),
            P("dp", None),
        ),
        check_vma=False,
    )
```

```python
import functools
import types

import jax
import jax.numpy as jnp
from jax import lax
from jax.experimental import pallas as pl
from jax.experimental.pallas import tpu as pltpu
from jax.sharding import PartitionSpec as P

MESH = pl.DeviceIdType.MESH
F32 = jnp.float32
BF16 = jnp.bfloat16


class Place:
    def __init__(self, spare):
        self.spare = spare
        dp = lax.axis_index("dp")
        self.core = lax.axis_index("outer")
        self.rest = lax.rem(dp, spare)
        group = lax.div(dp, spare)
        self.far = lax.div(group, 4)
        self.near = lax.rem(group, 4)
        high, low = lax.div(self.near, 2), lax.rem(self.near, 2)
        self.first = 2 * lax.rem(high + 1 - self.core, 2) + lax.rem(low + self.core, 2)
        self.second = 2 * lax.rem(high + self.core, 2) + lax.rem(low + 1 - self.core, 2)
        self.both = 3 - self.near

    def device(self, far=None, near=None, core=None, rest=None):
        far = self.far if far is None else far
        near = self.near if near is None else near
        core = self.core if core is None else core
        rest = self.rest if rest is None else rest
        return ((far * 4 + near) * self.spare + rest, core)

    def fars(self):
        return [self.device(far=lax.rem(self.far + k, 4)) for k in range(1, 4)]

    def nears(self):
        return [self.device(near=lax.rem(self.near + k, 4)) for k in range(1, 4)]

    def cross_nears(self):
        return [
            self.device(near=lax.rem(self.near + k, 4), core=1 - self.core) for k in range(1, 4)
        ]

    def sibling(self):
        return self.device(core=1 - self.core)

    def rests(self):
        return [
            self.device(rest=lax.rem(self.rest + k, self.spare)) for k in range(1, self.spare)
        ]


def greet(devices):
    barrier = pltpu.get_barrier_semaphore()
    for device in devices:
        pl.semaphore_signal(barrier, inc=1, device_id=device, device_id_type=MESH)
    pl.semaphore_wait(barrier, len(devices))


def send(src, dst, send_sem, recv_sem, device):
    pltpu.make_async_remote_copy(
        src_ref=src,
        dst_ref=dst,
        send_sem=send_sem,
        recv_sem=recv_sem,
        device_id=device,
        device_id_type=MESH,
    ).start()


def await_bytes(like, sem):
    pltpu.make_async_copy(like, like, sem).wait()


class Reduce:
    def __init__(self, place, split, refs):
        self.place = place
        self.split = split
        self.refs = refs

    @staticmethod
    def scratch(rows, width, spare, split):
        piece = width // 2 if split else width
        shapes = []
        for count in Reduce.counts(spare, split):
            shapes.append(pltpu.VMEM((count, rows, piece), F32))
            shapes.append(pltpu.VMEM((rows, piece), F32))
        phases = len(Reduce.counts(spare, split))
        shapes.append(pltpu.SemaphoreType.DMA((phases + 1,)))
        shapes.append(pltpu.SemaphoreType.DMA((phases + 1,)))
        return shapes

    @staticmethod
    def counts(spare, split):
        counts = [1, 3, 3] if split else [7, 3]
        return counts + ([spare - 1] if spare > 1 else [])

    def run(self, src, out, between=None):
        place, split = self.place, self.split
        send_sem, recv_sem = self.refs[-2:]
        width = src.shape[1]
        piece = width // 2
        if split:
            phases = [[place.sibling()], place.nears(), place.fars()]
            mine = pl.ds(pl.multiple_of(place.core * piece, 128), piece)
            other = pl.ds(pl.multiple_of((1 - place.core) * piece, 128), piece)
        else:
            phases = [[place.sibling()] + place.nears() + place.cross_nears(), place.fars()]
        if place.spare > 1:
            phases.append(place.rests())
        held = src
        for p, devices in enumerate(phases):
            slots, total = self.refs[2 * p], self.refs[2 * p + 1]
            crossing = split and p == 0
            sent = src.at[:, other] if crossing else held
            for k, device in enumerate(devices):
                send(sent, slots.at[k], send_sem.at[p], recv_sem.at[p], device)
            if between is not None:
                between(p)
            await_bytes(slots, recv_sem.at[p])
            value = src[:, mine] if crossing else held[...]
            for k in range(len(devices)):
                value = value + slots[k]
            last = p == len(phases) - 1 and not split
            if last:
                out[...] = value
            else:
                total[...] = value
            held = total
        if split:
            send(held, out.at[:, mine], send_sem.at[len(phases)], recv_sem.at[len(phases)], place.sibling())
            out[:, mine] = held[...]
            await_bytes(out.at[:, other], recv_sem.at[len(phases)])
        for p in range(len(phases)):
            await_bytes(self.refs[2 * p], send_sem.at[p])
        if split:
            await_bytes(held, send_sem.at[len(phases)])


class Piece:
    def __init__(self, layer, band=0, bands=1, strip=0, strips=1, halved=True, direct=False):
        self.layer, self.halved, self.direct = layer, halved, direct
        self.band, self.bands, self.strip, self.strips = band, bands, strip, strips

    def sizes(self, shape):
        return shape[-2] // self.bands, shape[-1] // (2 if self.halved else 1) // self.strips

    def window(self, place, shape):
        count, width = self.sizes(shape)
        rows = pl.ds(self.band * count, count)
        if not self.halved:
            return rows, pl.ds(0, width), None
        half, skip = shape[-1] // 2, self.strip * width
        cols = pl.ds(pl.multiple_of(place.core * half + skip, 128), width)
        others = pl.ds(pl.multiple_of((1 - place.core) * half + skip, 128), width)
        return rows, cols, others


class Gather:
    PHASES = 5

    def __init__(self, place, whole, piece, send_sem, recv_sem):
        self.place, self.whole, self.piece = place, whole, piece
        self.halved, self.direct = piece.halved, piece.direct
        self.send_sem, self.recv_sem = send_sem, recv_sem
        self.rows, self.cols, self.others = piece.window(place, whole.shape)

    def part(self, far, near):
        return self.whole.at[far, near, self.rows, self.cols]

    def start(self):
        place = self.place
        for device in place.fars():
            block = self.part(place.far, place.near)
            send(block, block, self.send_sem.at[0], self.recv_sem.at[0], device)

    def near(self):
        place = self.place
        await_bytes(self.part(pl.ds(0, 3), 0), self.recv_sem.at[0])
        block = self.part(pl.ds(0, 4), place.near)
        partners = [place.first, place.second] + ([place.both] if self.direct else [])
        for phase, partner in enumerate(partners, 1):
            send(
                block,
                block,
                self.send_sem.at[phase],
                self.recv_sem.at[phase],
                place.device(near=partner),
            )

    def forward(self):
        place = self.place
        block = self.part(pl.ds(0, 4), place.first)
        await_bytes(block, self.recv_sem.at[1])
        if self.direct:
            return
        send(
            block, block, self.send_sem.at[3], self.recv_sem.at[3], place.device(near=place.second)
        )

    def cross(self):
        place = self.place
        await_bytes(self.part(pl.ds(0, 4), place.second), self.recv_sem.at[2])
        await_bytes(self.part(pl.ds(0, 4), place.both), self.recv_sem.at[3])
        if self.halved:
            block = self.part(pl.ds(0, 4), pl.ds(0, 4))
            send(block, block, self.send_sem.at[4], self.recv_sem.at[4], place.sibling())

    def finish(self):
        if self.halved:
            await_bytes(
                self.whole.at[pl.ds(0, 4), pl.ds(0, 4), self.rows, self.others], self.recv_sem.at[4]
            )

    def settle(self):
        await_bytes(self.part(pl.ds(0, 3), 0), self.send_sem.at[0])
        for phase in (1, 2, 3):
            await_bytes(self.part(pl.ds(0, 4), 0), self.send_sem.at[phase])
        if self.halved:
            await_bytes(self.part(pl.ds(0, 4), pl.ds(0, 4)), self.send_sem.at[4])


class Scatter:
    PHASES = 5

    def __init__(self, place, whole, piece, landing, done, send_sem, recv_sem):
        self.place, self.whole, self.landing, self.done = place, whole, landing, done
        self.direct = piece.direct
        self.send_sem, self.recv_sem = send_sem, recv_sem
        self.rows, self.cols, self.others = piece.window(place, whole.shape)
        self.half = piece.sizes(whole.shape)[1]
        self.base = place.core * (whole.shape[3] // 2) + piece.strip * self.half

    @staticmethod
    def scratch(rows, half):
        return [
            pltpu.VMEM((4, 4, rows, half), BF16),
            pltpu.VMEM((2, 4, rows, half), BF16),
            pltpu.VMEM((4, rows, half), BF16),
            pltpu.VMEM((3, rows, half), BF16),
        ]

    def add(self, near, block):
        blocks = self.half // 128
        whole, base, rows = self.whole, self.base, self.rows

        @pl.loop(0, 4 * blocks)
        def _(i):
            far, b = lax.div(i, blocks), lax.rem(i, blocks)
            here = pl.ds(pl.multiple_of(base + b * 128, 128), 128)
            there = pl.ds(pl.multiple_of(b * 128, 128), 128)
            total = whole[far, near, rows, here].astype(F32) + block[far, :, there].astype(F32)
            whole[far, near, rows, here] = total.astype(BF16)

    def start(self):
        send(
            self.whole.at[pl.ds(0, 4), pl.ds(0, 4), self.rows, self.others],
            self.landing[0],
            self.send_sem.at[0],
            self.recv_sem.at[0],
            self.place.sibling(),
        )

    def second(self):
        place = self.place
        await_bytes(self.landing[0], self.recv_sem.at[0])
        blocks = self.half // 128
        whole, base, rows, block = self.whole, self.base, self.rows, self.landing[0]

        @pl.loop(0, 16 * blocks)
        def _(i):
            group, b = lax.div(i, blocks), lax.rem(i, blocks)
            far, near = lax.div(group, 4), lax.rem(group, 4)
            here = pl.ds(pl.multiple_of(base + b * 128, 128), 128)
            there = pl.ds(pl.multiple_of(b * 128, 128), 128)
            total = whole[far, near, rows, here].astype(F32) + block[far, near, :, there].astype(F32)
            whole[far, near, rows, here] = total.astype(BF16)

        if self.direct:
            landings = (self.landing[1].at[0], self.landing[1].at[1], self.landing[2])
            for k, near in enumerate((place.second, place.both, place.first)):
                send(
                    whole.at[pl.ds(0, 4), near, self.rows, self.cols],
                    landings[k],
                    self.send_sem.at[max(k, 1)],
                    self.recv_sem.at[max(k, 1)],
                    place.device(near=near),
                )
            return
        for k, near in enumerate((place.second, place.both)):
            send(
                whole.at[pl.ds(0, 4), near, self.rows, self.cols],
                self.landing[1].at[k],
                self.send_sem.at[1],
                self.recv_sem.at[1],
                place.device(near=place.second),
            )

    def first(self):
        place = self.place
        await_bytes(self.landing[1], self.recv_sem.at[1])
        if self.direct:
            self.add(place.near, self.landing[1].at[1])
            self.add(place.near, self.landing[1].at[0])
            return
        self.add(place.first, self.landing[1].at[1])
        send(
            self.whole.at[pl.ds(0, 4), place.first, self.rows, self.cols],
            self.landing[2],
            self.send_sem.at[2],
            self.recv_sem.at[2],
            place.device(near=place.first),
        )
        self.add(place.near, self.landing[1].at[0])

    def fars(self):
        place = self.place
        await_bytes(self.landing[2], self.recv_sem.at[2])
        self.add(place.near, self.landing[2])
        for k in range(1, 4):
            far = lax.rem(place.far + k, 4)
            send(
                self.whole.at[far, place.near, self.rows, self.cols],
                self.landing[3].at[k - 1],
                self.send_sem.at[3],
                self.recv_sem.at[3],
                place.device(far=far),
            )

    def cross(self):
        place = self.place
        await_bytes(self.landing[3], self.recv_sem.at[3])
        blocks = self.half // 128
        whole, base, rows, block, done = self.whole, self.base, self.rows, self.landing[3], self.done

        @pl.loop(0, blocks)
        def _(b):
            here = pl.ds(pl.multiple_of(base + b * 128, 128), 128)
            there = pl.ds(pl.multiple_of(b * 128, 128), 128)
            total = whole[place.far, place.near, rows, here].astype(F32)
            for k in range(3):
                total = total + block[k, :, there].astype(F32)
            done[rows, here] = total.astype(BF16)

        half = done.at[self.rows, self.cols]
        send(half, half, self.send_sem.at[4], self.recv_sem.at[4], place.sibling())

    def finish(self):
        await_bytes(self.done.at[self.rows, self.others], self.recv_sem.at[4])

    def settle(self):
        await_bytes(self.landing[0], self.send_sem.at[0])
        await_bytes(self.landing[1], self.send_sem.at[1])
        await_bytes(self.landing[2], self.send_sem.at[2])
        await_bytes(self.landing[3], self.send_sem.at[3])
        await_bytes(self.done.at[self.rows, self.cols], self.send_sem.at[4])
EPS = 1e-05
KERNEL_ID = 1
NARROW, SPATIAL, WIDEN, SHRINK, STRIDE, EXPAND, BYPASS = range(7)
TABLE = 7
LAST = 5
NN = (((1,), (0,)), ((), ()))
NT = (((1,), (1,)), ((), ()))
TN = (((0,), (0,)), ((), ()))


def mul(a, b, dims):
    return lax.dot_general(a, b, dims, preferred_element_type=F32)


def lanes(i, width=128):
    return pl.ds(pl.multiple_of(i * width, width), width)


def normal_parts(value):
    bell = jnp.exp(-0.5 * value * value) * 0.3989422804014327
    step = 1.0 / (1.0 + 0.2316419 * jnp.abs(value))
    series = 1.330274429 * step - 1.821255978
    series = series * step + 1.781477937
    series = series * step - 0.356563782
    series = series * step + 0.319381530
    tail = bell * (series * step)
    cdf = jnp.where(value >= 0.0, 1.0 - tail, tail)
    return cdf, value * bell


class Image:
    def __init__(self, index, group, side, at, half_at):
        self.index, self.group, self.side = index, group, side
        self.half_side = (side - 1) // 2 + 1
        self.at, self.count = at, (side + 1) * 16
        self.half_at, self.half_count = half_at, -(-(self.half_side + 1) * 8 // 16) * 16

    def rows(self, half):
        return pl.ds(self.half_at, self.half_count) if half else pl.ds(self.at, self.count)

    def inside(self, half):
        count = self.half_count if half else self.count
        side = self.half_side if half else self.side
        bits = 3 if half else 4
        place = lax.broadcasted_iota(jnp.int32, (count, 128), 0)
        return jnp.logical_and(
            lax.shift_right_logical(place, bits) < side, lax.bitwise_and(place, (1 << bits) - 1) < side
        )


def images_of(counts, sides):
    images, at, half_at = [], 0, 0
    for group in range(2):
        for _ in range(counts[group]):
            image = Image(len(images), group, sides[group], at, half_at)
            images.append(image)
            at += image.count
            half_at += image.half_count
    return images, at, half_at


def widths_of(c_in, mid1, mid2, c_out):
    return [mid1, mid1, c_in, mid2, mid2, c_out, c_out]


class Layer:
    def __init__(self, width, half, at):
        self.width, self.half, self.at = width, half, at


def rows_piece(whole, start, count, cols):
    rows, pieces = whole.shape[2], []
    while count:
        shard, skip = divmod(start, rows)
        taken = min(rows - skip, count)
        pieces.append(whole[shard // 4, shard % 4, skip : skip + taken, cols])
        start, count = start + taken, count - taken
    return pieces[0] if len(pieces) == 1 else jnp.concatenate(pieces, axis=0)


def store_piece(whole, start, value):
    rows, done = whole.shape[2], 0
    while done < value.shape[0]:
        shard, skip = divmod(start + done, rows)
        taken = min(rows - skip, value.shape[0] - done)
        whole[shard // 4, shard % 4, skip : skip + taken, :] = value[done : done + taken]
        done += taken


def table_places(shares):
    places, at = [], 0
    for share in shares:
        if at % 128 + share > 128:
            at = -(-at // 128) * 128
        places.append(at)
        at += share
    return places


def step_kernel(spare, images, widths, refs):
    place = Place(spare)
    full_rows, half_rows = refs.x.shape[0], refs.cot.shape[0]
    hot, cnt = refs.hot_v, refs.cnt
    whole = refs.whole
    c_in, mid1, mid2, c_out = widths
    loads = []

    def load(src, dst):
        copy = pltpu.make_async_copy(src, dst, refs.load_sem.at[len(loads)])
        copy.start()
        loads.append(copy)
        return copy

    gathers = [
        Gather(place, whole[piece.layer], piece, refs.gather_send.at[k], refs.gather_recv.at[k])
        for k, piece in enumerate(PIECES)
    ]
    shard_loads = [
        load(
            refs.shards[item.piece.layer].at[item.rows, item.cols], item.part(place.far, place.near)
        )
        for item in gathers
    ]
    load_hot = load(refs.hot, hot)
    load_x = load(refs.x, refs.x_v)
    load_cot = load(refs.cot, refs.cot_v)
    scatters = [
        Scatter(
            place,
            whole[piece.layer],
            piece,
            refs.landing[k],
            refs.done[piece.layer],
            refs.scatter_send.at[k],
            refs.scatter_recv.at[k],
        )
        for k, piece in enumerate(PIECES[:-1])
    ]

    def pieces_of(items, layer):
        return [item for item, piece in zip(items, PIECES) if piece.layer == layer]

    def arrive(layer):
        for item in pieces_of(gathers, layer):
            item.finish()

    def let_go(layer):
        for item in pieces_of(gathers, layer):
            item.settle()

    def send_off(layer):
        for item in pieces_of(scatters, layer):
            item.start()

    def begin(k):
        shard_loads[k].wait()
        gathers[k].start()

    points = []

    def point():
        now = len(points)
        points.append(now)
        for step, *items in PLAN.get(now, ()):
            for k in items:
                if step is BEGIN:
                    begin(k)
                else:
                    step(gathers[k] if step in GATHER_STEPS else scatters[k])

    greet([place.sibling()] + place.nears() + place.cross_nears() + place.fars() + place.rests())

    layers, lane = [], 0
    for k, width in enumerate(widths_of(*widths)):
        layers.append(Layer(width, k in (STRIDE, EXPAND, BYPASS), lane))
        lane += width
        layers[k].normed, layers[k].slope = refs.normed[k], refs.slope[k]
        layers[k].affine, layers[k].scale = refs.affine[k], refs.scale[k]

    def reduce(way, k, during=None):
        def between(p):
            if p < 2:
                point()
                if during is not None:
                    during(p)

        slots = refs.slots[way if k in (NARROW, LAST) else 0][k]
        Reduce(place, k == LAST, list(slots) + list(refs.sums_sem[way][k])).run(
            refs.given[way][k], refs.total[way][k], between
        )
        point()

    def hot_row(image, view):
        row = 2 * image.index + view
        return hot[row : row + 1, :]

    def of_image(image, by_view):
        row = 2 * image.group
        return hot_row(image, 0) * by_view[row : row + 1] + hot_row(image, 1) * by_view[row + 1 : row + 2]

    def by_view(values):
        out = []
        for group in range(2):
            for view in range(2):
                total = None
                for image in images:
                    if image.group == group:
                        term = values[image.index] * hot_row(image, view)
                        total = term if total is None else total + term
                out.append(total)
        return out

    def put_sums(st, cols, firsts, seconds):
        st[:, cols] = jnp.concatenate(by_view(firsts) + by_view(seconds), axis=0)

    def column_sum(value):
        return jnp.sum(value, axis=0, keepdims=True)

    def field_sums(layer, st, field, i, masked, cols=None):
        firsts, seconds = [], []
        for image in images:
            z = field(image, i)
            if masked:
                z = jnp.where(image.inside(layer.half), z, 0.0)
            firsts.append(column_sum(z))
            seconds.append(column_sum(z * z))
        put_sums(st, lanes(i) if cols is None else cols, firsts, seconds)

    def statistics(total):
        counted = cnt[0:4, :]
        mean = total[0:4] / counted
        return mean, lax.rsqrt(total[4:8] / counted - mean * mean + EPS)

    def normed_of(layer, image, cols, z, mean, scale):
        stretch = of_image(image, scale)
        layer.scale[image.index : image.index + 1, cols] = stretch
        return (z - of_image(image, mean)) * stretch

    def forward(name, field, sink, extra=None):
        layer = layers[name]

        @pl.loop(0, layer.width // 128)
        def _(i):
            cols = lanes(i)
            mean, scale = statistics(refs.total[0][name][:, cols])
            gain, bias = layer.affine[0:1, cols], layer.affine[1:2, cols]
            for image in images:
                rows, inside = image.rows(layer.half), image.inside(layer.half)
                normed = normed_of(layer, image, cols, field(image, i), mean, scale)
                value = normed * gain + bias
                if extra is not None:
                    value = value + extra[rows, cols].astype(F32)
                cdf, rest = normal_parts(value)
                layer.normed[rows, cols] = normed.astype(BF16)
                layer.slope[rows, cols] = jnp.where(inside, cdf + rest, 0.0).astype(BF16)
                sink(image, i, jnp.where(inside, value * cdf, 0.0))

    def gradient_sums(name, grad, st):
        layer = layers[name]

        @pl.loop(0, layer.width // 128)
        def _(i):
            cols = lanes(i)
            firsts, seconds = [], []
            for image in images:
                g = grad(image, i)
                firsts.append(column_sum(g))
                seconds.append(column_sum(g * layer.normed[image.rows(layer.half), cols].astype(F32)))
            put_sums(st, cols, firsts, seconds)

    def gradient(name, grad, sums, sink=None):
        layer = layers[name]

        @pl.loop(0, layer.width // 128)
        def _(i):
            cols = lanes(i)
            first, second = sums(i)
            here = pl.ds(pl.multiple_of(layer.at + i * 128, 128), 128)
            refs.daffine_v[0:1, here] = column_sum(second)
            refs.daffine_v[1:2, here] = column_sum(first)
            first, second = first / cnt[0:4, :], second / cnt[0:4, :]
            gain = layer.affine[0:1, cols]
            for image in images:
                rows = image.rows(layer.half)
                stretch = gain * layer.scale[image.index : image.index + 1, cols]
                normed = layer.normed[rows, cols].astype(F32)
                value = stretch * (grad(image, i) - of_image(image, first) - normed * of_image(image, second))
                value = jnp.where(image.inside(layer.half), value, 0.0)
                if sink is None:
                    layer.normed[rows, cols] = value.astype(BF16)
                else:
                    sink(image, i, value)

    def totals_of(name):
        def sums(i):
            total = refs.total[1][name][:, lanes(i)]
            return total[0:4], total[4:8]

        return sums

    def shifted(target, image, i, value):
        width = target.shape[1] // 3
        rows = pl.ds(16 + image.at, image.count)
        for q in range(3):
            moved = value if q == 1 else pltpu.roll(value, 1 if q == 0 else image.count - 1, 0)
            target[rows, pl.ds(pl.multiple_of(q * width + i * 128, 128), 128)] = moved.astype(BF16)

    def clear_ends(target, top, from_row):
        target[0:top, :] = jnp.zeros((top, target.shape[1]), target.dtype)
        target[from_row:, :] = jnp.zeros((target.shape[0] - from_row, target.shape[1]), target.dtype)

    def strided(start):
        return pl.ds(start, 8, stride=2)

    F, G, K, S = refs.F, refs.G, refs.K, refs.S
    x_v, taps1, act_spatial, upper = refs.x_v, refs.taps1, refs.act_spatial, refs.upper
    taps2, act_stride, even, grad3 = refs.taps2, refs.act_stride, refs.even, refs.grad3
    clear_ends(taps1, 16, 16 + full_rows)
    clear_ends(grad3, 16, 16 + full_rows)
    blocks2 = mid2 // 128
    K[:, 0:32, :] = jnp.zeros((blocks2, 32, 128), F32)
    K[:, 32 + full_rows :, :] = jnp.zeros((blocks2, K.shape[1] - 32 - full_rows, 128), F32)
    EVEN, SPREAD = refs.EVEN, refs.SPREAD
    SPREAD[...] = jnp.zeros(SPREAD.shape, F32)

    places = table_places([layer.width // 16 for layer in layers])

    def spread_affine(k):
        table, layer = whole[TABLE], layers[k]
        share = layer.width // 16
        row, skip = divmod(places[k], 128)
        to = lax.broadcasted_iota(jnp.int32, (16, 128), 1)
        owner = lax.broadcasted_iota(jnp.int32, (16, 128), 0)
        pick_from = lax.broadcasted_iota(jnp.int32, (128, 128), 0)
        pick_to = lax.broadcasted_iota(jnp.int32, (128, 128), 1)
        chosen = (pick_from == skip + lax.rem(pick_to, share)).astype(BF16)
        for kind in range(2):
            held = [
                table[g // 4, g % 4, :, :].astype(F32)[row + 4 * kind : row + 4 * kind + 1] for g in range(16)
            ]
            spread = mul(jnp.concatenate(held, axis=0).astype(BF16), chosen, NN)
            for b in range(layer.width // 128):
                mine = jnp.where(lax.div(b * 128 + to, share) == owner, spread, 0.0)
                layer.affine[kind : kind + 1, b * 128 : (b + 1) * 128] = column_sum(mine)

    load_hot.wait()
    load_x.wait()
    point()

    def plain(buffer):
        return lambda image, i: buffer[image.rows(False), lanes(i)]

    def plain_half(buffer):
        return lambda image, i: buffer[image.rows(True), lanes(i)]

    def halves(buffer, base):
        blocks = F.shape[1] // 128

        def field(image, i):
            band = base + lax.div(i, blocks)
            rows = pl.ds(pl.multiple_of(band * half_rows + image.half_at, 8), image.half_count)
            return buffer[rows, lanes(lax.rem(i, blocks))]

        return field

    arrive(NARROW)
    F[0:full_rows, 0:mid1] = mul(x_v[...], whole[NARROW][...].reshape(c_in, mid1), NN)

    @pl.loop(0, mid1 // 128)
    def _(i):
        field_sums(layers[NARROW], refs.given[0][NARROW], plain(F), i, False)

    pixels = []
    for image in images:
        pixels.append(jnp.full((1, 128), float(image.side * image.side), F32))
    empty = [jnp.zeros((1, 128), F32) for _ in images]
    put_sums(refs.given[0][NARROW], pl.ds(mid1, 128), pixels, empty)

    def during(p):
        if p == 0:
            for k in (NARROW, SPATIAL, WIDEN):
                spread_affine(k)

    point()
    reduce(0, NARROW, during)
    cnt[...] = refs.total[0][NARROW][:, mid1 : mid1 + 128]
    forward(NARROW, plain(F), functools.partial(shifted, taps1))

    point()
    arrive(SPATIAL)
    for r in range(3):
        kernel = rows_piece(whole[SPATIAL], r * 3 * mid1, 3 * mid1, slice(None))
        term = mul(taps1[16 * r : 16 * r + full_rows, :], kernel, NN)
        F[0:full_rows, 0:mid1] = term if r == 0 else F[0:full_rows, 0:mid1] + term

    @pl.loop(0, mid1 // 128)
    def _(i):
        field_sums(layers[SPATIAL], refs.given[0][SPATIAL], plain(F), i, True)

    def during(p):
        if p == 0:
            for k in (SHRINK, STRIDE):
                spread_affine(k)

    point()
    reduce(0, SPATIAL, during)

    def to_spatial(image, i, value):
        act_spatial[image.rows(False), lanes(i)] = value.astype(BF16)

    forward(SPATIAL, plain(F), to_spatial)

    point()
    arrive(WIDEN)

    @pl.loop(0, c_in // 256)
    def _(j):
        cols = lanes(j, 256)
        F[0:full_rows, cols] = mul(act_spatial[...], whole[WIDEN][:, :, :, cols].reshape(mid1, 256), NN)
        for k in range(2):
            field_sums(layers[WIDEN], refs.given[0][WIDEN], plain(F), 2 * j + k, False)

    def during(p):
        if p == 0:
            for k in (EXPAND, BYPASS):
                spread_affine(k)

    point()
    reduce(0, WIDEN, during)

    def to_upper(image, i, value):
        upper[image.rows(False), lanes(i)] = value.astype(BF16)
        rows = image.rows(False)
        EVEN[rows, :] = value
        for pair in range(image.half_count // 16):
            both = [EVEN[strided(image.at + 32 * min(2 * pair + k, image.half_side - 1)), :] for k in range(2)]
            here = pl.ds(image.half_at + 16 * pair, 16)
            even[here, lanes(i)] = jnp.concatenate(both, axis=0).astype(BF16)

    forward(WIDEN, plain(F), to_upper, x_v)

    point()
    arrive(SHRINK)

    @pl.loop(0, mid2 // 256)
    def _(j):
        cols = lanes(j, 256)
        F[0:full_rows, cols] = mul(upper[...], whole[SHRINK][:, :, :, cols].reshape(c_in, 256), NN)
        for k in range(2):
            field_sums(layers[SHRINK], refs.given[0][SHRINK], plain(F), 2 * j + k, False)

    point()
    reduce(0, SHRINK)

    def to_shrink(image, i, value):
        K[i, pl.ds(32 + image.at, image.count), :] = value

    forward(SHRINK, plain(F), to_shrink)

    for image in images:

        @pl.loop(0, image.half_count // 16)
        def _(pair):
            rows = pl.ds(pl.multiple_of(image.half_at + 16 * pair, 16), 16)
            for r in range(3):
                for q in range(3):
                    start = 32 + image.at + 64 * pair + (r - 1) * 16 + q - 1
                    for b in range(blocks2):
                        both = [K[b, strided(start + 32 * k), :] for k in range(2)]
                        at = (3 * r + q) * mid2 + b * 128
                        taps2[rows, at : at + 128] = jnp.concatenate(both, axis=0).astype(BF16)

    point()
    arrive(STRIDE)

    @pl.loop(0, mid2 // 256)
    def _(j):
        cols = lanes(j, 256)
        depth = 9 * mid2 // 4
        for far in range(4):
            kernel = whole[STRIDE][far, :, :, cols].reshape(depth, 256)
            term = mul(taps2[:, far * depth : (far + 1) * depth], kernel, NN)
            G[:, cols] = term if far == 0 else G[:, cols] + term
        for k in range(2):
            field_sums(layers[STRIDE], refs.given[0][STRIDE], plain_half(G), 2 * j + k, True)

    def bypass_field():
        arrive(BYPASS)

        @pl.loop(0, c_out // 256)
        def _(j):
            value = mul(even[...], whole[BYPASS][:, :, :, lanes(j, 256)].reshape(c_in, 256), NN)
            blocks = c_in // 256
            rows = pl.ds(pl.multiple_of((2 + lax.div(j, blocks)) * half_rows, 8), half_rows)
            F[rows, lanes(lax.rem(j, blocks), 256)] = value
            for k in range(2):
                i = 2 * j + k
                cols = pl.ds(pl.multiple_of(c_out + i * 128, 128), 128)
                field_sums(layers[BYPASS], refs.given[0][LAST], halves(F, 2), i, True, cols)

    point()
    reduce(0, STRIDE)

    def to_stride(image, i, value):
        act_stride[image.rows(True), lanes(i)] = value.astype(BF16)

    forward(STRIDE, plain_half(G), to_stride)

    point()
    arrive(EXPAND)

    @pl.loop(0, c_out // 256)
    def _(j):
        value = mul(act_stride[...], whole[EXPAND][:, :, :, lanes(j, 256)].reshape(mid2, 256), NN)
        blocks = c_in // 256
        rows = pl.ds(pl.multiple_of(lax.div(j, blocks) * half_rows, 8), half_rows)
        F[rows, lanes(lax.rem(j, blocks), 256)] = value
        for k in range(2):
            field_sums(layers[EXPAND], refs.given[0][LAST], halves(F, 0), 2 * j + k, True)

    point()
    bypass_field()
    reduce(0, LAST)
    load_cot.wait()
    expand_z, bypass_z = halves(F, 0), halves(F, 2)

    @pl.loop(0, c_out // 128)
    def _(i):
        cols = lanes(i)
        upper_cols = pl.ds(pl.multiple_of(c_out + i * 128, 128), 128)
        stats_e = statistics(refs.total[0][LAST][:, cols])
        stats_b = statistics(refs.total[0][LAST][:, upper_cols])
        el, bl = layers[EXPAND], layers[BYPASS]
        firsts, seconds, thirds = [], [], []
        for image in images:
            rows, inside = image.rows(True), image.inside(True)
            normed_e = normed_of(el, image, cols, expand_z(image, i), *stats_e)
            normed_b = normed_of(bl, image, cols, bypass_z(image, i), *stats_b)
            value = normed_e * el.affine[0:1, cols] + el.affine[1:2, cols]
            value = value + (normed_b * bl.affine[0:1, cols] + bl.affine[1:2, cols])
            cdf, rest = normal_parts(value)
            el.normed[rows, cols] = normed_e.astype(BF16)
            bl.normed[rows, cols] = normed_b.astype(BF16)
            grad = jnp.where(inside, refs.cot_v[rows, cols].astype(F32) * (cdf + rest), 0.0)
            refs.cot_v[rows, cols] = (value * cdf).astype(BF16)
            blocks = F.shape[1] // 128
            band = lax.div(i, blocks)
            here = pl.ds(pl.multiple_of(band * half_rows + image.half_at, 8), image.half_count)
            F[here, lanes(lax.rem(i, blocks))] = grad
            firsts.append(column_sum(grad))
            seconds.append(column_sum(grad * normed_e))
            thirds.append(column_sum(grad * normed_b))
        put_sums(refs.given[1][LAST], cols, firsts, seconds)
        put_sums(refs.given[1][LAST], upper_cols, thirds, thirds)

    store_out = pltpu.make_async_copy(refs.cot_v, refs.out, refs.store_sem.at[0])
    store_out.start()
    point()
    reduce(1, LAST)

    def sums_expand(i):
        total = refs.total[1][LAST][:, lanes(i)]
        return total[0:4], total[4:8]

    def sums_bypass(i):
        first = refs.total[1][LAST][:, lanes(i)]
        second = refs.total[1][LAST][:, pl.ds(pl.multiple_of(c_out + i * 128, 128), 128)]
        return first[0:4], second[0:4]

    gradient(EXPAND, halves(F, 0), sums_expand)
    gradient(BYPASS, halves(F, 0), sums_bypass)
    expand_grad, bypass_grad = layers[EXPAND].normed, layers[BYPASS].normed

    point()
    @pl.loop(0, mid2 // 256)
    def _(j):
        kernel = whole[EXPAND][pl.ds(2 * j, 2)].reshape(256, c_out)
        cols = lanes(j, 256)
        G[:, cols] = mul(expand_grad[...], kernel, NT) * layers[STRIDE].slope[:, cols].astype(F32)

    gradient_sums(STRIDE, plain_half(G), refs.given[1][STRIDE])

    def filter_grad(name, left, right, fars):
        let_go(name)
        target = whole[name]
        shard, columns = target.shape[2], target.shape[3]
        depth = fars * 4 * shard
        width = min(columns, 512 if depth <= 512 else 256)

        @pl.loop(0, (4 // fars) * (columns // width))
        def _(i):
            j, b = lax.div(i, columns // width), lax.rem(i, columns // width)
            value = mul(left[:, lanes(j, depth)], right[:, lanes(b, width)], TN)
            target[pl.ds(j * fars, fars), :, :, lanes(b, width)] = value.astype(BF16).reshape(fars, 4, shard, width)

    def during(p):
        if p == 0:
            filter_grad(EXPAND, act_stride, expand_grad, 2)
            send_off(EXPAND)
        if p == 1:

            @pl.loop(0, 4)
            def _(j):
                kernel = whole[BYPASS][j].reshape(256, c_out)
                S[pl.ds(pl.multiple_of(j * half_rows, 8), half_rows), :] = mul(bypass_grad[...], kernel, NT)

            filter_grad(BYPASS, even, bypass_grad, 1)
            send_off(BYPASS)

    point()
    reduce(1, STRIDE, during)
    gradient(STRIDE, plain_half(G), totals_of(STRIDE))
    stride_grad = layers[STRIDE].normed

    point()
    K[...] = jnp.zeros(K.shape, F32)
    for r in range(3):
        for q in range(3):
            kernel = rows_piece(whole[STRIDE], (3 * r + q) * mid2, mid2, slice(None))
            F[0:half_rows, 0:mid2] = mul(stride_grad[...], kernel, NT)
            for image in images:

                @pl.loop(0, image.half_side)
                def _(i):
                    there = strided(32 + image.at + 32 * i + (r - 1) * 16 + q - 1)
                    here = pl.ds(pl.multiple_of(image.half_at + 8 * i, 8), 8)
                    for b in range(blocks2):
                        K[b, there, :] = K[b, there, :] + F[here, b * 128 : (b + 1) * 128]

    @pl.loop(0, mid2 // 128)
    def _(i):
        cols = lanes(i)
        firsts, seconds = [], []
        for image in images:
            rows = pl.ds(32 + image.at, image.count)
            g = K[i, rows, :] * layers[SHRINK].slope[image.rows(False), cols].astype(F32)
            K[i, rows, :] = g
            firsts.append(column_sum(g))
            seconds.append(column_sum(g * layers[SHRINK].normed[image.rows(False), cols].astype(F32)))
        put_sums(refs.given[1][SHRINK], cols, firsts, seconds)

    def during(p):
        if p == 0:
            filter_grad(STRIDE, taps2, stride_grad, 1)
            send_off(STRIDE)

    point()
    reduce(1, SHRINK, during)
    gradient(SHRINK, lambda image, i: K[i, pl.ds(32 + image.at, image.count), :], totals_of(SHRINK))
    shrink_grad = layers[SHRINK].normed

    point()

    @pl.loop(0, 4)
    def _(j):
        cols = lanes(j, 256)
        kernel = whole[SHRINK][j].reshape(256, mid2)
        F[0:full_rows, cols] = mul(shrink_grad[...], kernel, NT)

    @pl.loop(0, c_in // 128)
    def _(i):
        cols = lanes(i)
        firsts, seconds = [], []
        for image in images:
            rows = image.rows(False)
            for j in range(image.half_side):
                start = pl.multiple_of(lax.div(i, 2) * half_rows + image.half_at + 8 * j, 8)
                SPREAD[strided(image.at + 32 * j), :] = S[pl.ds(start, 8), lanes(lax.rem(i, 2))]
            g = (F[rows, cols] + SPREAD[rows, :]) * layers[WIDEN].slope[rows, cols].astype(F32)
            F[rows, cols] = g
            firsts.append(column_sum(g))
            seconds.append(column_sum(g * layers[WIDEN].normed[rows, cols].astype(F32)))
        put_sums(refs.given[1][WIDEN], cols, firsts, seconds)

    def during(p):
        if p == 0:
            filter_grad(SHRINK, upper, shrink_grad, 1)
            send_off(SHRINK)

    point()
    reduce(1, WIDEN, during)
    gradient(WIDEN, plain(F), totals_of(WIDEN))
    widen_grad = layers[WIDEN].normed

    point()
    S[0:full_rows, :] = mul(widen_grad[...], whole[WIDEN][...].reshape(mid1, c_in), NT) * layers[SPATIAL].slope[...].astype(F32)
    gradient_sums(SPATIAL, plain(S), refs.given[1][SPATIAL])

    def during(p):
        if p == 0:
            filter_grad(WIDEN, act_spatial, widen_grad, 4)
            send_off(WIDEN)

    point()
    reduce(1, SPATIAL, during)
    gradient(SPATIAL, plain(S), totals_of(SPATIAL), functools.partial(shifted, grad3))

    point()
    for r in range(3):
        kernel = jnp.concatenate(
            [rows_piece(whole[SPATIAL], (3 * r + 2 - q) * mid1, mid1, slice(None)) for q in range(3)], axis=1
        )
        term = mul(grad3[16 * (2 - r) : 16 * (2 - r) + full_rows, :], kernel, NT)
        S[0:full_rows, :] = term if r == 0 else S[0:full_rows, :] + term
    S[0:full_rows, :] = S[0:full_rows, :] * layers[NARROW].slope[...].astype(F32)
    gradient_sums(NARROW, plain(S), refs.given[1][NARROW])

    def during(p):
        if p == 0:
            let_go(SPATIAL)
            for r in range(3):
                value = mul(taps1[16 * r : 16 * r + full_rows, :], grad3[16 : 16 + full_rows, mid1 : 2 * mid1], TN)
                store_piece(whole[SPATIAL], r * 3 * mid1, value.astype(BF16))
            send_off(SPATIAL)

    point()
    reduce(1, NARROW, during)
    gradient(NARROW, plain(S), totals_of(NARROW))
    narrow_grad = layers[NARROW].normed

    point()
    for j in range(4):
        upper[0:256, j * mid1 : (j + 1) * mid1] = whole[NARROW][j].reshape(256, mid1)
    filter_grad(NARROW, x_v, narrow_grad, 1)
    send_off(NARROW)
    point()
    for j in range(4):
        cols = slice(j * 256, (j + 1) * 256)
        kernel = upper[0:256, j * mid1 : (j + 1) * mid1]
        x_v[:, cols] = (F[0:full_rows, cols] + mul(narrow_grad[...], kernel, NT)).astype(BF16)
        point()
    stores = [
        pltpu.make_async_copy(x_v, refs.dinput, refs.store_sem.at[1]),
        pltpu.make_async_copy(refs.daffine_v, refs.daffine, refs.store_sem.at[2]),
    ]
    for store in stores:
        store.start()
    point()
    for k in (EXPAND, BYPASS, STRIDE, SHRINK, WIDEN, SPATIAL, NARROW):
        for item in pieces_of(scatters, k):
            item.finish()
        stores.append(pltpu.make_async_copy(refs.done[k], refs.dfilter[k], refs.store_sem.at[3 + k]))
        stores[-1].start()
    for item in scatters:
        item.settle()
    let_go(TABLE)
    store_out.wait()
    for store in stores:
        store.wait()


PIECES = [
    Piece(NARROW, direct=True),
    Piece(SPATIAL),
    Piece(WIDEN),
    Piece(SHRINK),
    Piece(STRIDE, 0, 2, 0, 2),
    Piece(STRIDE, 0, 2, 1, 2),
    Piece(STRIDE, 1, 2, 0, 2),
    Piece(STRIDE, 1, 2, 1, 2),
    Piece(EXPAND, 0, 1, 0, 2),
    Piece(EXPAND, 0, 1, 1, 2),
    Piece(BYPASS, 0, 1, 0, 4),
    Piece(BYPASS, 0, 1, 1, 4),
    Piece(BYPASS, 0, 1, 2, 4),
    Piece(BYPASS, 0, 1, 3, 4),
    Piece(TABLE, halved=False, direct=True),
]
N, S, W, K, T0, T1, T2, T3, E0, E1, B0, B1, B2, B3, TAB = range(15)
BEGIN = object()
GATHER_STEPS = (Gather.near, Gather.forward, Gather.cross)
NEAR, FORWARD, CROSS = GATHER_STEPS
R2, R3, R4, R5 = Scatter.second, Scatter.first, Scatter.fars, Scatter.cross
PLAN = {
    0: [
        (BEGIN, TAB, N),
        (NEAR, TAB, N),
        (BEGIN, S, W, K, T0),
        (FORWARD, TAB, N),
        (CROSS, N),
        (NEAR, S),
    ],
    1: [(CROSS, TAB)],
    2: [(FORWARD, S), (NEAR, W, K), (BEGIN, T1)],
    3: [(CROSS, S)],
    4: [(FORWARD, W), (NEAR, T0), (BEGIN, T2)],
    6: [(CROSS, W)],
    7: [(FORWARD, K, T0), (NEAR, T1), (BEGIN, T3)],
    8: [(CROSS, K, T0)],
    9: [(NEAR, T2), (BEGIN, E0)],
    12: [(FORWARD, T1, T2), (NEAR, T3), (BEGIN, E1)],
    13: [(CROSS, T1, T2)],
    14: [(NEAR, E0), (FORWARD, T3), (BEGIN, B0)],
    17: [(FORWARD, E0), (NEAR, E1), (BEGIN, B1)],
    18: [(CROSS, T3, E0)],
    19: [(NEAR, B0), (BEGIN, B2)],
    22: [(FORWARD, E1, B0), (NEAR, B1), (BEGIN, B3)],
    23: [(CROSS, E1, B0)],
    24: [(NEAR, B2), (FORWARD, B1)],
    25: [(NEAR, B3), (FORWARD, B2), (CROSS, B1)],
    26: [(FORWARD, B3), (CROSS, B2, B3)],
    37: [(R2, E0, E1)],
    38: [(R2, B0)],
    39: [(R3, E0, E1), (R2, B1)],
    40: [(R4, E0)],
    41: [(R3, B0, B1), (R2, B2), (R4, E1)],
    42: [(R5, E0)],
    43: [(R2, B3), (R3, B2), (R4, B0)],
    44: [(R2, T0), (R4, B1)],
    46: [(R3, B3, T0), (R2, T1), (R4, B2)],
    47: [(R5, E1, B0)],
    48: [(R2, T2), (R4, B3)],
    49: [(R3, T1), (R4, T0)],
    51: [(R3, T2), (R2, T3), (R4, T1)],
    52: [(R5, B1, B2)],
    53: [(R2, K), (R3, T3), (R4, T2)],
    54: [(R2, W)],
    56: [(R3, K, W), (R4, T3)],
    57: [(R5, B3, T0, T1), (R2, S)],
    58: [(R3, S), (R4, K, W)],
    60: [(R4, S), (R5, T2, T3)],
    61: [(R5, K, W)],
    62: [(R2, N)],
    63: [(R5, S)],
    65: [(R3, N), (R4, N), (R5, N)],
}


def spare_groups(spare):
    count = lax.axis_size("dp")
    return [list(range(at, at + spare)) for at in range(0, count, spare)]


def padded(field, rows, across):
    side = field.shape[1]
    field = jnp.pad(field, ((0, 0), (0, rows - side), (0, across - side), (0, 0)))
    return field.reshape(-1, field.shape[3])


def local(
    input_big,
    input_small,
    views_big,
    views_small,
    cotan_big,
    cotan_small,
    *params,
):
    filters, affines = params[0::2], params[1::2]
    devices = lax.axis_size("dp")
    spare = devices // 16
    inputs, cotans, views = (input_big, input_small), (cotan_big, cotan_small), (views_big, views_small)
    counts = [item.shape[0] for item in inputs]
    images, full_rows, half_rows = images_of(counts, [item.shape[1] for item in inputs])
    c_in, c_out = input_big.shape[3], cotan_big.shape[3]
    mid1, mid2 = filters[NARROW].shape[1], filters[SHRINK].shape[1]
    widths = (c_in, mid1, mid2, c_out)
    wide = widths_of(*widths)
    by_group = [next(image for image in images if image.group == g) for g in range(2)]
    x = jnp.concatenate([padded(inputs[g], by_group[g].count // 16, 16) for g in range(2)])
    cot = jnp.concatenate([padded(cotans[g], by_group[g].half_count // 8, 8) for g in range(2)])
    view = jnp.concatenate(views)
    hot = (view[:, None] == jnp.arange(2, dtype=jnp.int32)[None, :]).astype(F32)
    hot = jnp.broadcast_to(hot.reshape(-1, 1), (2 * len(images), 128))

    parts = [item.T for item in affines]
    shards = list(filters)
    if spare > 1:
        groups = spare_groups(spare)
        shards = [lax.all_gather(item, "dp", axis_index_groups=groups, tiled=True) for item in filters]
        gathered = lax.all_gather(jnp.concatenate(parts, axis=1), "dp", axis_index_groups=groups)
        parts, at = [], 0
        for item in affines:
            share = item.shape[0]
            parts.append(jnp.moveaxis(gathered[:, :, at : at + share], 0, 1).reshape(2, -1))
            at += share
    places = table_places([item.shape[1] for item in parts]) + [512]
    parts = [
        jnp.pad(item, ((0, 0), (0, places[k + 1] - places[k] - item.shape[1]))) for k, item in enumerate(parts)
    ]
    shards.append(jnp.pad(jnp.concatenate(parts, axis=1).reshape(8, 128), ((0, 8), (0, 0))))
    shapes = [item.shape for item in shards]
    lane_total = sum(wide)

    def field(*shape):
        return pltpu.VMEM(shape, F32)

    def rounded(*shape):
        return pltpu.VMEM(shape, BF16)

    def layer_rows(k):
        return half_rows if k in (STRIDE, EXPAND, BYPASS) else full_rows

    rounds = [wide[:5] + [2 * c_out], wide[:5] + [2 * c_out]]
    rounds[0][NARROW] += 128
    sums = [[Reduce.scratch(8, width, spare, k == LAST) for k, width in enumerate(way)] for way in rounds]
    slots = [[item[:-2] for item in way] for way in sums]
    slots[1] = [item if k in (NARROW, LAST) else [] for k, item in enumerate(slots[1])]
    operands = dict(x=x, cot=cot, hot=hot, shards=shards)
    results = dict(
        out=jax.ShapeDtypeStruct((half_rows, c_out), BF16),
        dinput=jax.ShapeDtypeStruct((full_rows, c_in), BF16),
        daffine=jax.ShapeDtypeStruct((8, lane_total), F32),
        dfilter=[jax.ShapeDtypeStruct(shape, BF16) for shape in shapes[:7]],
    )
    scratch = dict(
        whole=[rounded(4, 4, *shape) for shape in shapes],
        done=[rounded(*shape) for shape in shapes[:7]],
        landing=[Scatter.scratch(*piece.sizes(shapes[piece.layer])) for piece in PIECES[:-1]],
        normed=[rounded(layer_rows(k), wide[k]) for k in range(7)],
        slope=[None if k in (EXPAND, BYPASS) else rounded(layer_rows(k), wide[k]) for k in range(7)],
        affine=[field(8, width) for width in wide],
        scale=[field(-(-len(images) // 8) * 8, width) for width in wide],
        x_v=rounded(full_rows, c_in),
        cot_v=rounded(half_rows, c_out),
        hot_v=field(*hot.shape),
        cnt=field(8, 128),
        daffine_v=field(8, lane_total),
        F=field(max(full_rows, 4 * half_rows), c_in),
        G=field(half_rows, mid2),
        S=field(max(full_rows, 4 * half_rows), mid1),
        K=field(mid2 // 128, full_rows + 64, 128),
        EVEN=field(full_rows, 128),
        SPREAD=field(full_rows, 128),
        taps1=rounded(full_rows + 32, 3 * mid1),
        grad3=rounded(full_rows + 32, 3 * mid1),
        act_spatial=rounded(full_rows, mid1),
        upper=rounded(full_rows, c_in),
        taps2=rounded(half_rows, 9 * mid2),
        act_stride=rounded(half_rows, mid2),
        even=rounded(half_rows, c_in),
        given=[[field(8, width) for width in way] for way in rounds],
        total=[[field(8, width) for width in way] for way in rounds],
        slots=slots,
        sums_sem=[[item[-2:] for item in way] for way in sums],
        load_sem=pltpu.SemaphoreType.DMA((len(PIECES) + 3,)),
        store_sem=pltpu.SemaphoreType.DMA((16,)),
        gather_send=pltpu.SemaphoreType.DMA((len(PIECES), Gather.PHASES)),
        gather_recv=pltpu.SemaphoreType.DMA((len(PIECES), Gather.PHASES)),
        scatter_send=pltpu.SemaphoreType.DMA((len(PIECES), Scatter.PHASES)),
        scatter_recv=pltpu.SemaphoreType.DMA((len(PIECES), Scatter.PHASES)),
    )
    flat_in, in_tree = jax.tree.flatten(operands)
    flat_out, out_tree = jax.tree.flatten(results)
    flat_scratch, scratch_tree = jax.tree.flatten(scratch)

    def kernel(*flat):
        here = len(flat_in) + len(flat_out)
        refs = jax.tree.unflatten(in_tree, flat[: len(flat_in)])
        refs |= jax.tree.unflatten(out_tree, flat[len(flat_in) : here])
        refs |= jax.tree.unflatten(scratch_tree, flat[here:])
        step_kernel(spare, images, widths, types.SimpleNamespace(**refs))

    flat_out = pl.pallas_call(
        kernel,
        out_shape=flat_out,
        in_specs=[pl.BlockSpec(memory_space=pl.ANY)] * len(flat_in),
        out_specs=[pl.BlockSpec(memory_space=pl.ANY)] * len(flat_out),
        scratch_shapes=flat_scratch,
        compiler_params=pltpu.CompilerParams(
            collective_id=KERNEL_ID, has_side_effects=True, vmem_limit_bytes=VMEM_BYTES
        ),
    )(*flat_in)
    done = types.SimpleNamespace(**jax.tree.unflatten(out_tree, flat_out))

    def unpadded(rows, half):
        outs = []
        for group in range(2):
            image, width = by_group[group], rows.shape[1]
            across, side = (8, image.half_side) if half else (16, image.side)
            start = image.half_at if half else image.at
            count = image.half_count if half else image.count
            part = rows[start : start + counts[group] * count].reshape(counts[group], count // across, across, width)
            outs.append(part[:, :side, :side])
        return outs

    me = lax.axis_index("dp")
    outs = unpadded(done.out, True) + unpadded(done.dinput, False)
    at = 0
    for k, grad in enumerate(done.dfilter):
        if spare > 1:
            grad = lax.psum_scatter(grad.astype(F32), "dp", axis_index_groups=spare_groups(spare), tiled=True)
        share = wide[k] // devices
        affine = lax.dynamic_slice(done.daffine, (0, at + me * share), (2, share)).T
        outs += [grad.astype(F32), affine]
        at += wide[k]
    return tuple(outs)


VMEM_BYTES = 65400 * 1024


def solution(mesh):
    images = P(("dp", "outer"), None, None, None)
    rows = P("dp", None)
    return jax.shard_map(
        local,
        mesh=mesh,
        in_specs=(images, images, P(("dp", "outer")), P(("dp", "outer")), images, images) + (rows,) * 14,
        out_specs=(images,) * 4 + (rows,) * 14,
        check_vma=False,
    )
```

```python
import functools
import types

import jax
import jax.numpy as jnp
from jax import lax
from jax.experimental import pallas as pl
from jax.experimental.pallas import tpu as pltpu
from jax.sharding import PartitionSpec as P

MESH = pl.DeviceIdType.MESH
F32 = jnp.float32
BF16 = jnp.bfloat16


class Place:
    def __init__(self, spare):
        self.spare = spare
        dp = lax.axis_index("dp")
        self.core = lax.axis_index("outer")
        self.rest = lax.rem(dp, spare)
        group = lax.div(dp, spare)
        self.far = lax.div(group, 4)
        self.near = lax.rem(group, 4)
        high, low = lax.div(self.near, 2), lax.rem(self.near, 2)
        self.first = 2 * lax.rem(high + 1 - self.core, 2) + lax.rem(low + self.core, 2)
        self.second = 2 * lax.rem(high + self.core, 2) + lax.rem(low + 1 - self.core, 2)
        self.both = 3 - self.near

    def device(self, far=None, near=None, core=None, rest=None):
        far = self.far if far is None else far
        near = self.near if near is None else near
        core = self.core if core is None else core
        rest = self.rest if rest is None else rest
        return ((far * 4 + near) * self.spare + rest, core)

    def fars(self):
        return [self.device(far=lax.rem(self.far + k, 4)) for k in range(1, 4)]

    def nears(self):
        return [self.device(near=lax.rem(self.near + k, 4)) for k in range(1, 4)]

    def cross_nears(self):
        return [
            self.device(near=lax.rem(self.near + k, 4), core=1 - self.core) for k in range(1, 4)
        ]

    def sibling(self):
        return self.device(core=1 - self.core)

    def rests(self):
        return [
            self.device(rest=lax.rem(self.rest + k, self.spare)) for k in range(1, self.spare)
        ]


def greet(devices):
    barrier = pltpu.get_barrier_semaphore()
    for device in devices:
        pl.semaphore_signal(barrier, inc=1, device_id=device, device_id_type=MESH)
    pl.semaphore_wait(barrier, len(devices))


def send(src, dst, send_sem, recv_sem, device):
    pltpu.make_async_remote_copy(
        src_ref=src,
        dst_ref=dst,
        send_sem=send_sem,
        recv_sem=recv_sem,
        device_id=device,
        device_id_type=MESH,
    ).start()


def await_bytes(like, sem):
    pltpu.make_async_copy(like, like, sem).wait()


class Reduce:
    def __init__(self, place, split, refs):
        self.place = place
        self.split = split
        self.refs = refs

    @staticmethod
    def scratch(rows, width, spare, split, kind=F32):
        piece = width // 2 if split else width
        shapes = []
        for count in Reduce.counts(spare, split):
            shapes.append(pltpu.VMEM((count, rows, piece), kind))
            shapes.append(pltpu.VMEM((rows, piece), kind))
        phases = len(Reduce.counts(spare, split))
        shapes.append(pltpu.SemaphoreType.DMA((phases + 1,)))
        shapes.append(pltpu.SemaphoreType.DMA((phases + 1,)))
        return shapes

    @staticmethod
    def counts(spare, split):
        counts = [1, 3, 3] if split else [7, 3]
        return counts + ([spare - 1] if spare > 1 else [])

    def run(self, src, out, between=None):
        place, split = self.place, self.split
        send_sem, recv_sem = self.refs[-2:]
        width = src.shape[1]
        piece = width // 2
        if split:
            phases = [[place.sibling()], place.nears(), place.fars()]
            mine = pl.ds(pl.multiple_of(place.core * piece, 128), piece)
            other = pl.ds(pl.multiple_of((1 - place.core) * piece, 128), piece)
        else:
            phases = [[place.sibling()] + place.nears() + place.cross_nears(), place.fars()]
        if place.spare > 1:
            phases.append(place.rests())
        held = src
        for p, devices in enumerate(phases):
            slots, total = self.refs[2 * p], self.refs[2 * p + 1]
            crossing = split and p == 0
            sent = src.at[:, other] if crossing else held
            for k, device in enumerate(devices):
                send(sent, slots.at[k], send_sem.at[p], recv_sem.at[p], device)
            if between is not None:
                between(p)
            await_bytes(slots, recv_sem.at[p])
            value = (src[:, mine] if crossing else held[...]).astype(F32)
            for k in range(len(devices)):
                value = value + slots[k].astype(F32)
            last = p == len(phases) - 1 and not split
            if last:
                out[...] = value
            else:
                total[...] = value.astype(total.dtype)
            held = total
        if split:
            send(held, out.at[:, mine], send_sem.at[len(phases)], recv_sem.at[len(phases)], place.sibling())
            out[:, mine] = held[...]
            await_bytes(out.at[:, other], recv_sem.at[len(phases)])
        for p in range(len(phases)):
            await_bytes(self.refs[2 * p], send_sem.at[p])
        if split:
            await_bytes(held, send_sem.at[len(phases)])


class Piece:
    def __init__(self, layer, band=0, bands=1, strip=0, strips=1, halved=True, direct=False):
        self.layer, self.halved, self.direct = layer, halved, direct
        self.band, self.bands, self.strip, self.strips = band, bands, strip, strips

    def sizes(self, shape):
        return shape[-2] // self.bands, shape[-1] // (2 if self.halved else 1) // self.strips

    def window(self, place, shape):
        count, width = self.sizes(shape)
        rows = pl.ds(self.band * count, count)
        if not self.halved:
            return rows, pl.ds(0, width), None
        half, skip = shape[-1] // 2, self.strip * width
        cols = pl.ds(pl.multiple_of(place.core * half + skip, 128), width)
        others = pl.ds(pl.multiple_of((1 - place.core) * half + skip, 128), width)
        return rows, cols, others


class Gather:
    PHASES = 5

    def __init__(self, place, whole, piece, send_sem, recv_sem):
        self.place, self.whole, self.piece = place, whole, piece
        self.halved, self.direct = piece.halved, piece.direct
        self.send_sem, self.recv_sem = send_sem, recv_sem
        self.rows, self.cols, self.others = piece.window(place, whole.shape)

    def part(self, far, near):
        return self.whole.at[far, near, self.rows, self.cols]

    def start(self):
        place = self.place
        for device in place.fars():
            block = self.part(place.far, place.near)
            send(block, block, self.send_sem.at[0], self.recv_sem.at[0], device)

    def near(self):
        place = self.place
        await_bytes(self.part(pl.ds(0, 3), 0), self.recv_sem.at[0])
        block = self.part(pl.ds(0, 4), place.near)
        partners = [place.first, place.second] + ([place.both] if self.direct else [])
        for phase, partner in enumerate(partners, 1):
            send(
                block,
                block,
                self.send_sem.at[phase],
                self.recv_sem.at[phase],
                place.device(near=partner),
            )

    def forward(self):
        place = self.place
        block = self.part(pl.ds(0, 4), place.first)
        await_bytes(block, self.recv_sem.at[1])
        if self.direct:
            return
        send(
            block, block, self.send_sem.at[3], self.recv_sem.at[3], place.device(near=place.second)
        )

    def cross(self):
        place = self.place
        await_bytes(self.part(pl.ds(0, 4), place.second), self.recv_sem.at[2])
        await_bytes(self.part(pl.ds(0, 4), place.both), self.recv_sem.at[3])
        if self.halved:
            block = self.part(pl.ds(0, 4), pl.ds(0, 4))
            send(block, block, self.send_sem.at[4], self.recv_sem.at[4], place.sibling())

    def finish(self):
        if self.halved:
            await_bytes(
                self.whole.at[pl.ds(0, 4), pl.ds(0, 4), self.rows, self.others], self.recv_sem.at[4]
            )

    def settle(self):
        await_bytes(self.part(pl.ds(0, 3), 0), self.send_sem.at[0])
        for phase in (1, 2, 3):
            await_bytes(self.part(pl.ds(0, 4), 0), self.send_sem.at[phase])
        if self.halved:
            await_bytes(self.part(pl.ds(0, 4), pl.ds(0, 4)), self.send_sem.at[4])


class Scatter:
    PHASES = 5

    def __init__(self, place, whole, piece, landing, done, send_sem, recv_sem):
        self.place, self.whole, self.landing, self.done = place, whole, landing, done
        self.direct = piece.direct
        self.send_sem, self.recv_sem = send_sem, recv_sem
        self.rows, self.cols, self.others = piece.window(place, whole.shape)
        self.half = piece.sizes(whole.shape)[1]
        self.base = place.core * (whole.shape[3] // 2) + piece.strip * self.half

    @staticmethod
    def scratch(rows, half):
        return [
            pltpu.VMEM((4, 4, rows, half), BF16),
            pltpu.VMEM((2, 4, rows, half), BF16),
            pltpu.VMEM((4, rows, half), BF16),
            pltpu.VMEM((3, rows, half), BF16),
        ]

    def stretch(self):
        rows = self.landing[2].shape[1]
        width = 512 if rows < 64 else 256 if rows < 128 else 128
        return min(width, self.half)

    def add(self, near, block):
        width = self.stretch()
        whole, base, rows = self.whole, self.base, self.rows

        @pl.loop(0, self.half // width)
        def _(b):
            here = pl.ds(pl.multiple_of(base + b * width, 128), width)
            there = pl.ds(pl.multiple_of(b * width, 128), width)
            whole[:, near, rows, here] = whole[:, near, rows, here] + block[:, :, there]

    def start(self):
        send(
            self.whole.at[pl.ds(0, 4), pl.ds(0, 4), self.rows, self.others],
            self.landing[0],
            self.send_sem.at[0],
            self.recv_sem.at[0],
            self.place.sibling(),
        )

    def second(self):
        place = self.place
        await_bytes(self.landing[0], self.recv_sem.at[0])
        width = self.stretch()
        whole, base, rows, block = self.whole, self.base, self.rows, self.landing[0]
        strips = self.half // width

        @pl.loop(0, 4 * strips)
        def _(i):
            near, b = lax.div(i, strips), lax.rem(i, strips)
            here = pl.ds(pl.multiple_of(base + b * width, 128), width)
            there = pl.ds(pl.multiple_of(b * width, 128), width)
            whole[:, near, rows, here] = whole[:, near, rows, here] + block[:, near, :, there]

        if self.direct:
            landings = (self.landing[1].at[0], self.landing[1].at[1], self.landing[2])
            for k, near in enumerate((place.second, place.both, place.first)):
                send(
                    whole.at[pl.ds(0, 4), near, self.rows, self.cols],
                    landings[k],
                    self.send_sem.at[max(k, 1)],
                    self.recv_sem.at[max(k, 1)],
                    place.device(near=near),
                )
            return
        for k, near in enumerate((place.second, place.both)):
            send(
                whole.at[pl.ds(0, 4), near, self.rows, self.cols],
                self.landing[1].at[k],
                self.send_sem.at[1],
                self.recv_sem.at[1],
                place.device(near=place.second),
            )

    def first(self):
        place = self.place
        await_bytes(self.landing[1], self.recv_sem.at[1])
        if self.direct:
            self.add(place.near, self.landing[1].at[1])
            self.add(place.near, self.landing[1].at[0])
            return
        self.add(place.first, self.landing[1].at[1])
        send(
            self.whole.at[pl.ds(0, 4), place.first, self.rows, self.cols],
            self.landing[2],
            self.send_sem.at[2],
            self.recv_sem.at[2],
            place.device(near=place.first),
        )
        self.add(place.near, self.landing[1].at[0])

    def fars(self):
        place = self.place
        await_bytes(self.landing[2], self.recv_sem.at[2])
        self.add(place.near, self.landing[2])
        for k in range(1, 4):
            far = lax.rem(place.far + k, 4)
            send(
                self.whole.at[far, place.near, self.rows, self.cols],
                self.landing[3].at[k - 1],
                self.send_sem.at[3],
                self.recv_sem.at[3],
                place.device(far=far),
            )

    def cross(self):
        place = self.place
        await_bytes(self.landing[3], self.recv_sem.at[3])
        blocks = self.half // 128
        whole, base, rows, block, done = self.whole, self.base, self.rows, self.landing[3], self.done

        @pl.loop(0, blocks)
        def _(b):
            here = pl.ds(pl.multiple_of(base + b * 128, 128), 128)
            there = pl.ds(pl.multiple_of(b * 128, 128), 128)
            total = whole[place.far, place.near, rows, here].astype(F32)
            for k in range(3):
                total = total + block[k, :, there].astype(F32)
            done[rows, here] = total.astype(BF16)

        half = done.at[self.rows, self.cols]
        send(half, half, self.send_sem.at[4], self.recv_sem.at[4], place.sibling())

    def finish(self):
        await_bytes(self.done.at[self.rows, self.others], self.recv_sem.at[4])

    def settle(self):
        await_bytes(self.landing[0], self.send_sem.at[0])
        await_bytes(self.landing[1], self.send_sem.at[1])
        await_bytes(self.landing[2], self.send_sem.at[2])
        await_bytes(self.landing[3], self.send_sem.at[3])
        await_bytes(self.done.at[self.rows, self.cols], self.send_sem.at[4])
EPS = 1e-05
KERNEL_ID = 1
NARROW, SPATIAL, WIDEN, SHRINK, STRIDE, EXPAND, BYPASS = range(7)
TABLE = 7
LAST = 5
NN = (((1,), (0,)), ((), ()))
NT = (((1,), (1,)), ((), ()))
TN = (((0,), (0,)), ((), ()))


def mul(a, b, dims):
    return lax.dot_general(a, b, dims, preferred_element_type=F32)


def lanes(i, width=128):
    return pl.ds(pl.multiple_of(i * width, width), width)


def normal_parts(value):
    bell = jnp.exp(-0.5 * value * value) * 0.3989422804014327
    step = 1.0 / (1.0 + 0.2316419 * jnp.abs(value))
    series = 1.330274429 * step - 1.821255978
    series = series * step + 1.781477937
    series = series * step - 0.356563782
    series = series * step + 0.319381530
    tail = bell * (series * step)
    cdf = jnp.where(value >= 0.0, 1.0 - tail, tail)
    return cdf, value * bell


class Image:
    def __init__(self, index, group, side, at, half_at):
        self.index, self.group, self.side = index, group, side
        self.half_side = (side - 1) // 2 + 1
        self.at, self.count = at, (side + 1) * 16
        self.half_at, self.half_count = half_at, -(-(self.half_side + 1) * 8 // 16) * 16

    def rows(self, half):
        return pl.ds(self.half_at, self.half_count) if half else pl.ds(self.at, self.count)

    def inside(self, half):
        count = self.half_count if half else self.count
        side = self.half_side if half else self.side
        bits = 3 if half else 4
        place = lax.broadcasted_iota(jnp.int32, (count, 128), 0)
        return jnp.logical_and(
            lax.shift_right_logical(place, bits) < side, lax.bitwise_and(place, (1 << bits) - 1) < side
        )


def images_of(counts, sides):
    images, at, half_at = [], 0, 0
    for group in range(2):
        for _ in range(counts[group]):
            image = Image(len(images), group, sides[group], at, half_at)
            images.append(image)
            at += image.count
            half_at += image.half_count
    return images, at, half_at


def widths_of(c_in, mid1, mid2, c_out):
    return [mid1, mid1, c_in, mid2, mid2, c_out, c_out]


class Layer:
    def __init__(self, width, half, at):
        self.width, self.half, self.at = width, half, at


def rows_piece(whole, start, count, cols):
    rows, pieces = whole.shape[2], []
    while count:
        shard, skip = divmod(start, rows)
        taken = min(rows - skip, count)
        pieces.append(whole[shard // 4, shard % 4, skip : skip + taken, cols])
        start, count = start + taken, count - taken
    return pieces[0] if len(pieces) == 1 else jnp.concatenate(pieces, axis=0)


def store_piece(whole, start, value):
    rows, done = whole.shape[2], 0
    while done < value.shape[0]:
        shard, skip = divmod(start + done, rows)
        taken = min(rows - skip, value.shape[0] - done)
        whole[shard // 4, shard % 4, skip : skip + taken, :] = value[done : done + taken]
        done += taken


def table_places(shares):
    places, at = [], 0
    for share in shares:
        if at % 128 + share > 128:
            at = -(-at // 128) * 128
        places.append(at)
        at += share
    return places


def step_kernel(spare, images, widths, refs):
    place = Place(spare)
    full_rows, half_rows = refs.x.shape[0], refs.cot.shape[0]
    hot, cnt = refs.hot_v, refs.cnt
    whole = refs.whole
    c_in, mid1, mid2, c_out = widths
    loads = []

    def load(src, dst):
        copy = pltpu.make_async_copy(src, dst, refs.load_sem.at[len(loads)])
        copy.start()
        loads.append(copy)
        return copy

    gathers = [
        Gather(place, whole[piece.layer], piece, refs.gather_send.at[k], refs.gather_recv.at[k])
        for k, piece in enumerate(PIECES)
    ]
    shard_loads = [
        load(
            refs.shards[item.piece.layer].at[item.rows, item.cols], item.part(place.far, place.near)
        )
        for item in gathers
    ]
    load_hot = load(refs.hot, hot)
    load_x = load(refs.x, refs.x_v)
    load_cot = load(refs.cot, refs.cot_v)
    scatters = [
        Scatter(
            place,
            whole[piece.layer],
            piece,
            refs.landing[k],
            refs.done[piece.layer],
            refs.scatter_send.at[k],
            refs.scatter_recv.at[k],
        )
        for k, piece in enumerate(PIECES[:-1])
    ]

    def pieces_of(items, layer):
        return [item for item, piece in zip(items, PIECES) if piece.layer == layer]

    def arrive(layer):
        for item in pieces_of(gathers, layer):
            item.finish()

    def let_go(layer):
        for item in pieces_of(gathers, layer):
            item.settle()

    def send_off(layer):
        for item in pieces_of(scatters, layer):
            item.start()

    def begin(k):
        shard_loads[k].wait()
        gathers[k].start()

    points = []

    def point():
        now = len(points)
        points.append(now)
        for step, *items in PLAN.get(now, ()):
            for k in items:
                if step is BEGIN:
                    begin(k)
                else:
                    step(gathers[k] if step in GATHER_STEPS else scatters[k])

    greet([place.sibling()] + place.nears() + place.cross_nears() + place.fars() + place.rests())

    layers, lane = [], 0
    for k, width in enumerate(widths_of(*widths)):
        layers.append(Layer(width, k in (STRIDE, EXPAND, BYPASS), lane))
        lane += width
        layers[k].normed, layers[k].slope = refs.normed[k], refs.slope[k]
        layers[k].affine, layers[k].scale = refs.affine[k], refs.scale[k]

    def reduce(way, k, during=None):
        def between(p):
            if p < 2:
                point()
                if during is not None:
                    during(p)

        given, total = refs.given[way][k], refs.total[way][k]
        run = Reduce(place, k == LAST, list(refs.slots[way][k]) + list(refs.sums_sem[way][k])).run
        if way == 0:
            run(given, total, between)
        else:
            half = given.shape[1] // 2
            packed, summed = refs.packed[k], refs.summed[k]
            packed[...] = jnp.concatenate([given[:, 0:half], given[:, half:]], axis=0).astype(BF16)
            run(packed, summed, between)
            value = summed[...].astype(F32)
            total[:, 0:half], total[:, half:] = value[0:8], value[8:16]
        point()

    def hot_row(image, view):
        row = 2 * image.index + view
        return hot[row : row + 1, :]

    def of_image(image, by_view):
        row = 2 * image.group
        return hot_row(image, 0) * by_view[row : row + 1] + hot_row(image, 1) * by_view[row + 1 : row + 2]

    def by_view(values):
        out = []
        for group in range(2):
            for view in range(2):
                total = None
                for image in images:
                    if image.group == group:
                        term = values[image.index] * hot_row(image, view)
                        total = term if total is None else total + term
                out.append(total)
        return out

    def put_sums(st, cols, firsts, seconds):
        st[:, cols] = jnp.concatenate(by_view(firsts) + by_view(seconds), axis=0)

    def column_sum(value):
        return jnp.sum(value, axis=0, keepdims=True)

    def field_sums(layer, st, field, i, masked, cols=None):
        firsts, seconds = [], []
        for image in images:
            z = field(image, i)
            if masked:
                z = jnp.where(image.inside(layer.half), z, 0.0)
            firsts.append(column_sum(z))
            seconds.append(column_sum(z * z))
        put_sums(st, lanes(i) if cols is None else cols, firsts, seconds)

    def statistics(total):
        counted = cnt[0:4, :]
        mean = total[0:4] / counted
        return mean, lax.rsqrt(total[4:8] / counted - mean * mean + EPS)

    def normed_of(layer, image, cols, z, mean, scale):
        stretch = of_image(image, scale)
        layer.scale[image.index : image.index + 1, cols] = stretch
        return (z - of_image(image, mean)) * stretch

    def forward(name, field, sink, extra=None):
        layer = layers[name]

        @pl.loop(0, layer.width // 128)
        def _(i):
            cols = lanes(i)
            mean, scale = statistics(refs.total[0][name][:, cols])
            gain, bias = layer.affine[0:1, cols], layer.affine[1:2, cols]
            for image in images:
                rows, inside = image.rows(layer.half), image.inside(layer.half)
                normed = normed_of(layer, image, cols, field(image, i), mean, scale)
                value = normed * gain + bias
                if extra is not None:
                    value = value + extra[rows, cols].astype(F32)
                cdf, rest = normal_parts(value)
                layer.normed[rows, cols] = normed.astype(BF16)
                layer.slope[rows, cols] = jnp.where(inside, cdf + rest, 0.0).astype(BF16)
                sink(image, i, jnp.where(inside, value * cdf, 0.0))

    def gradient_sums(name, grad, st):
        layer = layers[name]

        @pl.loop(0, layer.width // 128)
        def _(i):
            cols = lanes(i)
            firsts, seconds = [], []
            for image in images:
                g = grad(image, i)
                firsts.append(column_sum(g))
                seconds.append(column_sum(g * layer.normed[image.rows(layer.half), cols].astype(F32)))
            put_sums(st, cols, firsts, seconds)

    def gradient(name, grad, sums, sink=None):
        layer = layers[name]

        @pl.loop(0, layer.width // 128)
        def _(i):
            cols = lanes(i)
            first, second = sums(i)
            here = pl.ds(pl.multiple_of(layer.at + i * 128, 128), 128)
            refs.daffine_v[0:1, here] = column_sum(second)
            refs.daffine_v[1:2, here] = column_sum(first)
            first, second = first / cnt[0:4, :], second / cnt[0:4, :]
            gain = layer.affine[0:1, cols]
            for image in images:
                rows = image.rows(layer.half)
                stretch = gain * layer.scale[image.index : image.index + 1, cols]
                normed = layer.normed[rows, cols].astype(F32)
                value = stretch * (grad(image, i) - of_image(image, first) - normed * of_image(image, second))
                value = jnp.where(image.inside(layer.half), value, 0.0)
                if sink is None:
                    layer.normed[rows, cols] = value.astype(BF16)
                else:
                    sink(image, i, value)

    def totals_of(name):
        def sums(i):
            total = refs.total[1][name][:, lanes(i)]
            return total[0:4], total[4:8]

        return sums

    def shifted(target, image, i, value):
        width = target.shape[1] // 3
        rows = pl.ds(16 + image.at, image.count)
        for q in range(3):
            moved = value if q == 1 else pltpu.roll(value, 1 if q == 0 else image.count - 1, 0)
            target[rows, pl.ds(pl.multiple_of(q * width + i * 128, 128), 128)] = moved.astype(BF16)

    def clear_ends(target, top, from_row):
        target[0:top, :] = jnp.zeros((top, target.shape[1]), target.dtype)
        target[from_row:, :] = jnp.zeros((target.shape[0] - from_row, target.shape[1]), target.dtype)

    def strided(start):
        return pl.ds(start, 8, stride=2)

    F, G, K, S = refs.F, refs.G, refs.K, refs.S
    x_v, taps1, act_spatial, upper = refs.x_v, refs.taps1, refs.act_spatial, refs.upper
    taps2, act_stride, even, grad3 = refs.taps2, refs.act_stride, refs.even, refs.grad3
    clear_ends(taps1, 16, 16 + full_rows)
    clear_ends(grad3, 16, 16 + full_rows)
    blocks2 = mid2 // 128
    K[:, 0:32, :] = jnp.zeros((blocks2, 32, 128), F32)
    K[:, 32 + full_rows :, :] = jnp.zeros((blocks2, K.shape[1] - 32 - full_rows, 128), F32)
    EVEN, SPREAD = refs.EVEN, refs.SPREAD
    SPREAD[...] = jnp.zeros(SPREAD.shape, F32)

    places = table_places([layer.width // 16 for layer in layers])

    def spread_affine(k):
        table, layer = whole[TABLE], layers[k]
        share = layer.width // 16
        row, skip = divmod(places[k], 128)
        to = lax.broadcasted_iota(jnp.int32, (16, 128), 1)
        owner = lax.broadcasted_iota(jnp.int32, (16, 128), 0)
        pick_from = lax.broadcasted_iota(jnp.int32, (128, 128), 0)
        pick_to = lax.broadcasted_iota(jnp.int32, (128, 128), 1)
        chosen = (pick_from == skip + lax.rem(pick_to, share)).astype(BF16)
        for kind in range(2):
            held = [
                table[g // 4, g % 4, :, :].astype(F32)[row + 4 * kind : row + 4 * kind + 1] for g in range(16)
            ]
            spread = mul(jnp.concatenate(held, axis=0).astype(BF16), chosen, NN)
            for b in range(layer.width // 128):
                mine = jnp.where(lax.div(b * 128 + to, share) == owner, spread, 0.0)
                layer.affine[kind : kind + 1, b * 128 : (b + 1) * 128] = column_sum(mine)

    load_hot.wait()
    load_x.wait()
    point()

    def plain(buffer):
        return lambda image, i: buffer[image.rows(False), lanes(i)]

    def plain_half(buffer):
        return lambda image, i: buffer[image.rows(True), lanes(i)]

    def halves(buffer, base):
        blocks = F.shape[1] // 128

        def field(image, i):
            band = base + lax.div(i, blocks)
            rows = pl.ds(pl.multiple_of(band * half_rows + image.half_at, 8), image.half_count)
            return buffer[rows, lanes(lax.rem(i, blocks))]

        return field

    arrive(NARROW)
    F[0:full_rows, 0:mid1] = mul(x_v[...], whole[NARROW][...].reshape(c_in, mid1), NN)

    @pl.loop(0, mid1 // 128)
    def _(i):
        field_sums(layers[NARROW], refs.given[0][NARROW], plain(F), i, False)

    pixels = []
    for image in images:
        pixels.append(jnp.full((1, 128), float(image.side * image.side), F32))
    empty = [jnp.zeros((1, 128), F32) for _ in images]
    put_sums(refs.given[0][NARROW], pl.ds(mid1, 128), pixels, empty)

    def during(p):
        if p == 0:
            for k in (NARROW, SPATIAL, WIDEN):
                spread_affine(k)

    point()
    reduce(0, NARROW, during)
    cnt[...] = refs.total[0][NARROW][:, mid1 : mid1 + 128]
    forward(NARROW, plain(F), functools.partial(shifted, taps1))

    point()
    arrive(SPATIAL)
    for r in range(3):
        kernel = rows_piece(whole[SPATIAL], r * 3 * mid1, 3 * mid1, slice(None))
        term = mul(taps1[16 * r : 16 * r + full_rows, :], kernel, NN)
        F[0:full_rows, 0:mid1] = term if r == 0 else F[0:full_rows, 0:mid1] + term

    @pl.loop(0, mid1 // 128)
    def _(i):
        field_sums(layers[SPATIAL], refs.given[0][SPATIAL], plain(F), i, True)

    def during(p):
        if p == 0:
            for k in (SHRINK, STRIDE):
                spread_affine(k)

    point()
    reduce(0, SPATIAL, during)

    def to_spatial(image, i, value):
        act_spatial[image.rows(False), lanes(i)] = value.astype(BF16)

    forward(SPATIAL, plain(F), to_spatial)

    point()
    arrive(WIDEN)

    @pl.loop(0, c_in // 256)
    def _(j):
        cols = lanes(j, 256)
        F[0:full_rows, cols] = mul(act_spatial[...], whole[WIDEN][:, :, :, cols].reshape(mid1, 256), NN)
        for k in range(2):
            field_sums(layers[WIDEN], refs.given[0][WIDEN], plain(F), 2 * j + k, False)

    def during(p):
        if p == 0:
            for k in (EXPAND, BYPASS):
                spread_affine(k)

    point()
    reduce(0, WIDEN, during)

    def to_upper(image, i, value):
        upper[image.rows(False), lanes(i)] = value.astype(BF16)
        rows = image.rows(False)
        EVEN[rows, :] = value
        for pair in range(image.half_count // 16):
            both = [EVEN[strided(image.at + 32 * min(2 * pair + k, image.half_side - 1)), :] for k in range(2)]
            here = pl.ds(image.half_at + 16 * pair, 16)
            even[here, lanes(i)] = jnp.concatenate(both, axis=0).astype(BF16)

    forward(WIDEN, plain(F), to_upper, x_v)

    point()
    arrive(SHRINK)

    @pl.loop(0, mid2 // 256)
    def _(j):
        cols = lanes(j, 256)
        F[0:full_rows, cols] = mul(upper[...], whole[SHRINK][:, :, :, cols].reshape(c_in, 256), NN)
        for k in range(2):
            field_sums(layers[SHRINK], refs.given[0][SHRINK], plain(F), 2 * j + k, False)

    point()
    reduce(0, SHRINK)

    def to_shrink(image, i, value):
        K[i, pl.ds(32 + image.at, image.count), :] = value

    forward(SHRINK, plain(F), to_shrink)

    for image in images:

        @pl.loop(0, image.half_count // 16)
        def _(pair):
            rows = pl.ds(pl.multiple_of(image.half_at + 16 * pair, 16), 16)
            for r in range(3):
                for q in range(3):
                    start = 32 + image.at + 64 * pair + (r - 1) * 16 + q - 1
                    for b in range(blocks2):
                        both = [K[b, strided(start + 32 * k), :] for k in range(2)]
                        at = (3 * r + q) * mid2 + b * 128
                        taps2[rows, at : at + 128] = jnp.concatenate(both, axis=0).astype(BF16)

    point()
    arrive(STRIDE)

    @pl.loop(0, mid2 // 256)
    def _(j):
        cols = lanes(j, 256)
        depth = 9 * mid2 // 4
        for far in range(4):
            kernel = whole[STRIDE][far, :, :, cols].reshape(depth, 256)
            term = mul(taps2[:, far * depth : (far + 1) * depth], kernel, NN)
            G[:, cols] = term if far == 0 else G[:, cols] + term
        for k in range(2):
            field_sums(layers[STRIDE], refs.given[0][STRIDE], plain_half(G), 2 * j + k, True)

    def bypass_field():
        arrive(BYPASS)

        @pl.loop(0, c_out // 256)
        def _(j):
            value = mul(even[...], whole[BYPASS][:, :, :, lanes(j, 256)].reshape(c_in, 256), NN)
            blocks = c_in // 256
            rows = pl.ds(pl.multiple_of((2 + lax.div(j, blocks)) * half_rows, 8), half_rows)
            F[rows, lanes(lax.rem(j, blocks), 256)] = value
            for k in range(2):
                i = 2 * j + k
                cols = pl.ds(pl.multiple_of(c_out + i * 128, 128), 128)
                field_sums(layers[BYPASS], refs.given[0][LAST], halves(F, 2), i, True, cols)

    point()
    reduce(0, STRIDE)

    def to_stride(image, i, value):
        act_stride[image.rows(True), lanes(i)] = value.astype(BF16)

    forward(STRIDE, plain_half(G), to_stride)

    point()
    arrive(EXPAND)

    @pl.loop(0, c_out // 256)
    def _(j):
        value = mul(act_stride[...], whole[EXPAND][:, :, :, lanes(j, 256)].reshape(mid2, 256), NN)
        blocks = c_in // 256
        rows = pl.ds(pl.multiple_of(lax.div(j, blocks) * half_rows, 8), half_rows)
        F[rows, lanes(lax.rem(j, blocks), 256)] = value
        for k in range(2):
            field_sums(layers[EXPAND], refs.given[0][LAST], halves(F, 0), 2 * j + k, True)

    point()
    bypass_field()
    reduce(0, LAST)
    load_cot.wait()
    expand_z, bypass_z = halves(F, 0), halves(F, 2)

    @pl.loop(0, c_out // 128)
    def _(i):
        cols = lanes(i)
        upper_cols = pl.ds(pl.multiple_of(c_out + i * 128, 128), 128)
        stats_e = statistics(refs.total[0][LAST][:, cols])
        stats_b = statistics(refs.total[0][LAST][:, upper_cols])
        el, bl = layers[EXPAND], layers[BYPASS]
        firsts, seconds, thirds = [], [], []
        for image in images:
            rows, inside = image.rows(True), image.inside(True)
            normed_e = normed_of(el, image, cols, expand_z(image, i), *stats_e)
            normed_b = normed_of(bl, image, cols, bypass_z(image, i), *stats_b)
            value = normed_e * el.affine[0:1, cols] + el.affine[1:2, cols]
            value = value + (normed_b * bl.affine[0:1, cols] + bl.affine[1:2, cols])
            cdf, rest = normal_parts(value)
            el.normed[rows, cols] = normed_e.astype(BF16)
            bl.normed[rows, cols] = normed_b.astype(BF16)
            grad = jnp.where(inside, refs.cot_v[rows, cols].astype(F32) * (cdf + rest), 0.0)
            refs.cot_v[rows, cols] = (value * cdf).astype(BF16)
            blocks = F.shape[1] // 128
            band = lax.div(i, blocks)
            here = pl.ds(pl.multiple_of(band * half_rows + image.half_at, 8), image.half_count)
            F[here, lanes(lax.rem(i, blocks))] = grad
            firsts.append(column_sum(grad))
            seconds.append(column_sum(grad * normed_e))
            thirds.append(column_sum(grad * normed_b))
        put_sums(refs.given[1][LAST], cols, firsts, seconds)
        put_sums(refs.given[1][LAST], upper_cols, thirds, thirds)

    store_out = pltpu.make_async_copy(refs.cot_v, refs.out, refs.store_sem.at[0])
    store_out.start()
    point()
    reduce(1, LAST)

    def sums_expand(i):
        total = refs.total[1][LAST][:, lanes(i)]
        return total[0:4], total[4:8]

    def sums_bypass(i):
        first = refs.total[1][LAST][:, lanes(i)]
        second = refs.total[1][LAST][:, pl.ds(pl.multiple_of(c_out + i * 128, 128), 128)]
        return first[0:4], second[0:4]

    gradient(EXPAND, halves(F, 0), sums_expand)
    gradient(BYPASS, halves(F, 0), sums_bypass)
    expand_grad, bypass_grad = layers[EXPAND].normed, layers[BYPASS].normed

    point()
    @pl.loop(0, mid2 // 256)
    def _(j):
        kernel = whole[EXPAND][pl.ds(2 * j, 2)].reshape(256, c_out)
        cols = lanes(j, 256)
        G[:, cols] = mul(expand_grad[...], kernel, NT) * layers[STRIDE].slope[:, cols].astype(F32)

    gradient_sums(STRIDE, plain_half(G), refs.given[1][STRIDE])

    def filter_grad(name, left, right, fars):
        let_go(name)
        target = whole[name]
        shard, columns = target.shape[2], target.shape[3]
        depth = fars * 4 * shard
        width = min(columns, 512 if depth <= 512 else 256)

        @pl.loop(0, (4 // fars) * (columns // width))
        def _(i):
            j, b = lax.div(i, columns // width), lax.rem(i, columns // width)
            value = mul(left[:, lanes(j, depth)], right[:, lanes(b, width)], TN)
            target[pl.ds(j * fars, fars), :, :, lanes(b, width)] = value.astype(BF16).reshape(fars, 4, shard, width)

    def during(p):
        if p == 0:
            filter_grad(EXPAND, act_stride, expand_grad, 2)
            send_off(EXPAND)
        if p == 1:

            @pl.loop(0, 4)
            def _(j):
                kernel = whole[BYPASS][j].reshape(256, c_out)
                S[pl.ds(pl.multiple_of(j * half_rows, 8), half_rows), :] = mul(bypass_grad[...], kernel, NT)

            filter_grad(BYPASS, even, bypass_grad, 1)
            send_off(BYPASS)

    point()
    reduce(1, STRIDE, during)
    gradient(STRIDE, plain_half(G), totals_of(STRIDE))
    stride_grad = layers[STRIDE].normed

    point()
    K[...] = jnp.zeros(K.shape, F32)
    for r in range(3):
        for q in range(3):
            kernel = rows_piece(whole[STRIDE], (3 * r + q) * mid2, mid2, slice(None))
            F[0:half_rows, 0:mid2] = mul(stride_grad[...], kernel, NT)
            for image in images:

                @pl.loop(0, image.half_side)
                def _(i):
                    there = strided(32 + image.at + 32 * i + (r - 1) * 16 + q - 1)
                    here = pl.ds(pl.multiple_of(image.half_at + 8 * i, 8), 8)
                    for b in range(blocks2):
                        K[b, there, :] = K[b, there, :] + F[here, b * 128 : (b + 1) * 128]

    @pl.loop(0, mid2 // 128)
    def _(i):
        cols = lanes(i)
        firsts, seconds = [], []
        for image in images:
            rows = pl.ds(32 + image.at, image.count)
            g = K[i, rows, :] * layers[SHRINK].slope[image.rows(False), cols].astype(F32)
            K[i, rows, :] = g
            firsts.append(column_sum(g))
            seconds.append(column_sum(g * layers[SHRINK].normed[image.rows(False), cols].astype(F32)))
        put_sums(refs.given[1][SHRINK], cols, firsts, seconds)

    def during(p):
        if p == 0:
            filter_grad(STRIDE, taps2, stride_grad, 1)
            send_off(STRIDE)

    point()
    reduce(1, SHRINK, during)
    gradient(SHRINK, lambda image, i: K[i, pl.ds(32 + image.at, image.count), :], totals_of(SHRINK))
    shrink_grad = layers[SHRINK].normed

    point()

    @pl.loop(0, 4)
    def _(j):
        cols = lanes(j, 256)
        kernel = whole[SHRINK][j].reshape(256, mid2)
        F[0:full_rows, cols] = mul(shrink_grad[...], kernel, NT)

    @pl.loop(0, c_in // 128)
    def _(i):
        cols = lanes(i)
        firsts, seconds = [], []
        for image in images:
            rows = image.rows(False)
            for j in range(image.half_side):
                start = pl.multiple_of(lax.div(i, 2) * half_rows + image.half_at + 8 * j, 8)
                SPREAD[strided(image.at + 32 * j), :] = S[pl.ds(start, 8), lanes(lax.rem(i, 2))]
            g = (F[rows, cols] + SPREAD[rows, :]) * layers[WIDEN].slope[rows, cols].astype(F32)
            F[rows, cols] = g
            firsts.append(column_sum(g))
            seconds.append(column_sum(g * layers[WIDEN].normed[rows, cols].astype(F32)))
        put_sums(refs.given[1][WIDEN], cols, firsts, seconds)

    def during(p):
        if p == 0:
            filter_grad(SHRINK, upper, shrink_grad, 1)
            send_off(SHRINK)

    point()
    reduce(1, WIDEN, during)
    gradient(WIDEN, plain(F), totals_of(WIDEN))
    widen_grad = layers[WIDEN].normed

    point()
    S[0:full_rows, :] = mul(widen_grad[...], whole[WIDEN][...].reshape(mid1, c_in), NT) * layers[SPATIAL].slope[...].astype(F32)
    gradient_sums(SPATIAL, plain(S), refs.given[1][SPATIAL])

    def during(p):
        if p == 0:
            filter_grad(WIDEN, act_spatial, widen_grad, 4)
            send_off(WIDEN)

    point()
    reduce(1, SPATIAL, during)
    gradient(SPATIAL, plain(S), totals_of(SPATIAL), functools.partial(shifted, grad3))

    point()
    for r in range(3):
        kernel = jnp.concatenate(
            [rows_piece(whole[SPATIAL], (3 * r + 2 - q) * mid1, mid1, slice(None)) for q in range(3)], axis=1
        )
        term = mul(grad3[16 * (2 - r) : 16 * (2 - r) + full_rows, :], kernel, NT)
        S[0:full_rows, :] = term if r == 0 else S[0:full_rows, :] + term
    S[0:full_rows, :] = S[0:full_rows, :] * layers[NARROW].slope[...].astype(F32)
    gradient_sums(NARROW, plain(S), refs.given[1][NARROW])

    def during(p):
        if p == 0:
            let_go(SPATIAL)
        if p < 2:
            for r in ((0, 1), (2,))[p]:
                value = mul(taps1[16 * r : 16 * r + full_rows, :], grad3[16 : 16 + full_rows, mid1 : 2 * mid1], TN)
                store_piece(whole[SPATIAL], r * 3 * mid1, value.astype(BF16))
        if p == 1:
            send_off(SPATIAL)

    point()
    reduce(1, NARROW, during)
    gradient(NARROW, plain(S), totals_of(NARROW))
    narrow_grad = layers[NARROW].normed

    point()
    for j in range(4):
        upper[0:256, j * mid1 : (j + 1) * mid1] = whole[NARROW][j].reshape(256, mid1)
    filter_grad(NARROW, x_v, narrow_grad, 1)
    send_off(NARROW)
    point()
    for j in range(4):
        cols = slice(j * 256, (j + 1) * 256)
        kernel = upper[0:256, j * mid1 : (j + 1) * mid1]
        x_v[:, cols] = (F[0:full_rows, cols] + mul(narrow_grad[...], kernel, NT)).astype(BF16)
        point()
    stores = [
        pltpu.make_async_copy(x_v, refs.dinput, refs.store_sem.at[1]),
        pltpu.make_async_copy(refs.daffine_v, refs.daffine, refs.store_sem.at[2]),
    ]
    for store in stores:
        store.start()
    point()
    for k in (EXPAND, BYPASS, STRIDE, SHRINK, WIDEN, SPATIAL, NARROW):
        for item in pieces_of(scatters, k):
            item.finish()
        stores.append(pltpu.make_async_copy(refs.done[k], refs.dfilter[k], refs.store_sem.at[3 + k]))
        stores[-1].start()
    for item in scatters:
        item.settle()
    let_go(TABLE)
    store_out.wait()
    for store in stores:
        store.wait()


PIECES = [
    Piece(NARROW, direct=True),
    Piece(SPATIAL),
    Piece(WIDEN),
    Piece(SHRINK),
    Piece(STRIDE, 0, 2, 0, 2),
    Piece(STRIDE, 0, 2, 1, 2),
    Piece(STRIDE, 1, 2, 0, 2),
    Piece(STRIDE, 1, 2, 1, 2),
    Piece(EXPAND, 0, 1, 0, 2),
    Piece(EXPAND, 0, 1, 1, 2),
    Piece(BYPASS, 0, 1, 0, 4),
    Piece(BYPASS, 0, 1, 1, 4),
    Piece(BYPASS, 0, 1, 2, 4),
    Piece(BYPASS, 0, 1, 3, 4),
    Piece(TABLE, halved=False, direct=True),
]
N, S, W, K, T0, T1, T2, T3, E0, E1, B0, B1, B2, B3, TAB = range(15)
BEGIN = object()
GATHER_STEPS = (Gather.near, Gather.forward, Gather.cross)
NEAR, FORWARD, CROSS = GATHER_STEPS
R2, R3, R4, R5 = Scatter.second, Scatter.first, Scatter.fars, Scatter.cross
PLAN = {
    0: [
        (BEGIN, TAB, N),
        (NEAR, TAB, N),
        (BEGIN, S, W, K, T0),
        (FORWARD, TAB, N),
        (CROSS, N),
        (NEAR, S),
    ],
    1: [(CROSS, TAB)],
    2: [(FORWARD, S), (NEAR, W, K), (BEGIN, T1)],
    3: [(CROSS, S)],
    4: [(FORWARD, W), (NEAR, T0), (BEGIN, T2)],
    6: [(CROSS, W)],
    7: [(FORWARD, K, T0), (NEAR, T1), (BEGIN, T3)],
    8: [(CROSS, K, T0)],
    9: [(NEAR, T2), (BEGIN, E0)],
    12: [(FORWARD, T1, T2), (NEAR, T3), (BEGIN, E1)],
    13: [(CROSS, T1, T2)],
    14: [(NEAR, E0), (FORWARD, T3), (BEGIN, B0)],
    17: [(FORWARD, E0), (NEAR, E1), (BEGIN, B1)],
    18: [(CROSS, T3, E0)],
    19: [(NEAR, B0), (BEGIN, B2)],
    21: [(BEGIN, B3)],
    22: [(FORWARD, E1, B0), (NEAR, B1)],
    23: [(CROSS, E1, B0)],
    24: [(NEAR, B2), (FORWARD, B1)],
    25: [(NEAR, B3), (FORWARD, B2), (CROSS, B1)],
    26: [(FORWARD, B3), (CROSS, B2, B3)],
    37: [(R2, E0, E1)],
    38: [(R2, B0)],
    39: [(R3, E0, E1), (R2, B1)],
    40: [(R4, E0)],
    41: [(R3, B0, B1), (R2, B2), (R4, E1)],
    42: [(R5, E0)],
    43: [(R2, B3), (R3, B2), (R4, B0)],
    44: [(R2, T0), (R4, B1)],
    46: [(R3, B3, T0), (R2, T1), (R4, B2)],
    47: [(R5, E1, B0)],
    48: [(R2, T2), (R4, B3)],
    49: [(R3, T1), (R4, T0)],
    51: [(R3, T2), (R2, T3), (R4, T1)],
    52: [(R5, B1, B2)],
    53: [(R2, K), (R3, T3), (R4, T2)],
    54: [(R2, W)],
    55: [(R3, W)],
    56: [(R3, K), (R4, T3)],
    57: [(R5, B3, T0, T1)],
    58: [(R2, S), (R4, K, W)],
    59: [(R3, S)],
    60: [(R4, S), (R5, T2, T3)],
    61: [(R5, K, W)],
    62: [(R2, N)],
    63: [(R5, S)],
    65: [(R3, N), (R4, N), (R5, N)],
}


def spare_groups(spare):
    count = lax.axis_size("dp")
    return [list(range(at, at + spare)) for at in range(0, count, spare)]


def padded(field, rows, across):
    side = field.shape[1]
    field = jnp.pad(field, ((0, 0), (0, rows - side), (0, across - side), (0, 0)))
    return field.reshape(-1, field.shape[3])


def local(
    input_big,
    input_small,
    views_big,
    views_small,
    cotan_big,
    cotan_small,
    *params,
):
    filters, affines = params[0::2], params[1::2]
    devices = lax.axis_size("dp")
    spare = devices // 16
    inputs, cotans = (input_big, input_small), (cotan_big, cotan_small)
    counts = [item.shape[0] for item in inputs]
    images, full_rows, half_rows = images_of(counts, [item.shape[1] for item in inputs])
    c_in, c_out = input_big.shape[3], cotan_big.shape[3]
    mid1, mid2 = filters[NARROW].shape[1], filters[SHRINK].shape[1]
    widths = (c_in, mid1, mid2, c_out)
    wide = widths_of(*widths)
    by_group = [next(image for image in images if image.group == g) for g in range(2)]
    x = jnp.concatenate([padded(inputs[g], by_group[g].count // 16, 16) for g in range(2)])
    cot = jnp.concatenate([padded(cotans[g], by_group[g].half_count // 8, 8) for g in range(2)])
    view = jnp.concatenate([views_big, views_small])
    hot = (view[:, None] == jnp.arange(2, dtype=jnp.int32)[None, :]).astype(F32)
    hot = jnp.broadcast_to(hot.reshape(-1, 1), (2 * len(images), 128))

    parts = [item.T for item in affines]
    shards = list(filters)
    if spare > 1:
        groups = spare_groups(spare)
        shards = [lax.all_gather(item, "dp", axis_index_groups=groups, tiled=True) for item in filters]
        gathered = lax.all_gather(jnp.concatenate(parts, axis=1), "dp", axis_index_groups=groups)
        parts, at = [], 0
        for item in affines:
            share = item.shape[0]
            parts.append(jnp.moveaxis(gathered[:, :, at : at + share], 0, 1).reshape(2, -1))
            at += share
    places = table_places([item.shape[1] for item in parts]) + [512]
    parts = [
        jnp.pad(item, ((0, 0), (0, places[k + 1] - places[k] - item.shape[1]))) for k, item in enumerate(parts)
    ]
    shards.append(jnp.pad(jnp.concatenate(parts, axis=1).reshape(8, 128), ((0, 8), (0, 0))))
    shapes = [item.shape for item in shards]
    lane_total = sum(wide)

    def field(*shape):
        return pltpu.VMEM(shape, F32)

    def rounded(*shape):
        return pltpu.VMEM(shape, BF16)

    def layer_rows(k):
        return half_rows if k in (STRIDE, EXPAND, BYPASS) else full_rows

    rounds = [wide[:5] + [2 * c_out], wide[:5] + [2 * c_out]]
    rounds[0][NARROW] += 128
    sums = [
        [Reduce.scratch(8, width, spare, k == LAST) for k, width in enumerate(rounds[0])],
        [Reduce.scratch(16, width // 2, spare, k == LAST, BF16) for k, width in enumerate(rounds[1])],
    ]
    operands = dict(x=x, cot=cot, hot=hot, shards=shards)
    results = dict(
        out=jax.ShapeDtypeStruct((half_rows, c_out), BF16),
        dinput=jax.ShapeDtypeStruct((full_rows, c_in), BF16),
        daffine=jax.ShapeDtypeStruct((8, lane_total), F32),
        dfilter=[jax.ShapeDtypeStruct(shape, BF16) for shape in shapes[:7]],
    )
    scratch = dict(
        whole=[rounded(4, 4, *shape) for shape in shapes],
        done=[rounded(*shape) for shape in shapes[:7]],
        landing=[Scatter.scratch(*piece.sizes(shapes[piece.layer])) for piece in PIECES[:-1]],
        normed=[rounded(layer_rows(k), wide[k]) for k in range(7)],
        slope=[None if k in (EXPAND, BYPASS) else rounded(layer_rows(k), wide[k]) for k in range(7)],
        affine=[field(8, width) for width in wide],
        scale=[field(-(-len(images) // 8) * 8, width) for width in wide],
        x_v=rounded(full_rows, c_in),
        cot_v=rounded(half_rows, c_out),
        hot_v=field(*hot.shape),
        cnt=field(8, 128),
        daffine_v=field(8, lane_total),
        F=field(max(full_rows, 4 * half_rows), c_in),
        G=field(half_rows, mid2),
        S=field(max(full_rows, 4 * half_rows), mid1),
        K=field(mid2 // 128, full_rows + 64, 128),
        EVEN=field(full_rows, 128),
        SPREAD=field(full_rows, 128),
        taps1=rounded(full_rows + 32, 3 * mid1),
        grad3=rounded(full_rows + 32, 3 * mid1),
        act_spatial=rounded(full_rows, mid1),
        upper=rounded(full_rows, c_in),
        taps2=rounded(half_rows, 9 * mid2),
        act_stride=rounded(half_rows, mid2),
        even=rounded(half_rows, c_in),
        given=[[field(8, width) for width in way] for way in rounds],
        total=[[field(8, width) for width in way] for way in rounds],
        slots=[[item[:-2] for item in way] for way in sums],
        packed=[rounded(16, width // 2) for width in rounds[1]],
        summed=[(rounded if k == LAST else field)(16, width // 2) for k, width in enumerate(rounds[1])],
        sums_sem=[[item[-2:] for item in way] for way in sums],
        load_sem=pltpu.SemaphoreType.DMA((len(PIECES) + 3,)),
        store_sem=pltpu.SemaphoreType.DMA((16,)),
        gather_send=pltpu.SemaphoreType.DMA((len(PIECES), Gather.PHASES)),
        gather_recv=pltpu.SemaphoreType.DMA((len(PIECES), Gather.PHASES)),
        scatter_send=pltpu.SemaphoreType.DMA((len(PIECES), Scatter.PHASES)),
        scatter_recv=pltpu.SemaphoreType.DMA((len(PIECES), Scatter.PHASES)),
    )
    flat_in, in_tree = jax.tree.flatten(operands)
    flat_out, out_tree = jax.tree.flatten(results)
    flat_scratch, scratch_tree = jax.tree.flatten(scratch)

    def kernel(*flat):
        here = len(flat_in) + len(flat_out)
        refs = jax.tree.unflatten(in_tree, flat[: len(flat_in)])
        refs |= jax.tree.unflatten(out_tree, flat[len(flat_in) : here])
        refs |= jax.tree.unflatten(scratch_tree, flat[here:])
        step_kernel(spare, images, widths, types.SimpleNamespace(**refs))

    flat_out = pl.pallas_call(
        kernel,
        out_shape=flat_out,
        in_specs=[pl.BlockSpec(memory_space=pl.ANY)] * len(flat_in),
        out_specs=[pl.BlockSpec(memory_space=pl.ANY)] * len(flat_out),
        scratch_shapes=flat_scratch,
        compiler_params=pltpu.CompilerParams(
            collective_id=KERNEL_ID, has_side_effects=True, vmem_limit_bytes=VMEM_BYTES
        ),
    )(*flat_in)
    done = types.SimpleNamespace(**jax.tree.unflatten(out_tree, flat_out))

    shares = [width // devices for width in wide]
    views = [(group, half) for half in (True, False) for group in range(2)]

    def image_shape(group, half):
        side = by_group[group].half_side if half else by_group[group].side
        return counts[group], side, side, c_out if half else c_in

    def finish(*flat):
        given, images_out, grads_out, affine_out = flat[:10], flat[10:14], flat[14:21], flat[21:28]
        held, sem = flat[28:38], flat[38]
        copies = [pltpu.make_async_copy(given[k], held[k], sem.at[k]) for k in range(10)]
        for copy in copies:
            copy.start()
        for copy in copies:
            copy.wait()
        out, dinput, daffine, *grads = held
        for ref, (group, half) in zip(images_out, views):
            image, rows = by_group[group], out if half else dinput
            start = image.half_at if half else image.at
            count = image.half_count if half else image.count
            across = 8 if half else 16
            number, side, _, width = ref.shape
            for n in range(number):
                for row in range(side):
                    here = start + n * count + row * across
                    ref[n, row] = rows[here : here + across, :][:side]
        for ref, grad in zip(grads_out, grads):
            ref[...] = grad[...].astype(F32)
        me, at = lax.axis_index("dp"), 0
        for k, ref in enumerate(affine_out):
            first = me * shares[k]
            block, shift = lax.div(first, 128), lax.rem(first, 128)
            rows = daffine[:, pl.ds(pl.multiple_of(at + block * 128, 128), 128)]
            ref[...] = pltpu.roll(rows, lax.rem(128 - shift, 128), 1)[0:2, 0 : shares[k]]
            at += wide[k]

    finals = [done.out, done.dinput, done.daffine, *done.dfilter]
    outs = pl.pallas_call(
        finish,
        out_shape=[jax.ShapeDtypeStruct(image_shape(*view), BF16) for view in views]
        + [jax.ShapeDtypeStruct(shape, F32) for shape in shapes[:7]]
        + [jax.ShapeDtypeStruct((2, share), F32) for share in shares],
        in_specs=[pl.BlockSpec(memory_space=pl.ANY)] * 10,
        out_specs=[pl.BlockSpec(memory_space=pltpu.VMEM)] * 18,
        scratch_shapes=[pltpu.VMEM(item.shape, item.dtype) for item in finals] + [pltpu.SemaphoreType.DMA((10,))],
        compiler_params=pltpu.CompilerParams(vmem_limit_bytes=VMEM_BYTES),
    )(*finals)
    results = list(outs[:4])
    for grad, affine in zip(outs[4:11], outs[11:]):
        if spare > 1:
            grad = lax.psum_scatter(grad, "dp", axis_index_groups=spare_groups(spare), tiled=True)
        results += [grad, affine.T]
    return tuple(results)


VMEM_BYTES = 65400 * 1024


def solution(mesh):
    images = P(("dp", "outer"), None, None, None)
    rows = P("dp", None)
    return jax.shard_map(
        local,
        mesh=mesh,
        in_specs=(images, images, P(("dp", "outer")), P(("dp", "outer")), images, images) + (rows,) * 14,
        out_specs=(images,) * 4 + (rows,) * 14,
        check_vma=False,
    )
```

```python
import functools
import types

import jax
import jax.numpy as jnp
from jax import lax
from jax.experimental import pallas as pl
from jax.experimental.pallas import tpu as pltpu
from jax.sharding import PartitionSpec as P

MESH = pl.DeviceIdType.MESH
F32 = jnp.float32
BF16 = jnp.bfloat16


class Place:
    def __init__(self, spare):
        self.spare = spare
        dp = lax.axis_index("dp")
        self.core = lax.axis_index("outer")
        self.rest = lax.rem(dp, spare)
        group = lax.div(dp, spare)
        self.far = lax.div(group, 4)
        self.near = lax.rem(group, 4)
        high, low = lax.div(self.near, 2), lax.rem(self.near, 2)
        self.first = 2 * lax.rem(high + 1 - self.core, 2) + lax.rem(low + self.core, 2)
        self.second = 2 * lax.rem(high + self.core, 2) + lax.rem(low + 1 - self.core, 2)
        self.both = 3 - self.near

    def device(self, far=None, near=None, core=None, rest=None):
        far = self.far if far is None else far
        near = self.near if near is None else near
        core = self.core if core is None else core
        rest = self.rest if rest is None else rest
        return ((far * 4 + near) * self.spare + rest, core)

    def fars(self):
        return [self.device(far=lax.rem(self.far + k, 4)) for k in range(1, 4)]

    def nears(self):
        return [self.device(near=lax.rem(self.near + k, 4)) for k in range(1, 4)]

    def cross_nears(self):
        return [
            self.device(near=lax.rem(self.near + k, 4), core=1 - self.core) for k in range(1, 4)
        ]

    def sibling(self):
        return self.device(core=1 - self.core)

    def rests(self):
        return [
            self.device(rest=lax.rem(self.rest + k, self.spare)) for k in range(1, self.spare)
        ]


def greet(devices):
    barrier = pltpu.get_barrier_semaphore()
    for device in devices:
        pl.semaphore_signal(barrier, inc=1, device_id=device, device_id_type=MESH)
    pl.semaphore_wait(barrier, len(devices))


def send(src, dst, send_sem, recv_sem, device):
    pltpu.make_async_remote_copy(
        src_ref=src,
        dst_ref=dst,
        send_sem=send_sem,
        recv_sem=recv_sem,
        device_id=device,
        device_id_type=MESH,
    ).start()


def await_bytes(like, sem):
    pltpu.make_async_copy(like, like, sem).wait()


class Reduce:
    def __init__(self, place, split, refs):
        self.place = place
        self.split = split
        self.refs = refs

    @staticmethod
    def scratch(rows, width, spare, split, kind=F32):
        piece = width // 2 if split else width
        shapes = []
        for count in Reduce.counts(spare, split):
            shapes.append(pltpu.VMEM((count, rows, piece), kind))
            shapes.append(pltpu.VMEM((rows, piece), kind))
        phases = len(Reduce.counts(spare, split))
        shapes.append(pltpu.SemaphoreType.DMA((phases + 1,)))
        shapes.append(pltpu.SemaphoreType.DMA((phases + 1,)))
        return shapes

    @staticmethod
    def counts(spare, split):
        counts = [1, 3, 3] if split else [7, 3]
        return counts + ([spare - 1] if spare > 1 else [])

    def run(self, src, out, between=None):
        place, split = self.place, self.split
        send_sem, recv_sem = self.refs[-2:]
        width = src.shape[1]
        piece = width // 2
        if split:
            phases = [[place.sibling()], place.nears(), place.fars()]
            mine = pl.ds(pl.multiple_of(place.core * piece, 128), piece)
            other = pl.ds(pl.multiple_of((1 - place.core) * piece, 128), piece)
        else:
            phases = [[place.sibling()] + place.nears() + place.cross_nears(), place.fars()]
        if place.spare > 1:
            phases.append(place.rests())
        held = src
        for p, devices in enumerate(phases):
            slots, total = self.refs[2 * p], self.refs[2 * p + 1]
            crossing = split and p == 0
            sent = src.at[:, other] if crossing else held
            for k, device in enumerate(devices):
                send(sent, slots.at[k], send_sem.at[p], recv_sem.at[p], device)
            if between is not None:
                between(p)
            await_bytes(slots, recv_sem.at[p])
            value = (src[:, mine] if crossing else held[...]).astype(F32)
            for k in range(len(devices)):
                value = value + slots[k].astype(F32)
            last = p == len(phases) - 1 and not split
            if last:
                out[...] = value
            else:
                total[...] = value.astype(total.dtype)
            held = total
        if split:
            send(held, out.at[:, mine], send_sem.at[len(phases)], recv_sem.at[len(phases)], place.sibling())
            out[:, mine] = held[...]
            await_bytes(out.at[:, other], recv_sem.at[len(phases)])
        for p in range(len(phases)):
            await_bytes(self.refs[2 * p], send_sem.at[p])
        if split:
            await_bytes(held, send_sem.at[len(phases)])


class Piece:
    def __init__(self, layer, band=0, bands=1, strip=0, strips=1, halved=True, direct=False):
        self.layer, self.halved, self.direct = layer, halved, direct
        self.band, self.bands, self.strip, self.strips = band, bands, strip, strips

    def sizes(self, shape):
        return shape[-2] // self.bands, shape[-1] // (2 if self.halved else 1) // self.strips

    def window(self, place, shape):
        count, width = self.sizes(shape)
        rows = pl.ds(self.band * count, count)
        if not self.halved:
            return rows, pl.ds(0, width), None
        half, skip = shape[-1] // 2, self.strip * width
        cols = pl.ds(pl.multiple_of(place.core * half + skip, 128), width)
        others = pl.ds(pl.multiple_of((1 - place.core) * half + skip, 128), width)
        return rows, cols, others


class Gather:
    PHASES = 5

    def __init__(self, place, whole, piece, send_sem, recv_sem):
        self.place, self.whole, self.piece = place, whole, piece
        self.halved, self.direct = piece.halved, piece.direct
        self.send_sem, self.recv_sem = send_sem, recv_sem
        self.rows, self.cols, self.others = piece.window(place, whole.shape)

    def part(self, far, near):
        return self.whole.at[far, near, self.rows, self.cols]

    def start(self):
        place = self.place
        for device in place.fars():
            block = self.part(place.far, place.near)
            send(block, block, self.send_sem.at[0], self.recv_sem.at[0], device)

    def near(self):
        place = self.place
        await_bytes(self.part(pl.ds(0, 3), 0), self.recv_sem.at[0])
        block = self.part(pl.ds(0, 4), place.near)
        partners = [place.first, place.second] + ([place.both] if self.direct else [])
        for phase, partner in enumerate(partners, 1):
            send(
                block,
                block,
                self.send_sem.at[phase],
                self.recv_sem.at[phase],
                place.device(near=partner),
            )

    def forward(self):
        place = self.place
        block = self.part(pl.ds(0, 4), place.first)
        await_bytes(block, self.recv_sem.at[1])
        if self.direct:
            return
        send(
            block, block, self.send_sem.at[3], self.recv_sem.at[3], place.device(near=place.second)
        )

    def cross(self):
        place = self.place
        await_bytes(self.part(pl.ds(0, 4), place.second), self.recv_sem.at[2])
        await_bytes(self.part(pl.ds(0, 4), place.both), self.recv_sem.at[3])
        if self.halved:
            block = self.part(pl.ds(0, 4), pl.ds(0, 4))
            send(block, block, self.send_sem.at[4], self.recv_sem.at[4], place.sibling())

    def finish(self):
        if self.halved:
            await_bytes(
                self.whole.at[pl.ds(0, 4), pl.ds(0, 4), self.rows, self.others], self.recv_sem.at[4]
            )

    def settle(self):
        await_bytes(self.part(pl.ds(0, 3), 0), self.send_sem.at[0])
        for phase in (1, 2, 3):
            await_bytes(self.part(pl.ds(0, 4), 0), self.send_sem.at[phase])
        if self.halved:
            await_bytes(self.part(pl.ds(0, 4), pl.ds(0, 4)), self.send_sem.at[4])


class Scatter:
    PHASES = 5

    def __init__(self, place, whole, piece, landing, done, send_sem, recv_sem):
        self.place, self.whole, self.landing, self.done = place, whole, landing, done
        self.direct = piece.direct
        self.send_sem, self.recv_sem = send_sem, recv_sem
        self.rows, self.cols, self.others = piece.window(place, whole.shape)
        self.half = piece.sizes(whole.shape)[1]
        self.base = place.core * (whole.shape[3] // 2) + piece.strip * self.half

    @staticmethod
    def scratch(rows, half):
        return [
            pltpu.VMEM((4, 4, rows, half), BF16),
            pltpu.VMEM((2, 4, rows, half), BF16),
            pltpu.VMEM((4, rows, half), BF16),
            pltpu.VMEM((3, rows, half), BF16),
        ]

    def stretch(self):
        rows = self.landing[2].shape[1]
        width = 512 if rows < 64 else 256 if rows < 128 else 128
        return min(width, self.half)

    def add(self, near, block):
        width = self.stretch()
        whole, base, rows = self.whole, self.base, self.rows

        @pl.loop(0, self.half // width)
        def _(b):
            here = pl.ds(pl.multiple_of(base + b * width, 128), width)
            there = pl.ds(pl.multiple_of(b * width, 128), width)
            whole[:, near, rows, here] = whole[:, near, rows, here] + block[:, :, there]

    def start(self):
        send(
            self.whole.at[pl.ds(0, 4), pl.ds(0, 4), self.rows, self.others],
            self.landing[0],
            self.send_sem.at[0],
            self.recv_sem.at[0],
            self.place.sibling(),
        )

    def second(self):
        place = self.place
        await_bytes(self.landing[0], self.recv_sem.at[0])
        width = self.stretch()
        whole, base, rows, block = self.whole, self.base, self.rows, self.landing[0]
        strips = self.half // width

        @pl.loop(0, 4 * strips)
        def _(i):
            near, b = lax.div(i, strips), lax.rem(i, strips)
            here = pl.ds(pl.multiple_of(base + b * width, 128), width)
            there = pl.ds(pl.multiple_of(b * width, 128), width)
            whole[:, near, rows, here] = whole[:, near, rows, here] + block[:, near, :, there]

        if self.direct:
            landings = (self.landing[1].at[0], self.landing[1].at[1], self.landing[2])
            for k, near in enumerate((place.second, place.both, place.first)):
                send(
                    whole.at[pl.ds(0, 4), near, self.rows, self.cols],
                    landings[k],
                    self.send_sem.at[max(k, 1)],
                    self.recv_sem.at[max(k, 1)],
                    place.device(near=near),
                )
            return
        for k, near in enumerate((place.second, place.both)):
            send(
                whole.at[pl.ds(0, 4), near, self.rows, self.cols],
                self.landing[1].at[k],
                self.send_sem.at[1],
                self.recv_sem.at[1],
                place.device(near=place.second),
            )

    def first(self):
        place = self.place
        await_bytes(self.landing[1], self.recv_sem.at[1])
        if self.direct:
            self.add(place.near, self.landing[1].at[1])
            self.add(place.near, self.landing[1].at[0])
            return
        self.add(place.first, self.landing[1].at[1])
        send(
            self.whole.at[pl.ds(0, 4), place.first, self.rows, self.cols],
            self.landing[2],
            self.send_sem.at[2],
            self.recv_sem.at[2],
            place.device(near=place.first),
        )
        self.add(place.near, self.landing[1].at[0])

    def fars(self):
        place = self.place
        await_bytes(self.landing[2], self.recv_sem.at[2])
        self.add(place.near, self.landing[2])
        for k in range(1, 4):
            far = lax.rem(place.far + k, 4)
            send(
                self.whole.at[far, place.near, self.rows, self.cols],
                self.landing[3].at[k - 1],
                self.send_sem.at[3],
                self.recv_sem.at[3],
                place.device(far=far),
            )

    def cross(self):
        place = self.place
        await_bytes(self.landing[3], self.recv_sem.at[3])
        blocks = self.half // 128
        whole, base, rows, block, done = self.whole, self.base, self.rows, self.landing[3], self.done

        @pl.loop(0, blocks)
        def _(b):
            here = pl.ds(pl.multiple_of(base + b * 128, 128), 128)
            there = pl.ds(pl.multiple_of(b * 128, 128), 128)
            total = whole[place.far, place.near, rows, here].astype(F32)
            for k in range(3):
                total = total + block[k, :, there].astype(F32)
            done[rows, here] = total.astype(BF16)

        half = done.at[self.rows, self.cols]
        send(half, half, self.send_sem.at[4], self.recv_sem.at[4], place.sibling())

    def finish(self):
        await_bytes(self.done.at[self.rows, self.others], self.recv_sem.at[4])

    def settle(self):
        await_bytes(self.landing[0], self.send_sem.at[0])
        await_bytes(self.landing[1], self.send_sem.at[1])
        await_bytes(self.landing[2], self.send_sem.at[2])
        await_bytes(self.landing[3], self.send_sem.at[3])
        await_bytes(self.done.at[self.rows, self.cols], self.send_sem.at[4])
EPS = 1e-05
KERNEL_ID = 1
NARROW, SPATIAL, WIDEN, SHRINK, STRIDE, EXPAND, BYPASS = range(7)
TABLE = 7
LAST = 5
NN = (((1,), (0,)), ((), ()))
NT = (((1,), (1,)), ((), ()))
TN = (((0,), (0,)), ((), ()))


def mul(a, b, dims):
    return lax.dot_general(a, b, dims, preferred_element_type=F32)


def lanes(i, width=128):
    return pl.ds(pl.multiple_of(i * width, width), width)


def normal_parts(value):
    bell = jnp.exp(-0.5 * value * value) * 0.3989422804014327
    step = 1.0 / (1.0 + 0.2316419 * jnp.abs(value))
    series = 1.330274429 * step - 1.821255978
    series = series * step + 1.781477937
    series = series * step - 0.356563782
    series = series * step + 0.319381530
    tail = bell * (series * step)
    cdf = jnp.where(value >= 0.0, 1.0 - tail, tail)
    return cdf, value * bell


class Image:
    def __init__(self, index, group, side, at, half_at):
        self.index, self.group, self.side = index, group, side
        self.half_side = (side - 1) // 2 + 1
        self.at, self.count = at, (side + 1) * 16
        self.half_at, self.half_count = half_at, -(-(self.half_side + 1) * 8 // 16) * 16

    def rows(self, half):
        return pl.ds(self.half_at, self.half_count) if half else pl.ds(self.at, self.count)

    def inside(self, half):
        count = self.half_count if half else self.count
        side = self.half_side if half else self.side
        bits = 3 if half else 4
        place = lax.broadcasted_iota(jnp.int32, (count, 128), 0)
        return jnp.logical_and(
            lax.shift_right_logical(place, bits) < side, lax.bitwise_and(place, (1 << bits) - 1) < side
        )


def images_of(counts, sides):
    images, at, half_at = [], 0, 0
    for group in range(2):
        for _ in range(counts[group]):
            image = Image(len(images), group, sides[group], at, half_at)
            images.append(image)
            at += image.count
            half_at += image.half_count
    return images, at, half_at


def widths_of(c_in, mid1, mid2, c_out):
    return [mid1, mid1, c_in, mid2, mid2, c_out, c_out]


class Layer:
    def __init__(self, width, half, at):
        self.width, self.half, self.at = width, half, at


def rows_piece(whole, start, count, cols):
    rows, pieces = whole.shape[2], []
    while count:
        shard, skip = divmod(start, rows)
        taken = min(rows - skip, count)
        pieces.append(whole[shard // 4, shard % 4, skip : skip + taken, cols])
        start, count = start + taken, count - taken
    return pieces[0] if len(pieces) == 1 else jnp.concatenate(pieces, axis=0)


def store_piece(whole, start, value):
    rows, done = whole.shape[2], 0
    while done < value.shape[0]:
        shard, skip = divmod(start + done, rows)
        taken = min(rows - skip, value.shape[0] - done)
        whole[shard // 4, shard % 4, skip : skip + taken, :] = value[done : done + taken]
        done += taken


def table_places(shares):
    places, at = [], 0
    for share in shares:
        if at % 128 + share > 128:
            at = -(-at // 128) * 128
        places.append(at)
        at += share
    return places


def step_kernel(spare, images, widths, refs):
    place = Place(spare)
    full_rows, half_rows = refs.x.shape[0], refs.cot.shape[0]
    hot, cnt = refs.hot_v, refs.cnt
    whole = refs.whole
    c_in, mid1, mid2, c_out = widths
    loads = []

    def load(src, dst):
        copy = pltpu.make_async_copy(src, dst, refs.load_sem.at[len(loads)])
        copy.start()
        loads.append(copy)
        return copy

    gathers = [
        Gather(place, whole[piece.layer], piece, refs.gather_send.at[k], refs.gather_recv.at[k])
        for k, piece in enumerate(PIECES)
    ]
    shard_loads = [
        load(
            refs.shards[item.piece.layer].at[item.rows, item.cols], item.part(place.far, place.near)
        )
        for item in gathers
    ]
    load_hot = load(refs.hot, hot)
    load_x = load(refs.x, refs.x_v)
    load_cot = load(refs.cot, refs.cot_v)
    scatters = [
        Scatter(
            place,
            whole[piece.layer],
            piece,
            refs.landing[k],
            refs.done[piece.layer],
            refs.scatter_send.at[k],
            refs.scatter_recv.at[k],
        )
        for k, piece in enumerate(PIECES[:-1])
    ]

    def pieces_of(items, layer):
        return [item for item, piece in zip(items, PIECES) if piece.layer == layer]

    def arrive(layer):
        for item in pieces_of(gathers, layer):
            item.finish()

    def let_go(layer):
        for item in pieces_of(gathers, layer):
            item.settle()

    def send_off(layer):
        for item in pieces_of(scatters, layer):
            item.start()

    def begin(k):
        shard_loads[k].wait()
        gathers[k].start()

    points = []

    def point():
        now = len(points)
        points.append(now)
        for step, *items in PLAN.get(now, ()):
            for k in items:
                if step is BEGIN:
                    begin(k)
                else:
                    step(gathers[k] if step in GATHER_STEPS else scatters[k])

    greet([place.sibling()] + place.nears() + place.cross_nears() + place.fars() + place.rests())

    layers, lane = [], 0
    for k, width in enumerate(widths_of(*widths)):
        layers.append(Layer(width, k in (STRIDE, EXPAND, BYPASS), lane))
        lane += width
        layers[k].normed, layers[k].slope = refs.normed[k], refs.slope[k]
        layers[k].affine, layers[k].scale = refs.affine[k], refs.scale[k]

    def reduce(way, k, during=None):
        def between(p):
            if p < 2:
                point()
                if during is not None:
                    during(p)

        given, total = refs.given[way][k], refs.total[way][k]
        run = Reduce(place, k == LAST, list(refs.slots[way][k]) + list(refs.sums_sem[way][k])).run
        if way == 0:
            run(given, total, between)
        else:
            half = given.shape[1] // 2
            packed, summed = refs.packed[k], refs.summed[k]
            packed[...] = jnp.concatenate([given[:, 0:half], given[:, half:]], axis=0).astype(BF16)
            run(packed, summed, between)
            value = summed[...].astype(F32)
            total[:, 0:half], total[:, half:] = value[0:8], value[8:16]
        point()

    def hot_row(image, view):
        row = 2 * image.index + view
        return hot[row : row + 1, :]

    def of_image(image, by_view):
        row = 2 * image.group
        return hot_row(image, 0) * by_view[row : row + 1] + hot_row(image, 1) * by_view[row + 1 : row + 2]

    def by_view(values):
        out = []
        for group in range(2):
            for view in range(2):
                total = None
                for image in images:
                    if image.group == group:
                        term = values[image.index] * hot_row(image, view)
                        total = term if total is None else total + term
                out.append(total)
        return out

    def put_sums(st, cols, firsts, seconds):
        st[:, cols] = jnp.concatenate(by_view(firsts) + by_view(seconds), axis=0)

    def column_sum(value):
        return jnp.sum(value, axis=0, keepdims=True)

    def field_sums(layer, st, field, i, masked, cols=None):
        firsts, seconds = [], []
        for image in images:
            z = field(image, i)
            if masked:
                z = jnp.where(image.inside(layer.half), z, 0.0)
            firsts.append(column_sum(z))
            seconds.append(column_sum(z * z))
        put_sums(st, lanes(i) if cols is None else cols, firsts, seconds)

    def statistics(total):
        counted = cnt[0:4, :]
        mean = total[0:4] / counted
        return mean, lax.rsqrt(total[4:8] / counted - mean * mean + EPS)

    def normed_of(layer, image, cols, z, mean, scale):
        stretch = of_image(image, scale)
        layer.scale[image.index : image.index + 1, cols] = stretch
        return (z - of_image(image, mean)) * stretch

    def forward(name, field, sink, extra=None):
        layer = layers[name]

        @pl.loop(0, layer.width // 128)
        def _(i):
            cols = lanes(i)
            mean, scale = statistics(refs.total[0][name][:, cols])
            gain, bias = layer.affine[0:1, cols], layer.affine[1:2, cols]
            for image in images:
                rows, inside = image.rows(layer.half), image.inside(layer.half)
                normed = normed_of(layer, image, cols, field(image, i), mean, scale)
                value = normed * gain + bias
                if extra is not None:
                    value = value + extra[rows, cols].astype(F32)
                cdf, rest = normal_parts(value)
                layer.normed[rows, cols] = normed.astype(BF16)
                layer.slope[rows, cols] = jnp.where(inside, cdf + rest, 0.0).astype(BF16)
                sink(image, i, jnp.where(inside, value * cdf, 0.0))

    def gradient_sums(name, grad, st):
        layer = layers[name]

        @pl.loop(0, layer.width // 128)
        def _(i):
            cols = lanes(i)
            firsts, seconds = [], []
            for image in images:
                g = grad(image, i)
                firsts.append(column_sum(g))
                seconds.append(column_sum(g * layer.normed[image.rows(layer.half), cols].astype(F32)))
            put_sums(st, cols, firsts, seconds)

    def gradient(name, grad, sums, sink=None):
        layer = layers[name]

        @pl.loop(0, layer.width // 128)
        def _(i):
            cols = lanes(i)
            first, second = sums(i)
            here = pl.ds(pl.multiple_of(layer.at + i * 128, 128), 128)
            refs.daffine_v[0:1, here] = column_sum(second)
            refs.daffine_v[1:2, here] = column_sum(first)
            first, second = first / cnt[0:4, :], second / cnt[0:4, :]
            gain = layer.affine[0:1, cols]
            for image in images:
                rows = image.rows(layer.half)
                stretch = gain * layer.scale[image.index : image.index + 1, cols]
                normed = layer.normed[rows, cols].astype(F32)
                value = stretch * (grad(image, i) - of_image(image, first) - normed * of_image(image, second))
                value = jnp.where(image.inside(layer.half), value, 0.0)
                if sink is None:
                    layer.normed[rows, cols] = value.astype(BF16)
                else:
                    sink(image, i, value)

    def totals_of(name):
        def sums(i):
            total = refs.total[1][name][:, lanes(i)]
            return total[0:4], total[4:8]

        return sums

    def shifted(target, image, i, value):
        width = target.shape[1] // 3
        rows = pl.ds(16 + image.at, image.count)
        for q in range(3):
            moved = value if q == 1 else pltpu.roll(value, 1 if q == 0 else image.count - 1, 0)
            target[rows, pl.ds(pl.multiple_of(q * width + i * 128, 128), 128)] = moved.astype(BF16)

    def clear_ends(target, top, from_row):
        target[0:top, :] = jnp.zeros((top, target.shape[1]), target.dtype)
        target[from_row:, :] = jnp.zeros((target.shape[0] - from_row, target.shape[1]), target.dtype)

    def strided(start):
        return pl.ds(start, 8, stride=2)

    F, G, K, S = refs.F, refs.G, refs.K, refs.S
    x_v, taps1, act_spatial, upper = refs.x_v, refs.taps1, refs.act_spatial, refs.upper
    taps2, act_stride, even, grad3 = refs.taps2, refs.act_stride, refs.even, refs.grad3
    clear_ends(taps1, 16, 16 + full_rows)
    clear_ends(grad3, 16, 16 + full_rows)
    blocks2 = mid2 // 128
    K[:, 0:32, :] = jnp.zeros((blocks2, 32, 128), F32)
    K[:, 32 + full_rows :, :] = jnp.zeros((blocks2, K.shape[1] - 32 - full_rows, 128), F32)
    EVEN, SPREAD = refs.EVEN, refs.SPREAD
    SPREAD[...] = jnp.zeros(SPREAD.shape, F32)

    places = table_places([layer.width // 16 for layer in layers])

    def spread_affine(k):
        table, layer = whole[TABLE], layers[k]
        share = layer.width // 16
        row, skip = divmod(places[k], 128)
        to = lax.broadcasted_iota(jnp.int32, (16, 128), 1)
        owner = lax.broadcasted_iota(jnp.int32, (16, 128), 0)
        pick_from = lax.broadcasted_iota(jnp.int32, (128, 128), 0)
        pick_to = lax.broadcasted_iota(jnp.int32, (128, 128), 1)
        chosen = (pick_from == skip + lax.rem(pick_to, share)).astype(BF16)
        for kind in range(2):
            held = [
                table[g // 4, g % 4, :, :].astype(F32)[row + 4 * kind : row + 4 * kind + 1] for g in range(16)
            ]
            spread = mul(jnp.concatenate(held, axis=0).astype(BF16), chosen, NN)
            for b in range(layer.width // 128):
                mine = jnp.where(lax.div(b * 128 + to, share) == owner, spread, 0.0)
                layer.affine[kind : kind + 1, b * 128 : (b + 1) * 128] = column_sum(mine)

    load_hot.wait()
    load_x.wait()
    point()

    def plain(buffer):
        return lambda image, i: buffer[image.rows(False), lanes(i)]

    def plain_half(buffer):
        return lambda image, i: buffer[image.rows(True), lanes(i)]

    def halves(buffer, base):
        blocks = F.shape[1] // 128

        def field(image, i):
            band = base + lax.div(i, blocks)
            rows = pl.ds(pl.multiple_of(band * half_rows + image.half_at, 8), image.half_count)
            return buffer[rows, lanes(lax.rem(i, blocks))]

        return field

    arrive(NARROW)
    F[0:full_rows, 0:mid1] = mul(x_v[...], whole[NARROW][...].reshape(c_in, mid1), NN)

    @pl.loop(0, mid1 // 128)
    def _(i):
        field_sums(layers[NARROW], refs.given[0][NARROW], plain(F), i, False)

    pixels = []
    for image in images:
        pixels.append(jnp.full((1, 128), float(image.side * image.side), F32))
    empty = [jnp.zeros((1, 128), F32) for _ in images]
    put_sums(refs.given[0][NARROW], pl.ds(mid1, 128), pixels, empty)

    def during(p):
        if p == 0:
            for k in (NARROW, SPATIAL, WIDEN):
                spread_affine(k)

    point()
    reduce(0, NARROW, during)
    cnt[...] = refs.total[0][NARROW][:, mid1 : mid1 + 128]
    forward(NARROW, plain(F), functools.partial(shifted, taps1))

    point()
    arrive(SPATIAL)
    for r in range(3):
        kernel = rows_piece(whole[SPATIAL], r * 3 * mid1, 3 * mid1, slice(None))
        term = mul(taps1[16 * r : 16 * r + full_rows, :], kernel, NN)
        F[0:full_rows, 0:mid1] = term if r == 0 else F[0:full_rows, 0:mid1] + term

    @pl.loop(0, mid1 // 128)
    def _(i):
        field_sums(layers[SPATIAL], refs.given[0][SPATIAL], plain(F), i, True)

    def during(p):
        if p == 0:
            for k in (SHRINK, STRIDE):
                spread_affine(k)

    point()
    reduce(0, SPATIAL, during)

    def to_spatial(image, i, value):
        act_spatial[image.rows(False), lanes(i)] = value.astype(BF16)

    forward(SPATIAL, plain(F), to_spatial)

    point()
    arrive(WIDEN)

    @pl.loop(0, c_in // 256)
    def _(j):
        cols = lanes(j, 256)
        F[0:full_rows, cols] = mul(act_spatial[...], whole[WIDEN][:, :, :, cols].reshape(mid1, 256), NN)
        for k in range(2):
            field_sums(layers[WIDEN], refs.given[0][WIDEN], plain(F), 2 * j + k, False)

    def during(p):
        if p == 0:
            for k in (EXPAND, BYPASS):
                spread_affine(k)

    point()
    reduce(0, WIDEN, during)

    def to_upper(image, i, value):
        upper[image.rows(False), lanes(i)] = value.astype(BF16)
        rows = image.rows(False)
        EVEN[rows, :] = value
        for pair in range(image.half_count // 16):
            both = [EVEN[strided(image.at + 32 * min(2 * pair + k, image.half_side - 1)), :] for k in range(2)]
            here = pl.ds(image.half_at + 16 * pair, 16)
            even[here, lanes(i)] = jnp.concatenate(both, axis=0).astype(BF16)

    forward(WIDEN, plain(F), to_upper, x_v)

    point()
    arrive(SHRINK)

    @pl.loop(0, mid2 // 256)
    def _(j):
        cols = lanes(j, 256)
        F[0:full_rows, cols] = mul(upper[...], whole[SHRINK][:, :, :, cols].reshape(c_in, 256), NN)
        for k in range(2):
            field_sums(layers[SHRINK], refs.given[0][SHRINK], plain(F), 2 * j + k, False)

    point()
    reduce(0, SHRINK)

    def to_shrink(image, i, value):
        K[i, pl.ds(32 + image.at, image.count), :] = value

    forward(SHRINK, plain(F), to_shrink)

    for image in images:

        @pl.loop(0, image.half_count // 16)
        def _(pair):
            rows = pl.ds(pl.multiple_of(image.half_at + 16 * pair, 16), 16)
            for r in range(3):
                for q in range(3):
                    start = 32 + image.at + 64 * pair + (r - 1) * 16 + q - 1
                    for b in range(blocks2):
                        both = [K[b, strided(start + 32 * k), :] for k in range(2)]
                        at = (3 * r + q) * mid2 + b * 128
                        taps2[rows, at : at + 128] = jnp.concatenate(both, axis=0).astype(BF16)

    point()
    arrive(STRIDE)

    @pl.loop(0, mid2 // 256)
    def _(j):
        cols = lanes(j, 256)
        depth = 9 * mid2 // 4
        for far in range(4):
            kernel = whole[STRIDE][far, :, :, cols].reshape(depth, 256)
            term = mul(taps2[:, far * depth : (far + 1) * depth], kernel, NN)
            G[:, cols] = term if far == 0 else G[:, cols] + term
        for k in range(2):
            field_sums(layers[STRIDE], refs.given[0][STRIDE], plain_half(G), 2 * j + k, True)

    def bypass_field():
        arrive(BYPASS)

        @pl.loop(0, c_out // 256)
        def _(j):
            value = mul(even[...], whole[BYPASS][:, :, :, lanes(j, 256)].reshape(c_in, 256), NN)
            blocks = c_in // 256
            rows = pl.ds(pl.multiple_of((2 + lax.div(j, blocks)) * half_rows, 8), half_rows)
            F[rows, lanes(lax.rem(j, blocks), 256)] = value
            for k in range(2):
                i = 2 * j + k
                cols = pl.ds(pl.multiple_of(c_out + i * 128, 128), 128)
                field_sums(layers[BYPASS], refs.given[0][LAST], halves(F, 2), i, True, cols)

    point()
    reduce(0, STRIDE)

    def to_stride(image, i, value):
        act_stride[image.rows(True), lanes(i)] = value.astype(BF16)

    forward(STRIDE, plain_half(G), to_stride)

    point()
    arrive(EXPAND)

    @pl.loop(0, c_out // 256)
    def _(j):
        value = mul(act_stride[...], whole[EXPAND][:, :, :, lanes(j, 256)].reshape(mid2, 256), NN)
        blocks = c_in // 256
        rows = pl.ds(pl.multiple_of(lax.div(j, blocks) * half_rows, 8), half_rows)
        F[rows, lanes(lax.rem(j, blocks), 256)] = value
        for k in range(2):
            field_sums(layers[EXPAND], refs.given[0][LAST], halves(F, 0), 2 * j + k, True)

    point()
    bypass_field()
    reduce(0, LAST)
    load_cot.wait()
    expand_z, bypass_z = halves(F, 0), halves(F, 2)

    @pl.loop(0, c_out // 128)
    def _(i):
        cols = lanes(i)
        upper_cols = pl.ds(pl.multiple_of(c_out + i * 128, 128), 128)
        stats_e = statistics(refs.total[0][LAST][:, cols])
        stats_b = statistics(refs.total[0][LAST][:, upper_cols])
        el, bl = layers[EXPAND], layers[BYPASS]
        firsts, seconds, thirds = [], [], []
        for image in images:
            rows, inside = image.rows(True), image.inside(True)
            normed_e = normed_of(el, image, cols, expand_z(image, i), *stats_e)
            normed_b = normed_of(bl, image, cols, bypass_z(image, i), *stats_b)
            value = normed_e * el.affine[0:1, cols] + el.affine[1:2, cols]
            value = value + (normed_b * bl.affine[0:1, cols] + bl.affine[1:2, cols])
            cdf, rest = normal_parts(value)
            el.normed[rows, cols] = normed_e.astype(BF16)
            bl.normed[rows, cols] = normed_b.astype(BF16)
            grad = jnp.where(inside, refs.cot_v[rows, cols].astype(F32) * (cdf + rest), 0.0)
            refs.cot_v[rows, cols] = (value * cdf).astype(BF16)
            blocks = F.shape[1] // 128
            band = lax.div(i, blocks)
            here = pl.ds(pl.multiple_of(band * half_rows + image.half_at, 8), image.half_count)
            F[here, lanes(lax.rem(i, blocks))] = grad
            firsts.append(column_sum(grad))
            seconds.append(column_sum(grad * normed_e))
            thirds.append(column_sum(grad * normed_b))
        put_sums(refs.given[1][LAST], cols, firsts, seconds)
        put_sums(refs.given[1][LAST], upper_cols, thirds, thirds)

    store_out = pltpu.make_async_copy(refs.cot_v, refs.out, refs.store_sem.at[0])
    store_out.start()
    point()
    reduce(1, LAST)

    def sums_expand(i):
        total = refs.total[1][LAST][:, lanes(i)]
        return total[0:4], total[4:8]

    def sums_bypass(i):
        first = refs.total[1][LAST][:, lanes(i)]
        second = refs.total[1][LAST][:, pl.ds(pl.multiple_of(c_out + i * 128, 128), 128)]
        return first[0:4], second[0:4]

    gradient(EXPAND, halves(F, 0), sums_expand)
    gradient(BYPASS, halves(F, 0), sums_bypass)
    expand_grad, bypass_grad = layers[EXPAND].normed, layers[BYPASS].normed

    point()
    @pl.loop(0, mid2 // 256)
    def _(j):
        kernel = whole[EXPAND][pl.ds(2 * j, 2)].reshape(256, c_out)
        cols = lanes(j, 256)
        G[:, cols] = mul(expand_grad[...], kernel, NT) * layers[STRIDE].slope[:, cols].astype(F32)

    gradient_sums(STRIDE, plain_half(G), refs.given[1][STRIDE])

    def filter_grad(name, left, right, fars):
        let_go(name)
        target = whole[name]
        shard, columns = target.shape[2], target.shape[3]
        depth = fars * 4 * shard
        width = min(columns, 512 if depth <= 512 else 256)

        @pl.loop(0, (4 // fars) * (columns // width))
        def _(i):
            j, b = lax.div(i, columns // width), lax.rem(i, columns // width)
            value = mul(left[:, lanes(j, depth)], right[:, lanes(b, width)], TN)
            target[pl.ds(j * fars, fars), :, :, lanes(b, width)] = value.astype(BF16).reshape(fars, 4, shard, width)

    def during(p):
        if p == 0:
            filter_grad(EXPAND, act_stride, expand_grad, 2)
            send_off(EXPAND)
        if p == 1:

            @pl.loop(0, 4)
            def _(j):
                kernel = whole[BYPASS][j].reshape(256, c_out)
                S[pl.ds(pl.multiple_of(j * half_rows, 8), half_rows), :] = mul(bypass_grad[...], kernel, NT)

            filter_grad(BYPASS, even, bypass_grad, 1)
            send_off(BYPASS)

    point()
    reduce(1, STRIDE, during)
    gradient(STRIDE, plain_half(G), totals_of(STRIDE))
    stride_grad = layers[STRIDE].normed

    point()
    K[...] = jnp.zeros(K.shape, F32)
    for r in range(3):
        for q in range(3):
            kernel = rows_piece(whole[STRIDE], (3 * r + q) * mid2, mid2, slice(None))
            F[0:half_rows, 0:mid2] = mul(stride_grad[...], kernel, NT)
            for image in images:

                @pl.loop(0, image.half_side)
                def _(i):
                    there = strided(32 + image.at + 32 * i + (r - 1) * 16 + q - 1)
                    here = pl.ds(pl.multiple_of(image.half_at + 8 * i, 8), 8)
                    for b in range(blocks2):
                        K[b, there, :] = K[b, there, :] + F[here, b * 128 : (b + 1) * 128]

    @pl.loop(0, mid2 // 128)
    def _(i):
        cols = lanes(i)
        firsts, seconds = [], []
        for image in images:
            rows = pl.ds(32 + image.at, image.count)
            g = K[i, rows, :] * layers[SHRINK].slope[image.rows(False), cols].astype(F32)
            K[i, rows, :] = g
            firsts.append(column_sum(g))
            seconds.append(column_sum(g * layers[SHRINK].normed[image.rows(False), cols].astype(F32)))
        put_sums(refs.given[1][SHRINK], cols, firsts, seconds)

    def during(p):
        if p == 0:
            filter_grad(STRIDE, taps2, stride_grad, 1)
            send_off(STRIDE)

    point()
    reduce(1, SHRINK, during)
    gradient(SHRINK, lambda image, i: K[i, pl.ds(32 + image.at, image.count), :], totals_of(SHRINK))
    shrink_grad = layers[SHRINK].normed

    point()

    @pl.loop(0, 4)
    def _(j):
        cols = lanes(j, 256)
        kernel = whole[SHRINK][j].reshape(256, mid2)
        F[0:full_rows, cols] = mul(shrink_grad[...], kernel, NT)

    @pl.loop(0, c_in // 128)
    def _(i):
        cols = lanes(i)
        firsts, seconds = [], []
        for image in images:
            rows = image.rows(False)
            for j in range(image.half_side):
                start = pl.multiple_of(lax.div(i, 2) * half_rows + image.half_at + 8 * j, 8)
                SPREAD[strided(image.at + 32 * j), :] = S[pl.ds(start, 8), lanes(lax.rem(i, 2))]
            g = (F[rows, cols] + SPREAD[rows, :]) * layers[WIDEN].slope[rows, cols].astype(F32)
            F[rows, cols] = g
            firsts.append(column_sum(g))
            seconds.append(column_sum(g * layers[WIDEN].normed[rows, cols].astype(F32)))
        put_sums(refs.given[1][WIDEN], cols, firsts, seconds)

    def during(p):
        if p == 0:
            filter_grad(SHRINK, upper, shrink_grad, 1)
            send_off(SHRINK)

    point()
    reduce(1, WIDEN, during)
    gradient(WIDEN, plain(F), totals_of(WIDEN))
    widen_grad = layers[WIDEN].normed

    point()
    S[0:full_rows, :] = mul(widen_grad[...], whole[WIDEN][...].reshape(mid1, c_in), NT) * layers[SPATIAL].slope[...].astype(F32)
    gradient_sums(SPATIAL, plain(S), refs.given[1][SPATIAL])

    def during(p):
        if p == 0:
            filter_grad(WIDEN, act_spatial, widen_grad, 4)
            send_off(WIDEN)

    point()
    reduce(1, SPATIAL, during)
    gradient(SPATIAL, plain(S), totals_of(SPATIAL), functools.partial(shifted, grad3))

    point()
    for r in range(3):
        kernel = jnp.concatenate(
            [rows_piece(whole[SPATIAL], (3 * r + 2 - q) * mid1, mid1, slice(None)) for q in range(3)], axis=1
        )
        term = mul(grad3[16 * (2 - r) : 16 * (2 - r) + full_rows, :], kernel, NT)
        S[0:full_rows, :] = term if r == 0 else S[0:full_rows, :] + term
    S[0:full_rows, :] = S[0:full_rows, :] * layers[NARROW].slope[...].astype(F32)
    gradient_sums(NARROW, plain(S), refs.given[1][NARROW])

    def during(p):
        if p == 0:
            let_go(SPATIAL)
        if p < 2:
            for r in ((0, 1), (2,))[p]:
                value = mul(taps1[16 * r : 16 * r + full_rows, :], grad3[16 : 16 + full_rows, mid1 : 2 * mid1], TN)
                store_piece(whole[SPATIAL], r * 3 * mid1, value.astype(BF16))
        if p == 1:
            send_off(SPATIAL)

    point()
    reduce(1, NARROW, during)
    gradient(NARROW, plain(S), totals_of(NARROW))
    narrow_grad = layers[NARROW].normed

    point()
    for j in range(4):
        upper[0:256, j * mid1 : (j + 1) * mid1] = whole[NARROW][j].reshape(256, mid1)
    filter_grad(NARROW, x_v, narrow_grad, 1)
    send_off(NARROW)
    point()
    for j in range(4):
        cols = slice(j * 256, (j + 1) * 256)
        kernel = upper[0:256, j * mid1 : (j + 1) * mid1]
        x_v[:, cols] = (F[0:full_rows, cols] + mul(narrow_grad[...], kernel, NT)).astype(BF16)
        point()
    stores = [
        pltpu.make_async_copy(x_v, refs.dinput, refs.store_sem.at[1]),
        pltpu.make_async_copy(refs.daffine_v, refs.daffine, refs.store_sem.at[2]),
    ]
    for store in stores:
        store.start()
    point()
    for k in (EXPAND, BYPASS, STRIDE, SHRINK, WIDEN, SPATIAL, NARROW):
        for item in pieces_of(scatters, k):
            item.finish()
        stores.append(pltpu.make_async_copy(refs.done[k], refs.dfilter[k], refs.store_sem.at[3 + k]))
        stores[-1].start()
    for item in scatters:
        item.settle()
    let_go(TABLE)
    store_out.wait()
    for store in stores:
        store.wait()


PIECES = [
    Piece(NARROW, direct=True),
    Piece(SPATIAL),
    Piece(WIDEN),
    Piece(SHRINK),
    Piece(STRIDE, 0, 2, 0, 2),
    Piece(STRIDE, 0, 2, 1, 2),
    Piece(STRIDE, 1, 2, 0, 2),
    Piece(STRIDE, 1, 2, 1, 2),
    Piece(EXPAND, 0, 1, 0, 2),
    Piece(EXPAND, 0, 1, 1, 2),
    Piece(BYPASS, 0, 1, 0, 4),
    Piece(BYPASS, 0, 1, 1, 4),
    Piece(BYPASS, 0, 1, 2, 4),
    Piece(BYPASS, 0, 1, 3, 4),
    Piece(TABLE, halved=False, direct=True),
]
N, S, W, K, T0, T1, T2, T3, E0, E1, B0, B1, B2, B3, TAB = range(15)
BEGIN = object()
GATHER_STEPS = (Gather.near, Gather.forward, Gather.cross)
NEAR, FORWARD, CROSS = GATHER_STEPS
R2, R3, R4, R5 = Scatter.second, Scatter.first, Scatter.fars, Scatter.cross
PLAN = {
    0: [(BEGIN, TAB, N, S, W, K, T0), (NEAR, TAB, N, S), (FORWARD, TAB, N), (CROSS, N)],
    1: [(CROSS, TAB), (BEGIN, T1)],
    2: [(FORWARD, S), (NEAR, W, K), (BEGIN, T2)],
    3: [(CROSS, S)],
    4: [(FORWARD, W), (NEAR, T0), (BEGIN, T3)],
    6: [(CROSS, W)],
    7: [(FORWARD, K, T0), (NEAR, T1), (BEGIN, E0)],
    8: [(CROSS, K, T0)],
    9: [(NEAR, T2), (BEGIN, E1)],
    12: [(FORWARD, T1, T2), (NEAR, T3), (BEGIN, B0)],
    13: [(CROSS, T1, T2)],
    14: [(NEAR, E0), (FORWARD, T3), (BEGIN, B1)],
    17: [(FORWARD, E0), (NEAR, E1, B0), (BEGIN, B2)],
    18: [(CROSS, T3, E0)],
    19: [(FORWARD, E1), (NEAR, B1), (BEGIN, B3)],
    22: [(FORWARD, B0, B1), (NEAR, B2, B3)],
    23: [(CROSS, E1, B0, B1)],
    24: [(FORWARD, B2)],
    25: [(FORWARD, B3)],
    26: [(CROSS, B2, B3)],
    37: [(R2, E0, E1)],
    38: [(R2, B0)],
    39: [(R3, E0, E1), (R2, B1)],
    40: [(R4, E0)],
    41: [(R3, B0, B1), (R2, B2, B3), (R4, E1)],
    42: [(R5, E0)],
    43: [(R3, B2), (R4, B0)],
    46: [(R3, B3), (R2, T0, T1), (R4, B1, B2)],
    47: [(R5, E1, B0)],
    48: [(R3, T0), (R4, B3)],
    49: [(R3, T1), (R4, T0)],
    51: [(R2, T2, T3), (R4, T1)],
    52: [(R5, B1, B2)],
    53: [(R2, K), (R3, T2)],
    54: [(R3, T3)],
    56: [(R3, K), (R2, W), (R4, T2)],
    57: [(R5, B3, T0, T1)],
    58: [(R2, S), (R3, W), (R4, K, T3)],
    59: [(R3, S), (R4, W)],
    60: [(R4, S), (R5, T2, T3)],
    61: [(R2, N), (R5, K, W)],
    63: [(R3, N), (R4, N), (R5, S)],
    65: [(R5, N)],
}


def spare_groups(spare):
    count = lax.axis_size("dp")
    return [list(range(at, at + spare)) for at in range(0, count, spare)]


def padded(field, rows, across):
    side = field.shape[1]
    field = jnp.pad(field, ((0, 0), (0, rows - side), (0, across - side), (0, 0)))
    return field.reshape(-1, field.shape[3])


def local(
    input_big,
    input_small,
    views_big,
    views_small,
    cotan_big,
    cotan_small,
    *params,
):
    filters, affines = params[0::2], params[1::2]
    devices = lax.axis_size("dp")
    spare = devices // 16
    inputs, cotans = (input_big, input_small), (cotan_big, cotan_small)
    counts = [item.shape[0] for item in inputs]
    images, full_rows, half_rows = images_of(counts, [item.shape[1] for item in inputs])
    c_in, c_out = input_big.shape[3], cotan_big.shape[3]
    mid1, mid2 = filters[NARROW].shape[1], filters[SHRINK].shape[1]
    widths = (c_in, mid1, mid2, c_out)
    wide = widths_of(*widths)
    by_group = [next(image for image in images if image.group == g) for g in range(2)]
    x = jnp.concatenate([padded(inputs[g], by_group[g].count // 16, 16) for g in range(2)])
    cot = jnp.concatenate([padded(cotans[g], by_group[g].half_count // 8, 8) for g in range(2)])
    view = jnp.concatenate([views_big, views_small])
    hot = (view[:, None] == jnp.arange(2, dtype=jnp.int32)[None, :]).astype(F32)
    hot = jnp.broadcast_to(hot.reshape(-1, 1), (2 * len(images), 128))

    parts = [item.T for item in affines]
    shards = list(filters)
    if spare > 1:
        groups = spare_groups(spare)
        shards = [lax.all_gather(item, "dp", axis_index_groups=groups, tiled=True) for item in filters]
        gathered = lax.all_gather(jnp.concatenate(parts, axis=1), "dp", axis_index_groups=groups)
        parts, at = [], 0
        for item in affines:
            share = item.shape[0]
            parts.append(jnp.moveaxis(gathered[:, :, at : at + share], 0, 1).reshape(2, -1))
            at += share
    places = table_places([item.shape[1] for item in parts]) + [512]
    parts = [
        jnp.pad(item, ((0, 0), (0, places[k + 1] - places[k] - item.shape[1]))) for k, item in enumerate(parts)
    ]
    shards.append(jnp.pad(jnp.concatenate(parts, axis=1).reshape(8, 128), ((0, 8), (0, 0))))
    shapes = [item.shape for item in shards]
    lane_total = sum(wide)

    def field(*shape):
        return pltpu.VMEM(shape, F32)

    def rounded(*shape):
        return pltpu.VMEM(shape, BF16)

    def layer_rows(k):
        return half_rows if k in (STRIDE, EXPAND, BYPASS) else full_rows

    rounds = [wide[:5] + [2 * c_out], wide[:5] + [2 * c_out]]
    rounds[0][NARROW] += 128
    sums = [
        [Reduce.scratch(8, width, spare, k == LAST) for k, width in enumerate(rounds[0])],
        [Reduce.scratch(16, width // 2, spare, k == LAST, BF16) for k, width in enumerate(rounds[1])],
    ]
    operands = dict(x=x, cot=cot, hot=hot, shards=shards)
    results = dict(
        out=jax.ShapeDtypeStruct((half_rows, c_out), BF16),
        dinput=jax.ShapeDtypeStruct((full_rows, c_in), BF16),
        daffine=jax.ShapeDtypeStruct((8, lane_total), F32),
        dfilter=[jax.ShapeDtypeStruct(shape, BF16) for shape in shapes[:7]],
    )
    scratch = dict(
        whole=[rounded(4, 4, *shape) for shape in shapes],
        done=[rounded(*shape) for shape in shapes[:7]],
        landing=[Scatter.scratch(*piece.sizes(shapes[piece.layer])) for piece in PIECES[:-1]],
        normed=[rounded(layer_rows(k), wide[k]) for k in range(7)],
        slope=[None if k in (EXPAND, BYPASS) else rounded(layer_rows(k), wide[k]) for k in range(7)],
        affine=[field(8, width) for width in wide],
        scale=[field(-(-len(images) // 8) * 8, width) for width in wide],
        x_v=rounded(full_rows, c_in),
        cot_v=rounded(half_rows, c_out),
        hot_v=field(*hot.shape),
        cnt=field(8, 128),
        daffine_v=field(8, lane_total),
        F=field(max(full_rows, 4 * half_rows), c_in),
        G=field(half_rows, mid2),
        S=field(max(full_rows, 4 * half_rows), mid1),
        K=field(mid2 // 128, full_rows + 64, 128),
        EVEN=field(full_rows, 128),
        SPREAD=field(full_rows, 128),
        taps1=rounded(full_rows + 32, 3 * mid1),
        grad3=rounded(full_rows + 32, 3 * mid1),
        act_spatial=rounded(full_rows, mid1),
        upper=rounded(full_rows, c_in),
        taps2=rounded(half_rows, 9 * mid2),
        act_stride=rounded(half_rows, mid2),
        even=rounded(half_rows, c_in),
        given=[[field(8, width) for width in way] for way in rounds],
        total=[[field(8, width) for width in way] for way in rounds],
        slots=[[item[:-2] for item in way] for way in sums],
        packed=[rounded(16, width // 2) for width in rounds[1]],
        summed=[(rounded if k == LAST else field)(16, width // 2) for k, width in enumerate(rounds[1])],
        sums_sem=[[item[-2:] for item in way] for way in sums],
        load_sem=pltpu.SemaphoreType.DMA((len(PIECES) + 3,)),
        store_sem=pltpu.SemaphoreType.DMA((16,)),
        gather_send=pltpu.SemaphoreType.DMA((len(PIECES), Gather.PHASES)),
        gather_recv=pltpu.SemaphoreType.DMA((len(PIECES), Gather.PHASES)),
        scatter_send=pltpu.SemaphoreType.DMA((len(PIECES), Scatter.PHASES)),
        scatter_recv=pltpu.SemaphoreType.DMA((len(PIECES), Scatter.PHASES)),
    )
    flat_in, in_tree = jax.tree.flatten(operands)
    flat_out, out_tree = jax.tree.flatten(results)
    flat_scratch, scratch_tree = jax.tree.flatten(scratch)

    def kernel(*flat):
        here = len(flat_in) + len(flat_out)
        refs = jax.tree.unflatten(in_tree, flat[: len(flat_in)])
        refs |= jax.tree.unflatten(out_tree, flat[len(flat_in) : here])
        refs |= jax.tree.unflatten(scratch_tree, flat[here:])
        step_kernel(spare, images, widths, types.SimpleNamespace(**refs))

    flat_out = pl.pallas_call(
        kernel,
        out_shape=flat_out,
        in_specs=[pl.BlockSpec(memory_space=pl.ANY)] * len(flat_in),
        out_specs=[pl.BlockSpec(memory_space=pl.ANY)] * len(flat_out),
        scratch_shapes=flat_scratch,
        compiler_params=pltpu.CompilerParams(
            collective_id=KERNEL_ID, has_side_effects=True, vmem_limit_bytes=VMEM_BYTES
        ),
    )(*flat_in)
    done = types.SimpleNamespace(**jax.tree.unflatten(out_tree, flat_out))

    shares = [width // devices for width in wide]
    views = [(group, half) for half in (True, False) for group in range(2)]

    def image_shape(group, half):
        side = by_group[group].half_side if half else by_group[group].side
        return counts[group], side, side, c_out if half else c_in

    def finish(*flat):
        given, images_out, grads_out, affine_out = flat[:10], flat[10:14], flat[14:21], flat[21:28]
        held, sem = flat[28:38], flat[38]
        copies = [pltpu.make_async_copy(given[k], held[k], sem.at[k]) for k in range(10)]
        for copy in copies:
            copy.start()
        for copy in copies:
            copy.wait()
        out, dinput, daffine, *grads = held
        for ref, (group, half) in zip(images_out, views):
            image, rows = by_group[group], out if half else dinput
            start = image.half_at if half else image.at
            count = image.half_count if half else image.count
            across = 8 if half else 16
            number, side, _, width = ref.shape
            for n in range(number):
                for row in range(side):
                    here = start + n * count + row * across
                    ref[n, row] = rows[here : here + across, :][:side]
        for ref, grad in zip(grads_out, grads):
            ref[...] = grad[...].astype(F32)
        me, at = lax.axis_index("dp"), 0
        for k, ref in enumerate(affine_out):
            first = me * shares[k]
            block, shift = lax.div(first, 128), lax.rem(first, 128)
            rows = daffine[:, pl.ds(pl.multiple_of(at + block * 128, 128), 128)]
            ref[...] = pltpu.roll(rows, lax.rem(128 - shift, 128), 1)[0:2, 0 : shares[k]]
            at += wide[k]

    finals = [done.out, done.dinput, done.daffine, *done.dfilter]
    outs = pl.pallas_call(
        finish,
        out_shape=[jax.ShapeDtypeStruct(image_shape(*view), BF16) for view in views]
        + [jax.ShapeDtypeStruct(shape, F32) for shape in shapes[:7]]
        + [jax.ShapeDtypeStruct((2, share), F32) for share in shares],
        in_specs=[pl.BlockSpec(memory_space=pl.ANY)] * 10,
        out_specs=[pl.BlockSpec(memory_space=pltpu.VMEM)] * 18,
        scratch_shapes=[pltpu.VMEM(item.shape, item.dtype) for item in finals] + [pltpu.SemaphoreType.DMA((10,))],
        compiler_params=pltpu.CompilerParams(vmem_limit_bytes=VMEM_BYTES),
    )(*finals)
    results = list(outs[:4])
    for grad, affine in zip(outs[4:11], outs[11:]):
        if spare > 1:
            grad = lax.psum_scatter(grad, "dp", axis_index_groups=spare_groups(spare), tiled=True)
        results += [grad, affine.T]
    return tuple(results)


VMEM_BYTES = 65400 * 1024


def solution(mesh):
    images = P(("dp", "outer"), None, None, None)
    rows = P("dp", None)
    return jax.shard_map(
        local,
        mesh=mesh,
        in_specs=(images, images, P(("dp", "outer")), P(("dp", "outer")), images, images) + (rows,) * 14,
        out_specs=(images,) * 4 + (rows,) * 14,
        check_vma=False,
    )
```

```python
import functools
import types

import jax
import jax.numpy as jnp
from jax import lax
from jax.experimental import pallas as pl
from jax.experimental.pallas import tpu as pltpu
from jax.sharding import PartitionSpec as P

MESH = pl.DeviceIdType.MESH
F32 = jnp.float32
BF16 = jnp.bfloat16


class Place:
    def __init__(self, spare):
        self.spare = spare
        dp = lax.axis_index("dp")
        self.core = lax.axis_index("outer")
        self.rest = lax.rem(dp, spare)
        group = lax.div(dp, spare)
        self.far = lax.div(group, 4)
        self.near = lax.rem(group, 4)
        high, low = lax.div(self.near, 2), lax.rem(self.near, 2)
        self.first = 2 * lax.rem(high + 1 - self.core, 2) + lax.rem(low + self.core, 2)
        self.second = 2 * lax.rem(high + self.core, 2) + lax.rem(low + 1 - self.core, 2)
        self.both = 3 - self.near

    def device(self, far=None, near=None, core=None, rest=None):
        far = self.far if far is None else far
        near = self.near if near is None else near
        core = self.core if core is None else core
        rest = self.rest if rest is None else rest
        return ((far * 4 + near) * self.spare + rest, core)

    def fars(self):
        return [self.device(far=lax.rem(self.far + k, 4)) for k in range(1, 4)]

    def nears(self):
        return [self.device(near=lax.rem(self.near + k, 4)) for k in range(1, 4)]

    def cross_nears(self):
        return [
            self.device(near=lax.rem(self.near + k, 4), core=1 - self.core) for k in range(1, 4)
        ]

    def sibling(self):
        return self.device(core=1 - self.core)

    def rests(self):
        return [
            self.device(rest=lax.rem(self.rest + k, self.spare)) for k in range(1, self.spare)
        ]


def greet(devices):
    barrier = pltpu.get_barrier_semaphore()
    for device in devices:
        pl.semaphore_signal(barrier, inc=1, device_id=device, device_id_type=MESH)
    pl.semaphore_wait(barrier, len(devices))


def send(src, dst, send_sem, recv_sem, device):
    pltpu.make_async_remote_copy(
        src_ref=src,
        dst_ref=dst,
        send_sem=send_sem,
        recv_sem=recv_sem,
        device_id=device,
        device_id_type=MESH,
    ).start()


def await_bytes(like, sem):
    pltpu.make_async_copy(like, like, sem).wait()


class Reduce:
    def __init__(self, place, split, refs):
        self.place = place
        self.split = split
        self.refs = refs

    @staticmethod
    def scratch(rows, width, spare, split, kind=F32):
        piece = width // 2 if split else width
        shapes = []
        for count in Reduce.counts(spare, split):
            shapes.append(pltpu.VMEM((count, rows, piece), kind))
            shapes.append(pltpu.VMEM((rows, piece), kind))
        phases = len(Reduce.counts(spare, split))
        shapes.append(pltpu.SemaphoreType.DMA((phases + 1,)))
        shapes.append(pltpu.SemaphoreType.DMA((phases + 1,)))
        return shapes

    @staticmethod
    def counts(spare, split):
        counts = [1, 3, 3] if split else [7, 3]
        return counts + ([spare - 1] if spare > 1 else [])

    def run(self, src, out, between=None):
        place, split = self.place, self.split
        send_sem, recv_sem = self.refs[-2:]
        width = src.shape[1]
        piece = width // 2
        if split:
            phases = [[place.sibling()], place.nears(), place.fars()]
            mine = pl.ds(pl.multiple_of(place.core * piece, 128), piece)
            other = pl.ds(pl.multiple_of((1 - place.core) * piece, 128), piece)
        else:
            phases = [place.cross_nears() + place.nears() + [place.sibling()], place.fars()]
        if place.spare > 1:
            phases.append(place.rests())
        held = src
        for p, devices in enumerate(phases):
            slots, total = self.refs[2 * p], self.refs[2 * p + 1]
            crossing = split and p == 0
            sent = src.at[:, other] if crossing else held
            for k, device in enumerate(devices):
                send(sent, slots.at[k], send_sem.at[p], recv_sem.at[p], device)
            if between is not None:
                between(p)
            await_bytes(slots, recv_sem.at[p])
            value = (src[:, mine] if crossing else held[...]).astype(F32)
            for k in range(len(devices)):
                value = value + slots[k].astype(F32)
            last = p == len(phases) - 1 and not split
            if last:
                out[...] = value
            else:
                total[...] = value.astype(total.dtype)
            held = total
        if split:
            send(held, out.at[:, mine], send_sem.at[len(phases)], recv_sem.at[len(phases)], place.sibling())
            out[:, mine] = held[...]
            await_bytes(out.at[:, other], recv_sem.at[len(phases)])
        for p in range(len(phases)):
            await_bytes(self.refs[2 * p], send_sem.at[p])
        if split:
            await_bytes(held, send_sem.at[len(phases)])


class Piece:
    def __init__(self, layer, band=0, bands=1, strip=0, strips=1, halved=True, direct=False):
        self.layer, self.halved, self.direct = layer, halved, direct
        self.band, self.bands, self.strip, self.strips = band, bands, strip, strips

    def sizes(self, shape):
        return shape[-2] // self.bands, shape[-1] // (2 if self.halved else 1) // self.strips

    def window(self, place, shape):
        count, width = self.sizes(shape)
        rows = pl.ds(self.band * count, count)
        if not self.halved:
            return rows, pl.ds(0, width), None
        half, skip = shape[-1] // 2, self.strip * width
        cols = pl.ds(pl.multiple_of(place.core * half + skip, 128), width)
        others = pl.ds(pl.multiple_of((1 - place.core) * half + skip, 128), width)
        return rows, cols, others


class Gather:
    PHASES = 5

    def __init__(self, place, whole, piece, send_sem, recv_sem):
        self.place, self.whole, self.piece = place, whole, piece
        self.halved, self.direct = piece.halved, piece.direct
        self.send_sem, self.recv_sem = send_sem, recv_sem
        self.rows, self.cols, self.others = piece.window(place, whole.shape)

    def part(self, far, near):
        return self.whole.at[far, near, self.rows, self.cols]

    def start(self):
        place = self.place
        for device in place.fars():
            block = self.part(place.far, place.near)
            send(block, block, self.send_sem.at[0], self.recv_sem.at[0], device)

    def near(self):
        place = self.place
        await_bytes(self.part(pl.ds(0, 3), 0), self.recv_sem.at[0])
        block = self.part(pl.ds(0, 4), place.near)
        partners = [place.first, place.second] + ([place.both] if self.direct else [])
        for phase, partner in enumerate(partners, 1):
            send(
                block,
                block,
                self.send_sem.at[phase],
                self.recv_sem.at[phase],
                place.device(near=partner),
            )

    def forward(self):
        place = self.place
        block = self.part(pl.ds(0, 4), place.first)
        await_bytes(block, self.recv_sem.at[1])
        if self.direct:
            return
        send(
            block, block, self.send_sem.at[3], self.recv_sem.at[3], place.device(near=place.second)
        )

    def cross(self):
        place = self.place
        await_bytes(self.part(pl.ds(0, 4), place.second), self.recv_sem.at[2])
        await_bytes(self.part(pl.ds(0, 4), place.both), self.recv_sem.at[3])
        if self.halved:
            block = self.part(pl.ds(0, 4), pl.ds(0, 4))
            send(block, block, self.send_sem.at[4], self.recv_sem.at[4], place.sibling())

    def finish(self):
        if self.halved:
            await_bytes(
                self.whole.at[pl.ds(0, 4), pl.ds(0, 4), self.rows, self.others], self.recv_sem.at[4]
            )

    def settle(self):
        await_bytes(self.part(pl.ds(0, 3), 0), self.send_sem.at[0])
        for phase in (1, 2, 3):
            await_bytes(self.part(pl.ds(0, 4), 0), self.send_sem.at[phase])
        if self.halved:
            await_bytes(self.part(pl.ds(0, 4), pl.ds(0, 4)), self.send_sem.at[4])


class Scatter:
    PHASES = 5

    def __init__(self, place, whole, piece, landing, done, send_sem, recv_sem):
        self.place, self.whole, self.landing, self.done = place, whole, landing, done
        self.direct = piece.direct
        self.send_sem, self.recv_sem = send_sem, recv_sem
        self.rows, self.cols, self.others = piece.window(place, whole.shape)
        self.half = piece.sizes(whole.shape)[1]
        self.base = place.core * (whole.shape[3] // 2) + piece.strip * self.half

    @staticmethod
    def scratch(rows, half):
        return [
            pltpu.VMEM((4, 4, rows, half), BF16),
            pltpu.VMEM((2, 4, rows, half), BF16),
            pltpu.VMEM((4, rows, half), BF16),
            pltpu.VMEM((3, rows, half), BF16),
        ]

    def stretch(self):
        rows = self.landing[2].shape[1]
        width = 512 if rows < 64 else 256 if rows < 128 else 128
        return min(width, self.half)

    def add(self, near, block):
        width = self.stretch()
        whole, base, rows = self.whole, self.base, self.rows

        @pl.loop(0, self.half // width)
        def _(b):
            here = pl.ds(pl.multiple_of(base + b * width, 128), width)
            there = pl.ds(pl.multiple_of(b * width, 128), width)
            whole[:, near, rows, here] = whole[:, near, rows, here] + block[:, :, there]

    def start(self):
        send(
            self.whole.at[pl.ds(0, 4), pl.ds(0, 4), self.rows, self.others],
            self.landing[0],
            self.send_sem.at[0],
            self.recv_sem.at[0],
            self.place.sibling(),
        )

    def second(self):
        place = self.place
        await_bytes(self.landing[0], self.recv_sem.at[0])
        width = self.stretch()
        whole, base, rows, block = self.whole, self.base, self.rows, self.landing[0]
        strips = self.half // width

        @pl.loop(0, 4 * strips)
        def _(i):
            near, b = lax.div(i, strips), lax.rem(i, strips)
            here = pl.ds(pl.multiple_of(base + b * width, 128), width)
            there = pl.ds(pl.multiple_of(b * width, 128), width)
            whole[:, near, rows, here] = whole[:, near, rows, here] + block[:, near, :, there]

        if self.direct:
            landings = (self.landing[1].at[0], self.landing[1].at[1], self.landing[2])
            for k, near in enumerate((place.second, place.both, place.first)):
                send(
                    whole.at[pl.ds(0, 4), near, self.rows, self.cols],
                    landings[k],
                    self.send_sem.at[max(k, 1)],
                    self.recv_sem.at[max(k, 1)],
                    place.device(near=near),
                )
            return
        for k, near in enumerate((place.second, place.both)):
            send(
                whole.at[pl.ds(0, 4), near, self.rows, self.cols],
                self.landing[1].at[k],
                self.send_sem.at[1],
                self.recv_sem.at[1],
                place.device(near=place.second),
            )

    def first(self):
        place = self.place
        await_bytes(self.landing[1], self.recv_sem.at[1])
        if self.direct:
            self.add(place.near, self.landing[1].at[1])
            self.add(place.near, self.landing[1].at[0])
            return
        self.add(place.first, self.landing[1].at[1])
        send(
            self.whole.at[pl.ds(0, 4), place.first, self.rows, self.cols],
            self.landing[2],
            self.send_sem.at[2],
            self.recv_sem.at[2],
            place.device(near=place.first),
        )
        self.add(place.near, self.landing[1].at[0])

    def fars(self):
        place = self.place
        await_bytes(self.landing[2], self.recv_sem.at[2])
        self.add(place.near, self.landing[2])
        for k in range(1, 4):
            far = lax.rem(place.far + k, 4)
            send(
                self.whole.at[far, place.near, self.rows, self.cols],
                self.landing[3].at[k - 1],
                self.send_sem.at[3],
                self.recv_sem.at[3],
                place.device(far=far),
            )

    def cross(self):
        place = self.place
        await_bytes(self.landing[3], self.recv_sem.at[3])
        blocks = self.half // 128
        whole, base, rows, block, done = self.whole, self.base, self.rows, self.landing[3], self.done

        @pl.loop(0, blocks)
        def _(b):
            here = pl.ds(pl.multiple_of(base + b * 128, 128), 128)
            there = pl.ds(pl.multiple_of(b * 128, 128), 128)
            total = whole[place.far, place.near, rows, here].astype(F32)
            for k in range(3):
                total = total + block[k, :, there].astype(F32)
            done[rows, here] = total.astype(BF16)

        half = done.at[self.rows, self.cols]
        send(half, half, self.send_sem.at[4], self.recv_sem.at[4], place.sibling())

    def finish(self):
        await_bytes(self.done.at[self.rows, self.others], self.recv_sem.at[4])

    def settle(self):
        await_bytes(self.landing[0], self.send_sem.at[0])
        await_bytes(self.landing[1], self.send_sem.at[1])
        await_bytes(self.landing[2], self.send_sem.at[2])
        await_bytes(self.landing[3], self.send_sem.at[3])
        await_bytes(self.done.at[self.rows, self.cols], self.send_sem.at[4])
EPS = 1e-05
KERNEL_ID = 1
NARROW, SPATIAL, WIDEN, SHRINK, STRIDE, EXPAND, BYPASS = range(7)
TABLE = 7
LAST = 5
NN = (((1,), (0,)), ((), ()))
NT = (((1,), (1,)), ((), ()))
TN = (((0,), (0,)), ((), ()))


def mul(a, b, dims):
    return lax.dot_general(a, b, dims, preferred_element_type=F32)


def lanes(i, width=128):
    return pl.ds(pl.multiple_of(i * width, width), width)


def normal_parts(value):
    bell = jnp.exp(-0.5 * value * value) * 0.3989422804014327
    step = 1.0 / (1.0 + 0.2316419 * jnp.abs(value))
    series = 1.330274429 * step - 1.821255978
    series = series * step + 1.781477937
    series = series * step - 0.356563782
    series = series * step + 0.319381530
    tail = bell * (series * step)
    cdf = jnp.where(value >= 0.0, 1.0 - tail, tail)
    return cdf, value * bell


class Image:
    def __init__(self, index, group, side, at, half_at):
        self.index, self.group, self.side = index, group, side
        self.half_side = (side - 1) // 2 + 1
        self.at, self.count = at, (side + 1) * 16
        self.half_at, self.half_count = half_at, -(-(self.half_side + 1) * 8 // 16) * 16

    def rows(self, half):
        return pl.ds(self.half_at, self.half_count) if half else pl.ds(self.at, self.count)

    def inside(self, half):
        count = self.half_count if half else self.count
        side = self.half_side if half else self.side
        bits = 3 if half else 4
        place = lax.broadcasted_iota(jnp.int32, (count, 128), 0)
        return jnp.logical_and(
            lax.shift_right_logical(place, bits) < side, lax.bitwise_and(place, (1 << bits) - 1) < side
        )


def images_of(counts, sides):
    images, at, half_at = [], 0, 0
    for group in range(2):
        for _ in range(counts[group]):
            image = Image(len(images), group, sides[group], at, half_at)
            images.append(image)
            at += image.count
            half_at += image.half_count
    return images, at, half_at


def widths_of(c_in, mid1, mid2, c_out):
    return [mid1, mid1, c_in, mid2, mid2, c_out, c_out]


class Layer:
    def __init__(self, width, half, at):
        self.width, self.half, self.at = width, half, at


def rows_piece(whole, start, count, cols):
    rows, pieces = whole.shape[2], []
    while count:
        shard, skip = divmod(start, rows)
        taken = min(rows - skip, count)
        pieces.append(whole[shard // 4, shard % 4, skip : skip + taken, cols])
        start, count = start + taken, count - taken
    return pieces[0] if len(pieces) == 1 else jnp.concatenate(pieces, axis=0)


def store_piece(whole, start, value):
    rows, done = whole.shape[2], 0
    while done < value.shape[0]:
        shard, skip = divmod(start + done, rows)
        taken = min(rows - skip, value.shape[0] - done)
        whole[shard // 4, shard % 4, skip : skip + taken, :] = value[done : done + taken]
        done += taken


def table_places(shares):
    places, at = [], 0
    for share in shares:
        if at % 128 + share > 128:
            at = -(-at // 128) * 128
        places.append(at)
        at += share
    return places


def step_kernel(spare, images, widths, refs):
    place = Place(spare)
    full_rows, half_rows = refs.x.shape[0], refs.cot.shape[0]
    hot, cnt = refs.hot_v, refs.cnt
    whole = refs.whole
    c_in, mid1, mid2, c_out = widths
    loads = []

    def load(src, dst):
        copy = pltpu.make_async_copy(src, dst, refs.load_sem.at[len(loads)])
        copy.start()
        loads.append(copy)
        return copy

    gathers = [
        Gather(place, whole[piece.layer], piece, refs.gather_send.at[k], refs.gather_recv.at[k])
        for k, piece in enumerate(PIECES)
    ]
    shard_loads = [
        load(
            refs.shards[item.piece.layer].at[item.rows, item.cols], item.part(place.far, place.near)
        )
        for item in gathers
    ]
    load_x = load(refs.x, refs.x_v)
    load_cot = load(refs.cot, refs.cot_v)
    scatters = [
        Scatter(
            place,
            whole[piece.layer],
            piece,
            refs.landing[k],
            refs.done[piece.layer],
            refs.scatter_send.at[k],
            refs.scatter_recv.at[k],
        )
        for k, piece in enumerate(PIECES[:-1])
    ]

    def pieces_of(items, layer):
        return [item for item, piece in zip(items, PIECES) if piece.layer == layer]

    def arrive(layer):
        for item in pieces_of(gathers, layer):
            item.finish()

    def let_go(layer):
        for item in pieces_of(gathers, layer):
            item.settle()

    def send_off(layer):
        for item in pieces_of(scatters, layer):
            item.start()

    def begin(k):
        shard_loads[k].wait()
        gathers[k].start()

    points = []

    def point():
        now = len(points)
        points.append(now)
        for step, *items in PLAN.get(now, ()):
            for k in items:
                if step is BEGIN:
                    begin(k)
                else:
                    step(gathers[k] if step in GATHER_STEPS else scatters[k])

    greet([place.sibling()] + place.nears() + place.cross_nears() + place.fars() + place.rests())

    at = [0, 0]
    for image in images:
        seen = refs.views[image.group][at[image.group]].astype(F32)
        at[image.group] += 1
        row = 2 * image.index
        hot[row : row + 1, :] = jnp.full((1, 128), 1.0 - seen)
        hot[row + 1 : row + 2, :] = jnp.full((1, 128), seen)

    layers, lane = [], 0
    for k, width in enumerate(widths_of(*widths)):
        layers.append(Layer(width, k in (STRIDE, EXPAND, BYPASS), lane))
        lane += width
        layers[k].normed, layers[k].slope = refs.normed[k], refs.slope[k]
        layers[k].affine, layers[k].scale = refs.affine[k], refs.scale[k]

    def reduce(way, k, during=None):
        def between(p):
            if p < 2:
                point()
                if during is not None:
                    during(p)

        given, total = refs.given[way][k], refs.total[way][k]
        run = Reduce(place, k == LAST, list(refs.slots[way][k]) + list(refs.sums_sem[way][k])).run
        if way == 0:
            run(given, total, between)
        else:
            half = given.shape[1] // 2
            packed, summed = refs.packed[k], refs.summed[k]
            packed[...] = jnp.concatenate([given[:, 0:half], given[:, half:]], axis=0).astype(BF16)
            run(packed, summed, between)
            value = summed[...].astype(F32)
            total[:, 0:half], total[:, half:] = value[0:8], value[8:16]
        point()

    def hot_row(image, view):
        row = 2 * image.index + view
        return hot[row : row + 1, :]

    def of_image(image, by_view):
        row = 2 * image.group
        return hot_row(image, 0) * by_view[row : row + 1] + hot_row(image, 1) * by_view[row + 1 : row + 2]

    def by_view(values):
        out = []
        for group in range(2):
            for view in range(2):
                total = None
                for image in images:
                    if image.group == group:
                        term = values[image.index] * hot_row(image, view)
                        total = term if total is None else total + term
                out.append(total)
        return out

    def put_sums(st, cols, firsts, seconds):
        st[:, cols] = jnp.concatenate(by_view(firsts) + by_view(seconds), axis=0)

    def column_sum(value):
        return jnp.sum(value, axis=0, keepdims=True)

    def field_sums(layer, st, field, i, masked, cols=None):
        firsts, seconds = [], []
        for image in images:
            z = field(image, i)
            if masked:
                z = jnp.where(image.inside(layer.half), z, 0.0)
            firsts.append(column_sum(z))
            seconds.append(column_sum(z * z))
        put_sums(st, lanes(i) if cols is None else cols, firsts, seconds)

    def statistics(total):
        counted = cnt[0:4, :]
        mean = total[0:4] / counted
        return mean, lax.rsqrt(total[4:8] / counted - mean * mean + EPS)

    def normed_of(layer, image, cols, z, mean, scale):
        stretch = of_image(image, scale)
        layer.scale[image.index : image.index + 1, cols] = stretch
        return (z - of_image(image, mean)) * stretch

    def forward(name, field, sink, extra=None):
        layer = layers[name]

        @pl.loop(0, layer.width // 128)
        def _(i):
            cols = lanes(i)
            mean, scale = statistics(refs.total[0][name][:, cols])
            gain, bias = layer.affine[0:1, cols], layer.affine[1:2, cols]
            for image in images:
                rows, inside = image.rows(layer.half), image.inside(layer.half)
                normed = normed_of(layer, image, cols, field(image, i), mean, scale)
                value = normed * gain + bias
                if extra is not None:
                    value = value + extra[rows, cols].astype(F32)
                cdf, rest = normal_parts(value)
                layer.normed[rows, cols] = normed.astype(BF16)
                layer.slope[rows, cols] = jnp.where(inside, cdf + rest, 0.0).astype(BF16)
                sink(image, i, jnp.where(inside, value * cdf, 0.0))

    def gradient_sums(name, grad, st):
        layer = layers[name]

        @pl.loop(0, layer.width // 128)
        def _(i):
            cols = lanes(i)
            firsts, seconds = [], []
            for image in images:
                g = grad(image, i)
                firsts.append(column_sum(g))
                seconds.append(column_sum(g * layer.normed[image.rows(layer.half), cols].astype(F32)))
            put_sums(st, cols, firsts, seconds)

    def gradient(name, grad, sums, sink=None):
        layer = layers[name]

        @pl.loop(0, layer.width // 128)
        def _(i):
            cols = lanes(i)
            first, second = sums(i)
            here = pl.ds(pl.multiple_of(layer.at + i * 128, 128), 128)
            refs.daffine_v[0:1, here] = column_sum(second)
            refs.daffine_v[1:2, here] = column_sum(first)
            first, second = first / cnt[0:4, :], second / cnt[0:4, :]
            gain = layer.affine[0:1, cols]
            for image in images:
                rows = image.rows(layer.half)
                stretch = gain * layer.scale[image.index : image.index + 1, cols]
                normed = layer.normed[rows, cols].astype(F32)
                value = stretch * (grad(image, i) - of_image(image, first) - normed * of_image(image, second))
                value = jnp.where(image.inside(layer.half), value, 0.0)
                if sink is None:
                    layer.normed[rows, cols] = value.astype(BF16)
                else:
                    sink(image, i, value)

    def totals_of(name):
        def sums(i):
            total = refs.total[1][name][:, lanes(i)]
            return total[0:4], total[4:8]

        return sums

    def shifted(target, image, i, value):
        width = target.shape[1] // 3
        rows = pl.ds(16 + image.at, image.count)
        for q in range(3):
            moved = value if q == 1 else pltpu.roll(value, 1 if q == 0 else image.count - 1, 0)
            target[rows, pl.ds(pl.multiple_of(q * width + i * 128, 128), 128)] = moved.astype(BF16)

    def clear_ends(target, top, from_row):
        target[0:top, :] = jnp.zeros((top, target.shape[1]), target.dtype)
        target[from_row:, :] = jnp.zeros((target.shape[0] - from_row, target.shape[1]), target.dtype)

    def strided(start):
        return pl.ds(start, 8, stride=2)

    F, G, K, S = refs.F, refs.G, refs.K, refs.S
    x_v, taps1, act_spatial, upper = refs.x_v, refs.taps1, refs.act_spatial, refs.upper
    taps2, act_stride, even, grad3 = refs.taps2, refs.act_stride, refs.even, refs.grad3
    clear_ends(taps1, 16, 16 + full_rows)
    clear_ends(grad3, 16, 16 + full_rows)
    blocks2 = mid2 // 128
    K[:, 0:32, :] = jnp.zeros((blocks2, 32, 128), F32)
    K[:, 32 + full_rows :, :] = jnp.zeros((blocks2, K.shape[1] - 32 - full_rows, 128), F32)
    EVEN, SPREAD = refs.EVEN, refs.SPREAD
    SPREAD[...] = jnp.zeros(SPREAD.shape, F32)

    places = table_places([layer.width // 16 for layer in layers])

    def spread_affine(k):
        table, layer = whole[TABLE], layers[k]
        share = layer.width // 16
        row, skip = divmod(places[k], 128)
        to = lax.broadcasted_iota(jnp.int32, (16, 128), 1)
        owner = lax.broadcasted_iota(jnp.int32, (16, 128), 0)
        pick_from = lax.broadcasted_iota(jnp.int32, (128, 128), 0)
        pick_to = lax.broadcasted_iota(jnp.int32, (128, 128), 1)
        chosen = (pick_from == skip + lax.rem(pick_to, share)).astype(BF16)
        for kind in range(2):
            held = [
                table[g // 4, g % 4, :, :].astype(F32)[row + 4 * kind : row + 4 * kind + 1] for g in range(16)
            ]
            spread = mul(jnp.concatenate(held, axis=0).astype(BF16), chosen, NN)
            for b in range(layer.width // 128):
                mine = jnp.where(lax.div(b * 128 + to, share) == owner, spread, 0.0)
                layer.affine[kind : kind + 1, b * 128 : (b + 1) * 128] = column_sum(mine)

    load_x.wait()
    point()

    def plain(buffer):
        return lambda image, i: buffer[image.rows(False), lanes(i)]

    def plain_half(buffer):
        return lambda image, i: buffer[image.rows(True), lanes(i)]

    def halves(buffer, base):
        blocks = F.shape[1] // 128

        def field(image, i):
            band = base + lax.div(i, blocks)
            rows = pl.ds(pl.multiple_of(band * half_rows + image.half_at, 8), image.half_count)
            return buffer[rows, lanes(lax.rem(i, blocks))]

        return field

    arrive(NARROW)
    F[0:full_rows, 0:mid1] = mul(x_v[...], whole[NARROW][...].reshape(c_in, mid1), NN)

    @pl.loop(0, mid1 // 128)
    def _(i):
        field_sums(layers[NARROW], refs.given[0][NARROW], plain(F), i, False)

    pixels = []
    for image in images:
        pixels.append(jnp.full((1, 128), float(image.side * image.side), F32))
    empty = [jnp.zeros((1, 128), F32) for _ in images]
    put_sums(refs.given[0][NARROW], pl.ds(mid1, 128), pixels, empty)

    def during(p):
        if p == 0:
            for k in (NARROW, SPATIAL, WIDEN):
                spread_affine(k)

    point()
    reduce(0, NARROW, during)
    cnt[...] = refs.total[0][NARROW][:, mid1 : mid1 + 128]
    forward(NARROW, plain(F), functools.partial(shifted, taps1))

    point()
    arrive(SPATIAL)
    for r in range(3):
        kernel = rows_piece(whole[SPATIAL], r * 3 * mid1, 3 * mid1, slice(None))
        term = mul(taps1[16 * r : 16 * r + full_rows, :], kernel, NN)
        F[0:full_rows, 0:mid1] = term if r == 0 else F[0:full_rows, 0:mid1] + term

    @pl.loop(0, mid1 // 128)
    def _(i):
        field_sums(layers[SPATIAL], refs.given[0][SPATIAL], plain(F), i, True)

    def during(p):
        if p == 0:
            for k in (SHRINK, STRIDE):
                spread_affine(k)

    point()
    reduce(0, SPATIAL, during)

    def to_spatial(image, i, value):
        act_spatial[image.rows(False), lanes(i)] = value.astype(BF16)

    forward(SPATIAL, plain(F), to_spatial)

    point()
    arrive(WIDEN)

    @pl.loop(0, c_in // 256)
    def _(j):
        cols = lanes(j, 256)
        F[0:full_rows, cols] = mul(act_spatial[...], whole[WIDEN][:, :, :, cols].reshape(mid1, 256), NN)
        for k in range(2):
            field_sums(layers[WIDEN], refs.given[0][WIDEN], plain(F), 2 * j + k, False)

    def during(p):
        if p == 0:
            for k in (EXPAND, BYPASS):
                spread_affine(k)

    point()
    reduce(0, WIDEN, during)

    def to_upper(image, i, value):
        upper[image.rows(False), lanes(i)] = value.astype(BF16)
        rows = image.rows(False)
        EVEN[rows, :] = value
        for pair in range(image.half_count // 16):
            both = [EVEN[strided(image.at + 32 * min(2 * pair + k, image.half_side - 1)), :] for k in range(2)]
            here = pl.ds(image.half_at + 16 * pair, 16)
            even[here, lanes(i)] = jnp.concatenate(both, axis=0).astype(BF16)

    forward(WIDEN, plain(F), to_upper, x_v)

    point()
    arrive(SHRINK)

    @pl.loop(0, mid2 // 256)
    def _(j):
        cols = lanes(j, 256)
        F[0:full_rows, cols] = mul(upper[...], whole[SHRINK][:, :, :, cols].reshape(c_in, 256), NN)
        for k in range(2):
            field_sums(layers[SHRINK], refs.given[0][SHRINK], plain(F), 2 * j + k, False)

    point()
    reduce(0, SHRINK)

    def to_shrink(image, i, value):
        K[i, pl.ds(32 + image.at, image.count), :] = value

    forward(SHRINK, plain(F), to_shrink)

    for image in images:

        @pl.loop(0, image.half_count // 16)
        def _(pair):
            rows = pl.ds(pl.multiple_of(image.half_at + 16 * pair, 16), 16)
            for r in range(3):
                for q in range(3):
                    start = 32 + image.at + 64 * pair + (r - 1) * 16 + q - 1
                    for b in range(blocks2):
                        both = [K[b, strided(start + 32 * k), :] for k in range(2)]
                        at = (3 * r + q) * mid2 + b * 128
                        taps2[rows, at : at + 128] = jnp.concatenate(both, axis=0).astype(BF16)

    point()
    arrive(STRIDE)

    @pl.loop(0, mid2 // 256)
    def _(j):
        cols = lanes(j, 256)
        depth = 9 * mid2 // 4
        for far in range(4):
            kernel = whole[STRIDE][far, :, :, cols].reshape(depth, 256)
            term = mul(taps2[:, far * depth : (far + 1) * depth], kernel, NN)
            G[:, cols] = term if far == 0 else G[:, cols] + term
        for k in range(2):
            field_sums(layers[STRIDE], refs.given[0][STRIDE], plain_half(G), 2 * j + k, True)

    def bypass_field():
        arrive(BYPASS)

        @pl.loop(0, c_out // 256)
        def _(j):
            value = mul(even[...], whole[BYPASS][:, :, :, lanes(j, 256)].reshape(c_in, 256), NN)
            blocks = c_in // 256
            rows = pl.ds(pl.multiple_of((2 + lax.div(j, blocks)) * half_rows, 8), half_rows)
            F[rows, lanes(lax.rem(j, blocks), 256)] = value
            for k in range(2):
                i = 2 * j + k
                cols = pl.ds(pl.multiple_of(c_out + i * 128, 128), 128)
                field_sums(layers[BYPASS], refs.given[0][LAST], halves(F, 2), i, True, cols)

    point()
    reduce(0, STRIDE)

    def to_stride(image, i, value):
        act_stride[image.rows(True), lanes(i)] = value.astype(BF16)

    forward(STRIDE, plain_half(G), to_stride)

    point()
    arrive(EXPAND)

    @pl.loop(0, c_out // 256)
    def _(j):
        value = mul(act_stride[...], whole[EXPAND][:, :, :, lanes(j, 256)].reshape(mid2, 256), NN)
        blocks = c_in // 256
        rows = pl.ds(pl.multiple_of(lax.div(j, blocks) * half_rows, 8), half_rows)
        F[rows, lanes(lax.rem(j, blocks), 256)] = value
        for k in range(2):
            field_sums(layers[EXPAND], refs.given[0][LAST], halves(F, 0), 2 * j + k, True)

    point()
    bypass_field()
    reduce(0, LAST)
    load_cot.wait()
    expand_z, bypass_z = halves(F, 0), halves(F, 2)

    @pl.loop(0, c_out // 128)
    def _(i):
        cols = lanes(i)
        upper_cols = pl.ds(pl.multiple_of(c_out + i * 128, 128), 128)
        stats_e = statistics(refs.total[0][LAST][:, cols])
        stats_b = statistics(refs.total[0][LAST][:, upper_cols])
        el, bl = layers[EXPAND], layers[BYPASS]
        firsts, seconds, thirds = [], [], []
        for image in images:
            rows, inside = image.rows(True), image.inside(True)
            normed_e = normed_of(el, image, cols, expand_z(image, i), *stats_e)
            normed_b = normed_of(bl, image, cols, bypass_z(image, i), *stats_b)
            value = normed_e * el.affine[0:1, cols] + el.affine[1:2, cols]
            value = value + (normed_b * bl.affine[0:1, cols] + bl.affine[1:2, cols])
            cdf, rest = normal_parts(value)
            el.normed[rows, cols] = normed_e.astype(BF16)
            bl.normed[rows, cols] = normed_b.astype(BF16)
            grad = jnp.where(inside, refs.cot_v[rows, cols].astype(F32) * (cdf + rest), 0.0)
            refs.cot_v[rows, cols] = (value * cdf).astype(BF16)
            blocks = F.shape[1] // 128
            band = lax.div(i, blocks)
            here = pl.ds(pl.multiple_of(band * half_rows + image.half_at, 8), image.half_count)
            F[here, lanes(lax.rem(i, blocks))] = grad
            firsts.append(column_sum(grad))
            seconds.append(column_sum(grad * normed_e))
            thirds.append(column_sum(grad * normed_b))
        put_sums(refs.given[1][LAST], cols, firsts, seconds)
        put_sums(refs.given[1][LAST], upper_cols, thirds, thirds)

    store_out = pltpu.make_async_copy(refs.cot_v, refs.out, refs.store_sem.at[0])
    store_out.start()
    point()
    reduce(1, LAST)

    def sums_expand(i):
        total = refs.total[1][LAST][:, lanes(i)]
        return total[0:4], total[4:8]

    def sums_bypass(i):
        first = refs.total[1][LAST][:, lanes(i)]
        second = refs.total[1][LAST][:, pl.ds(pl.multiple_of(c_out + i * 128, 128), 128)]
        return first[0:4], second[0:4]

    gradient(EXPAND, halves(F, 0), sums_expand)
    gradient(BYPASS, halves(F, 0), sums_bypass)
    expand_grad, bypass_grad = layers[EXPAND].normed, layers[BYPASS].normed

    point()
    @pl.loop(0, mid2 // 256)
    def _(j):
        kernel = whole[EXPAND][pl.ds(2 * j, 2)].reshape(256, c_out)
        cols = lanes(j, 256)
        G[:, cols] = mul(expand_grad[...], kernel, NT) * layers[STRIDE].slope[:, cols].astype(F32)

    gradient_sums(STRIDE, plain_half(G), refs.given[1][STRIDE])

    def filter_grad(name, left, right, fars):
        let_go(name)
        target = whole[name]
        shard, columns = target.shape[2], target.shape[3]
        depth = fars * 4 * shard
        width = min(columns, 512 if depth <= 512 else 256)

        @pl.loop(0, (4 // fars) * (columns // width))
        def _(i):
            j, b = lax.div(i, columns // width), lax.rem(i, columns // width)
            value = mul(left[:, lanes(j, depth)], right[:, lanes(b, width)], TN)
            target[pl.ds(j * fars, fars), :, :, lanes(b, width)] = value.astype(BF16).reshape(fars, 4, shard, width)

    def during(p):
        if p == 0:
            filter_grad(EXPAND, act_stride, expand_grad, 2)
            send_off(EXPAND)
        if p == 1:

            @pl.loop(0, 4)
            def _(j):
                kernel = whole[BYPASS][j].reshape(256, c_out)
                S[pl.ds(pl.multiple_of(j * half_rows, 8), half_rows), :] = mul(bypass_grad[...], kernel, NT)

            filter_grad(BYPASS, even, bypass_grad, 1)
            send_off(BYPASS)

    point()
    reduce(1, STRIDE, during)
    gradient(STRIDE, plain_half(G), totals_of(STRIDE))
    stride_grad = layers[STRIDE].normed

    point()
    K[...] = jnp.zeros(K.shape, F32)
    for r in range(3):
        for q in range(3):
            kernel = rows_piece(whole[STRIDE], (3 * r + q) * mid2, mid2, slice(None))
            F[0:half_rows, 0:mid2] = mul(stride_grad[...], kernel, NT)
            for image in images:

                @pl.loop(0, image.half_side)
                def _(i):
                    there = strided(32 + image.at + 32 * i + (r - 1) * 16 + q - 1)
                    here = pl.ds(pl.multiple_of(image.half_at + 8 * i, 8), 8)
                    for b in range(blocks2):
                        K[b, there, :] = K[b, there, :] + F[here, b * 128 : (b + 1) * 128]

    @pl.loop(0, mid2 // 128)
    def _(i):
        cols = lanes(i)
        firsts, seconds = [], []
        for image in images:
            rows = pl.ds(32 + image.at, image.count)
            g = K[i, rows, :] * layers[SHRINK].slope[image.rows(False), cols].astype(F32)
            K[i, rows, :] = g
            firsts.append(column_sum(g))
            seconds.append(column_sum(g * layers[SHRINK].normed[image.rows(False), cols].astype(F32)))
        put_sums(refs.given[1][SHRINK], cols, firsts, seconds)

    def during(p):
        if p == 1:
            filter_grad(STRIDE, taps2, stride_grad, 1)
            send_off(STRIDE)

    point()
    reduce(1, SHRINK, during)
    gradient(SHRINK, lambda image, i: K[i, pl.ds(32 + image.at, image.count), :], totals_of(SHRINK))
    shrink_grad = layers[SHRINK].normed

    point()

    @pl.loop(0, 4)
    def _(j):
        cols = lanes(j, 256)
        kernel = whole[SHRINK][j].reshape(256, mid2)
        F[0:full_rows, cols] = mul(shrink_grad[...], kernel, NT)

    @pl.loop(0, c_in // 128)
    def _(i):
        cols = lanes(i)
        firsts, seconds = [], []
        for image in images:
            rows = image.rows(False)
            for j in range(image.half_side):
                start = pl.multiple_of(lax.div(i, 2) * half_rows + image.half_at + 8 * j, 8)
                SPREAD[strided(image.at + 32 * j), :] = S[pl.ds(start, 8), lanes(lax.rem(i, 2))]
            g = (F[rows, cols] + SPREAD[rows, :]) * layers[WIDEN].slope[rows, cols].astype(F32)
            F[rows, cols] = g
            firsts.append(column_sum(g))
            seconds.append(column_sum(g * layers[WIDEN].normed[rows, cols].astype(F32)))
        put_sums(refs.given[1][WIDEN], cols, firsts, seconds)

    def during(p):
        if p == 0:
            filter_grad(SHRINK, upper, shrink_grad, 1)
            send_off(SHRINK)

    point()
    reduce(1, WIDEN, during)
    gradient(WIDEN, plain(F), totals_of(WIDEN))
    widen_grad = layers[WIDEN].normed

    point()
    S[0:full_rows, :] = mul(widen_grad[...], whole[WIDEN][...].reshape(mid1, c_in), NT) * layers[SPATIAL].slope[...].astype(F32)
    gradient_sums(SPATIAL, plain(S), refs.given[1][SPATIAL])

    def during(p):
        if p == 0:
            filter_grad(WIDEN, act_spatial, widen_grad, 4)
            send_off(WIDEN)

    point()
    reduce(1, SPATIAL, during)
    gradient(SPATIAL, plain(S), totals_of(SPATIAL), functools.partial(shifted, grad3))

    point()
    for r in range(3):
        kernel = jnp.concatenate(
            [rows_piece(whole[SPATIAL], (3 * r + 2 - q) * mid1, mid1, slice(None)) for q in range(3)], axis=1
        )
        term = mul(grad3[16 * (2 - r) : 16 * (2 - r) + full_rows, :], kernel, NT)
        S[0:full_rows, :] = term if r == 0 else S[0:full_rows, :] + term
    S[0:full_rows, :] = S[0:full_rows, :] * layers[NARROW].slope[...].astype(F32)
    gradient_sums(NARROW, plain(S), refs.given[1][NARROW])

    def during(p):
        if p == 0:
            let_go(SPATIAL)
        if p < 2:
            for r in ((0,), (1, 2))[p]:
                value = mul(taps1[16 * r : 16 * r + full_rows, :], grad3[16 : 16 + full_rows, mid1 : 2 * mid1], TN)
                store_piece(whole[SPATIAL], r * 3 * mid1, value.astype(BF16))
        if p == 1:
            send_off(SPATIAL)

    point()
    reduce(1, NARROW, during)
    gradient(NARROW, plain(S), totals_of(NARROW))
    narrow_grad = layers[NARROW].normed

    point()
    for j in range(4):
        upper[0:256, j * mid1 : (j + 1) * mid1] = whole[NARROW][j].reshape(256, mid1)
    filter_grad(NARROW, x_v, narrow_grad, 1)
    send_off(NARROW)
    point()
    for j in range(4):
        cols = slice(j * 256, (j + 1) * 256)
        kernel = upper[0:256, j * mid1 : (j + 1) * mid1]
        x_v[:, cols] = (F[0:full_rows, cols] + mul(narrow_grad[...], kernel, NT)).astype(BF16)
        point()
    stores = [
        pltpu.make_async_copy(x_v, refs.dinput, refs.store_sem.at[1]),
        pltpu.make_async_copy(refs.daffine_v, refs.daffine, refs.store_sem.at[2]),
    ]
    for store in stores:
        store.start()
    point()
    for k in (EXPAND, BYPASS, STRIDE, SHRINK, WIDEN, SPATIAL, NARROW):
        for item in pieces_of(scatters, k):
            item.finish()
        stores.append(pltpu.make_async_copy(refs.done[k], refs.dfilter[k], refs.store_sem.at[3 + k]))
        stores[-1].start()
    for item in scatters:
        item.settle()
    let_go(TABLE)
    store_out.wait()
    for store in stores:
        store.wait()


PIECES = [
    Piece(NARROW, direct=True),
    Piece(SPATIAL),
    Piece(WIDEN),
    Piece(SHRINK),
    Piece(STRIDE, 0, 2, 0, 2),
    Piece(STRIDE, 0, 2, 1, 2),
    Piece(STRIDE, 1, 2, 0, 2),
    Piece(STRIDE, 1, 2, 1, 2),
    Piece(EXPAND, 0, 1, 0, 2),
    Piece(EXPAND, 0, 1, 1, 2),
    Piece(BYPASS, 0, 1, 0, 4),
    Piece(BYPASS, 0, 1, 1, 4),
    Piece(BYPASS, 0, 1, 2, 4),
    Piece(BYPASS, 0, 1, 3, 4),
    Piece(TABLE, halved=False, direct=True),
]
N, S, W, K, T0, T1, T2, T3, E0, E1, B0, B1, B2, B3, TAB = range(15)
BEGIN = object()
GATHER_STEPS = (Gather.near, Gather.forward, Gather.cross)
NEAR, FORWARD, CROSS = GATHER_STEPS
R2, R3, R4, R5 = Scatter.second, Scatter.first, Scatter.fars, Scatter.cross
PLAN = {
    0: [(BEGIN, TAB, N, S, W, K, T0), (NEAR, TAB, N, S), (FORWARD, TAB, N), (CROSS, N)],
    1: [(CROSS, TAB), (BEGIN, T1)],
    2: [(FORWARD, S), (NEAR, W, K), (BEGIN, T2)],
    3: [(CROSS, S)],
    4: [(FORWARD, W), (NEAR, T0), (BEGIN, T3)],
    6: [(CROSS, W)],
    7: [(FORWARD, K, T0), (NEAR, T1), (BEGIN, E0)],
    8: [(CROSS, K, T0)],
    9: [(NEAR, T2), (BEGIN, E1)],
    12: [(FORWARD, T1, T2), (NEAR, T3), (BEGIN, B0)],
    13: [(CROSS, T1, T2)],
    14: [(NEAR, E0), (FORWARD, T3), (BEGIN, B1)],
    17: [(FORWARD, E0), (NEAR, E1, B0), (BEGIN, B2)],
    18: [(CROSS, T3, E0)],
    19: [(FORWARD, E1), (NEAR, B1), (BEGIN, B3)],
    22: [(FORWARD, B0, B1), (NEAR, B2, B3)],
    23: [(CROSS, E1, B0, B1)],
    24: [(FORWARD, B2)],
    25: [(FORWARD, B3)],
    26: [(CROSS, B2, B3)],
    37: [(R2, E0, E1)],
    38: [(R2, B0)],
    39: [(R3, E0, E1), (R2, B1)],
    40: [(R4, E0)],
    41: [(R3, B0, B1), (R2, B2, B3), (R4, E1)],
    42: [(R5, E0)],
    43: [(R3, B2), (R4, B0)],
    46: [(R3, B3), (R2, T0, T1), (R4, B1, B2)],
    47: [(R5, E1, B0)],
    48: [(R3, T0), (R4, B3)],
    49: [(R3, T1), (R4, T0)],
    51: [(R2, T2, T3), (R4, T1)],
    52: [(R5, B1, B2)],
    53: [(R2, K), (R3, T2)],
    54: [(R3, T3)],
    56: [(R3, K), (R2, W), (R4, T2)],
    57: [(R5, B3, T0, T1)],
    58: [(R2, S), (R3, W), (R4, K, T3)],
    59: [(R3, S), (R4, W)],
    60: [(R4, S), (R5, T2, T3)],
    61: [(R2, N), (R5, K, W)],
    63: [(R3, N), (R4, N), (R5, S)],
    65: [(R5, N)],
}


def spare_groups(spare):
    count = lax.axis_size("dp")
    return [list(range(at, at + spare)) for at in range(0, count, spare)]


def padded(field, rows, across):
    side = field.shape[1]
    field = jnp.pad(field, ((0, 0), (0, rows - side), (0, across - side), (0, 0)))
    return field.reshape(-1, field.shape[3])


def local(
    input_big,
    input_small,
    views_big,
    views_small,
    cotan_big,
    cotan_small,
    *params,
):
    filters, affines = params[0::2], params[1::2]
    devices = lax.axis_size("dp")
    spare = devices // 16
    inputs, cotans = (input_big, input_small), (cotan_big, cotan_small)
    counts = [item.shape[0] for item in inputs]
    images, full_rows, half_rows = images_of(counts, [item.shape[1] for item in inputs])
    c_in, c_out = input_big.shape[3], cotan_big.shape[3]
    mid1, mid2 = filters[NARROW].shape[1], filters[SHRINK].shape[1]
    widths = (c_in, mid1, mid2, c_out)
    wide = widths_of(*widths)
    by_group = [next(image for image in images if image.group == g) for g in range(2)]
    x = jnp.concatenate([padded(inputs[g], by_group[g].count // 16, 16) for g in range(2)])
    cot = jnp.concatenate([padded(cotans[g], by_group[g].half_count // 8, 8) for g in range(2)])

    parts = [item.T for item in affines]
    shards = list(filters)
    if spare > 1:
        groups = spare_groups(spare)
        shards = [lax.all_gather(item, "dp", axis_index_groups=groups, tiled=True) for item in filters]
        gathered = lax.all_gather(jnp.concatenate(parts, axis=1), "dp", axis_index_groups=groups)
        parts, at = [], 0
        for item in affines:
            share = item.shape[0]
            parts.append(jnp.moveaxis(gathered[:, :, at : at + share], 0, 1).reshape(2, -1))
            at += share
    places = table_places([item.shape[1] for item in parts]) + [512]
    parts = [
        jnp.pad(item, ((0, 0), (0, places[k + 1] - places[k] - item.shape[1]))) for k, item in enumerate(parts)
    ]
    shards.append(jnp.pad(jnp.concatenate(parts, axis=1).reshape(8, 128), ((0, 8), (0, 0))))
    shapes = [item.shape for item in shards]
    lane_total = sum(wide)

    def field(*shape):
        return pltpu.VMEM(shape, F32)

    def rounded(*shape):
        return pltpu.VMEM(shape, BF16)

    def layer_rows(k):
        return half_rows if k in (STRIDE, EXPAND, BYPASS) else full_rows

    rounds = [wide[:5] + [2 * c_out], wide[:5] + [2 * c_out]]
    rounds[0][NARROW] += 128
    sums = [
        [Reduce.scratch(8, width, spare, k == LAST) for k, width in enumerate(rounds[0])],
        [Reduce.scratch(16, width // 2, spare, k == LAST, BF16) for k, width in enumerate(rounds[1])],
    ]
    operands = dict(x=x, cot=cot, shards=shards, views=[views_big, views_small])
    anywhere, scalars = pl.BlockSpec(memory_space=pl.ANY), pl.BlockSpec(memory_space=pltpu.SMEM)
    specs = dict(x=anywhere, cot=anywhere, shards=[anywhere] * len(shards), views=[scalars] * 2)
    results = dict(
        out=jax.ShapeDtypeStruct((half_rows, c_out), BF16),
        dinput=jax.ShapeDtypeStruct((full_rows, c_in), BF16),
        daffine=jax.ShapeDtypeStruct((8, lane_total), F32),
        dfilter=[jax.ShapeDtypeStruct(shape, BF16) for shape in shapes[:7]],
    )
    scratch = dict(
        whole=[rounded(4, 4, *shape) for shape in shapes],
        done=[rounded(*shape) for shape in shapes[:7]],
        landing=[Scatter.scratch(*piece.sizes(shapes[piece.layer])) for piece in PIECES[:-1]],
        normed=[rounded(layer_rows(k), wide[k]) for k in range(7)],
        slope=[None if k in (EXPAND, BYPASS) else rounded(layer_rows(k), wide[k]) for k in range(7)],
        affine=[field(8, width) for width in wide],
        scale=[field(-(-len(images) // 8) * 8, width) for width in wide],
        x_v=rounded(full_rows, c_in),
        cot_v=rounded(half_rows, c_out),
        hot_v=field(2 * len(images), 128),
        cnt=field(8, 128),
        daffine_v=field(8, lane_total),
        F=field(max(full_rows, 4 * half_rows), c_in),
        G=field(half_rows, mid2),
        S=field(max(full_rows, 4 * half_rows), mid1),
        K=field(mid2 // 128, full_rows + 64, 128),
        EVEN=field(full_rows, 128),
        SPREAD=field(full_rows, 128),
        taps1=rounded(full_rows + 32, 3 * mid1),
        grad3=rounded(full_rows + 32, 3 * mid1),
        act_spatial=rounded(full_rows, mid1),
        upper=rounded(full_rows, c_in),
        taps2=rounded(half_rows, 9 * mid2),
        act_stride=rounded(half_rows, mid2),
        even=rounded(half_rows, c_in),
        given=[[field(8, width) for width in way] for way in rounds],
        total=[[field(8, width) for width in way] for way in rounds],
        slots=[[item[:-2] for item in way] for way in sums],
        packed=[rounded(16, width // 2) for width in rounds[1]],
        summed=[(rounded if k == LAST else field)(16, width // 2) for k, width in enumerate(rounds[1])],
        sums_sem=[[item[-2:] for item in way] for way in sums],
        load_sem=pltpu.SemaphoreType.DMA((len(PIECES) + 3,)),
        store_sem=pltpu.SemaphoreType.DMA((16,)),
        gather_send=pltpu.SemaphoreType.DMA((len(PIECES), Gather.PHASES)),
        gather_recv=pltpu.SemaphoreType.DMA((len(PIECES), Gather.PHASES)),
        scatter_send=pltpu.SemaphoreType.DMA((len(PIECES), Scatter.PHASES)),
        scatter_recv=pltpu.SemaphoreType.DMA((len(PIECES), Scatter.PHASES)),
    )
    flat_in, in_tree = jax.tree.flatten(operands)
    flat_out, out_tree = jax.tree.flatten(results)
    flat_scratch, scratch_tree = jax.tree.flatten(scratch)

    def kernel(*flat):
        here = len(flat_in) + len(flat_out)
        refs = jax.tree.unflatten(in_tree, flat[: len(flat_in)])
        refs |= jax.tree.unflatten(out_tree, flat[len(flat_in) : here])
        refs |= jax.tree.unflatten(scratch_tree, flat[here:])
        step_kernel(spare, images, widths, types.SimpleNamespace(**refs))

    flat_out = pl.pallas_call(
        kernel,
        out_shape=flat_out,
        in_specs=jax.tree.leaves(specs),
        out_specs=[pl.BlockSpec(memory_space=pl.ANY)] * len(flat_out),
        scratch_shapes=flat_scratch,
        compiler_params=pltpu.CompilerParams(
            collective_id=KERNEL_ID, has_side_effects=True, vmem_limit_bytes=VMEM_BYTES
        ),
    )(*flat_in)
    done = types.SimpleNamespace(**jax.tree.unflatten(out_tree, flat_out))

    shares = [width // devices for width in wide]
    views = [(group, half) for half in (True, False) for group in range(2)]

    def image_shape(group, half):
        side = by_group[group].half_side if half else by_group[group].side
        return counts[group], side, side, c_out if half else c_in

    def finish(*flat):
        given, images_out, grads_out, affine_out = flat[:10], flat[10:14], flat[14:21], flat[21:28]
        held, sem = flat[28:38], flat[38]
        copies = [pltpu.make_async_copy(given[k], held[k], sem.at[k]) for k in range(10)]
        for copy in copies:
            copy.start()
        for copy in copies:
            copy.wait()
        out, dinput, daffine, *grads = held
        for ref, (group, half) in zip(images_out, views):
            image, rows = by_group[group], out if half else dinput
            start = image.half_at if half else image.at
            count = image.half_count if half else image.count
            across = 8 if half else 16
            number, side, _, width = ref.shape
            for n in range(number):
                for row in range(side):
                    here = start + n * count + row * across
                    ref[n, row] = rows[here : here + across, :][:side]
        for ref, grad in zip(grads_out, grads):
            ref[...] = grad[...].astype(F32)
        me, at = lax.axis_index("dp"), 0
        for k, ref in enumerate(affine_out):
            first = me * shares[k]
            block, shift = lax.div(first, 128), lax.rem(first, 128)
            rows = daffine[:, pl.ds(pl.multiple_of(at + block * 128, 128), 128)]
            ref[...] = pltpu.roll(rows, lax.rem(128 - shift, 128), 1)[0:2, 0 : shares[k]]
            at += wide[k]

    finals = [done.out, done.dinput, done.daffine, *done.dfilter]
    outs = pl.pallas_call(
        finish,
        out_shape=[jax.ShapeDtypeStruct(image_shape(*view), BF16) for view in views]
        + [jax.ShapeDtypeStruct(shape, F32) for shape in shapes[:7]]
        + [jax.ShapeDtypeStruct((2, share), F32) for share in shares],
        in_specs=[pl.BlockSpec(memory_space=pl.ANY)] * 10,
        out_specs=[pl.BlockSpec(memory_space=pltpu.VMEM)] * 18,
        scratch_shapes=[pltpu.VMEM(item.shape, item.dtype) for item in finals] + [pltpu.SemaphoreType.DMA((10,))],
        compiler_params=pltpu.CompilerParams(vmem_limit_bytes=VMEM_BYTES),
    )(*finals)
    results = list(outs[:4])
    for grad, affine in zip(outs[4:11], outs[11:]):
        if spare > 1:
            grad = lax.psum_scatter(grad, "dp", axis_index_groups=spare_groups(spare), tiled=True)
        results += [grad, affine.T]
    return tuple(results)


VMEM_BYTES = 65400 * 1024


def solution(mesh):
    images = P(("dp", "outer"), None, None, None)
    rows = P("dp", None)
    return jax.shard_map(
        local,
        mesh=mesh,
        in_specs=(images, images, P(("dp", "outer")), P(("dp", "outer")), images, images) + (rows,) * 14,
        out_specs=(images,) * 4 + (rows,) * 14,
        check_vma=False,
    )
```
